32 devices in a mesh: pts: 8 (over y, x, core), bins: 4 (over z).
Axes of the slice: x: 2, y: 2, z: 4, core: 2. Of those that a mesh axis runs over, the one named last changes fastest.
Arguments:
- spectrum: bfloat16 [1296, 32, 512], P('bins', 'pts'), may hold values from 0.049804688 to 4
- courant: float32 [1296, 2], replicated, may hold values from 0.05 to 0.45
- upwind: int32 [1296, 2], replicated, may hold values from 0 to 1
- coupling: bfloat16 [1296, 1296], replicated, may hold values from -0.15625 to 0.15625
- sea: int32 [32, 512], P('pts'), may hold values 0 or 1
- owner: int32 [8, 4, 512, 1], P('pts', 'bins'), may hold values from 0 to 7; in each aligned block of 512 rows (0 to 511, 512 to 1023, ..., all dimensions but the last counted through in order) at most 128 rows name the same one
Outputs:
- owner_rows: bfloat16 [8, 4, 1024, 1296], P('pts', 'bins')
The draws below stay inside these ranges and needn't reach their ends.
Inputs may be any that keep to these rules, and one draw needn't show every extreme that they name: Among the 512 points of one block, at most 128 name the same owner, and in every draw some owner is named by exactly 128 points of some block.
All inputs are finite; a program needn't handle non-finite values. No bound on the sum of `sea` on one device may be relied on, other than what follows from the above.
Results may differ from the reference program's by a relative error of at most 0.0049.
Values may be sent and summed in bfloat16 or wider, within the bound.
No kernel may reach another device: no remote copies, remote signals or barrier semaphores. Data moves between devices by JAX's collectives and lax.ppermute only.
A program may use at most 64 MiB of HBM per device.

```python
import math
import jax
import jax.numpy as jnp
import numpy as np
from jax import lax

LON_DEV = 4
LAT_DEV = 128
BINS = 1296
NLON = 32
NLAT = 512
PB = 512
CAP = 128
N_PTS = 8
N_BINS = 4


def set_ends(drawn, stream_key, smallest, high):
    longest = drawn.shape.index(max(drawn.shape))
    spots = []
    for shift in (0, 1):
        where = [jax.random.randint(jax.random.fold_in(stream_key, axis), (), 0, length) for axis, length in enumerate(drawn.shape)]
        where[longest] = (where[longest] + shift) % drawn.shape[longest]
        spots.append(tuple(where))
    return drawn.at[spots[0]].set(smallest).at[spots[1]].set(high)


def block_scale(key, dims, cuts, low, top_value):
    def one(position, shards_of):
        heights = jax.random.uniform(jax.random.fold_in(jax.random.fold_in(key, 6), position), (shards_of,), jnp.float32, low / len(cuts), top_value / len(cuts))
        return jnp.repeat(jnp.exp(heights), dims[position] // shards_of).reshape((-1,) + (1,) * (len(dims) - position - 1))

    gain = one(*cuts[0])
    for cut in cuts[1:]:
        gain = gain * one(*cut)
    return gain


def shared_out(stream_key, own, number, rows, number_of, top, reach, slope):
    order = jax.random.permutation(stream_key, number_of)
    crowded, common = shares(number_of, rows * top, reach, slope, True), shares(number_of, rows * top, reach, slope, False)
    places = jnp.arange(number_of)

    def named(sizes, offset_by):
        used = int((sizes > 0).sum())
        fixed = max(1, used // 4)
        moved = fixed + (places - fixed + offset_by * (used - fixed)) % max(1, number_of - fixed)
        return jnp.zeros((number_of,), jnp.int32).at[order[jnp.where(places < fixed, places, moved)]].set(jnp.asarray(sizes, jnp.int32))

    sizes = jnp.where(number % 4 == 0, named(crowded, number // 4), named(common, number - number // 4 - 1))
    mixed = jax.random.permutation(jax.random.fold_in(own, 3), number_of)
    giver, receiver = mixed[0:number_of // 2 * 2:2], mixed[1:number_of // 2 * 2:2]
    room = jnp.minimum(sizes[giver] - 1, reach - sizes[receiver]) // 2
    room = jnp.where((giver == order[0]) | (receiver == order[0]) | (sizes[receiver] == 0), 0, jnp.maximum(room, 0))
    moved = jax.random.randint(jax.random.fold_in(own, 4), (number_of // 2,), 0, 1 << 20) % (room + 1)
    sizes = sizes.at[giver].add(-moved).at[receiver].add(moved)
    items = jnp.searchsorted(jnp.cumsum(sizes), jnp.arange(rows * top), side="right").astype(jnp.int32)
    grid = items.reshape(top, rows).T
    grid = grid[jax.random.permutation(jax.random.fold_in(own, 1), rows)]
    offset_by = jax.random.randint(jax.random.fold_in(own, 2), (rows, 1), 0, top)
    return jnp.take_along_axis(grid, (jnp.arange(top)[None, :] + offset_by) % top, axis=1)


def shares(number_of, total, limit, skew, full):
    loads = [(1 << 20) // math.isqrt(rank ** skew) + 1 for rank in range(1, number_of + 1)]
    largest = limit if full else min(limit, max(-(-total // number_of), total * loads[0] // sum(loads)))
    least = 1 if total - largest >= number_of - 1 else 0
    holding, surplus = [largest] + [least] * (number_of - 1), total - largest - least * (number_of - 1)
    while surplus > 0:
        candidates = [i for i in range(1, number_of) if holding[i] < largest] or [i for i in range(1, number_of) if holding[i] < limit]
        pool, budget = sum([loads[i] for i in candidates]), surplus
        for i in candidates:
            addition = min(limit - holding[i], max(1, budget * loads[i] // pool), surplus)
            holding[i] = holding[i] + addition
            surplus = surplus - addition
    return np.array(holding)


def scatter_about(stream_key, dims, spread, bound, held_as=jnp.bfloat16):
    return jnp.clip(spread * jax.random.normal(stream_key, dims, jnp.float32), -bound, bound).astype(held_as)


def setup_inputs(seed: int = 0) -> dict:
    seeds = jax.random.split(jax.random.key(seed), 7)
    spectrum = jnp.clip(jnp.exp(math.log(4.0) - 4.3859405 * jax.random.uniform(seeds[0], (BINS, NLON, NLAT), jnp.float32) ** block_scale(seeds[0], (BINS, NLON, NLAT), ((0, 4), (1, 8)), -0.2, 0.2)), 0.049804688, 4.0).astype(jnp.bfloat16)
    courant = jnp.clip(jax.random.uniform(seeds[1], (BINS, 2), jnp.float32, 0.05, 0.45), 0.05, 0.45)
    upwind = set_ends(jax.random.randint(seeds[2], (BINS, 2), 0, 2), jax.random.fold_in(seeds[2], 1), 0, 1).astype(jnp.int32)
    coupling = scatter_about(seeds[3], (BINS, BINS), BINS ** -0.5, 0.15625)
    sea = set_ends((jax.random.randint(seeds[4], (NLON, NLAT), 0, 10) < 7).astype(jnp.int32), jax.random.fold_in(seeds[4], 1), 0, 1)
    owner_keys = jax.random.split(jax.random.fold_in(seeds[5], 1), N_PTS * N_BINS * PB // PB)
    owner_turns = jax.random.permutation(jax.random.fold_in(seeds[5], 3), N_PTS * N_BINS * PB // PB)
    owner = jax.vmap(lambda own, number: shared_out(jax.random.fold_in(seeds[5], 2), own, number, PB, N_PTS, 1, CAP, 2))(owner_keys, owner_turns).reshape((N_PTS, N_BINS, PB, 1))
    return dict(spectrum=spectrum, courant=courant, upwind=upwind, coupling=coupling, sea=sea, owner=owner)


def reference(spectrum, courant, upwind, coupling, sea, owner):
    sea_mask = sea.astype(jnp.float32)
    masked = spectrum.astype(jnp.float32) * sea_mask[None]
    padded = jnp.pad(masked, ((0, 0), (1, 1), (1, 1)))
    center = padded[:, 1:-1, 1:-1]
    donor_x = jnp.where(upwind[:, 0][:, None, None] == 0, padded[:, :-2, 1:-1], padded[:, 2:, 1:-1])
    donor_y = jnp.where(upwind[:, 1][:, None, None] == 0, padded[:, 1:-1, :-2], padded[:, 1:-1, 2:])
    moved = center - courant[:, 0][:, None, None] * (center - donor_x) - courant[:, 1][:, None, None] * (center - donor_y)
    propagated = (moved * sea_mask[None]).astype(jnp.bfloat16)
    point_major = jnp.transpose(propagated, (1, 2, 0))

    def source_row(inputs):
        point_rows, weights = inputs
        energy = jnp.mean(point_rows.astype(jnp.float32), axis=1)
        coupled = jnp.dot(point_rows, coupling, preferred_element_type=jnp.float32)
        return (weights[:, None] * (point_rows.astype(jnp.float32) + coupled) / (1.0 + energy)[:, None]).astype(jnp.bfloat16)

    updated = lax.map(source_row, (point_major, sea_mask))
    blocks = updated.reshape(N_PTS, LON_DEV, N_BINS, LAT_DEV, BINS)
    blocks = jnp.transpose(blocks, (0, 2, 1, 3, 4)).reshape(N_PTS, N_BINS, PB, BINS)
    target = owner[..., 0].astype(jnp.int32)
    onehot = (target[..., None] == jnp.arange(N_PTS, dtype=jnp.int32)).astype(jnp.int32)
    slot_rank = jnp.sum(jnp.cumsum(onehot, axis=2) * onehot, axis=-1) - 1
    source = jnp.arange(N_PTS, dtype=jnp.int32)[:, None, None]
    slot_row = source * CAP + slot_rank
    bin_index = jnp.broadcast_to(jnp.arange(N_BINS, dtype=jnp.int32)[None, :, None], target.shape)
    result = jnp.zeros((N_PTS, N_BINS, N_PTS * CAP, BINS), jnp.bfloat16)
    return result.at[target, bin_index, slot_row].set(blocks)
```

```python
import functools

import jax
import jax.numpy as jnp
from jax import lax
from jax.experimental import pallas as pl
from jax.experimental.pallas import tpu as pltpu
from jax.sharding import PartitionSpec as P

F32 = jnp.float32
BF16 = jnp.bfloat16
I32 = jnp.int32
LANES = 128
CHUNKS = 2
NT = (((1,), (1,)), ((), ()))


def round_up(size, unit):
    return -(-size // unit) * unit


def iota(shape, axis):
    return lax.broadcasted_iota(I32, shape, axis)


def dot_nt(lhs, rhs):
    return lax.dot_general(lhs, rhs, NT, preferred_element_type=F32)


def pack_kernel(rows_out, bins_axis, owners_count, half, *refs):
    planes, low, high, coef, sea = refs[:5]
    owner = refs[5 : 5 + bins_axis]
    chunks = refs[5 + bins_axis : 5 + bins_axis + CHUNKS * bins_axis]
    meta = refs[5 + bins_axis + CHUNKS * bins_axis]
    moved = refs[-1]
    lon_rows, rows, lats = planes.shape
    points = lon_rows * LANES
    me = lax.axis_index("bins")
    me_pts = lax.axis_index("pts")

    tile = 16
    lane = iota((tile, lats), 1)
    sea_f = sea[...].astype(F32)

    def advect(step, carry):
        at = pl.ds(pl.multiple_of(step * tile, tile), tile)
        c = coef[at, :]
        cx, cy, ux, uy = c[:, 0:1], c[:, 1:2], c[:, 2:3], c[:, 3:4]
        masked = [low[at, :].astype(F32)]
        masked += [planes[l, at, :].astype(F32) for l in range(lon_rows)]
        masked += [high[at, :].astype(F32)]
        for l in range(lon_rows):
            center = masked[l + 1]
            donor_x = jnp.where(ux == 0.0, masked[l], masked[l + 2])
            left = jnp.where(lane == 0, 0.0, pltpu.roll(center, 1, 1))
            right = jnp.where(lane == lats - 1, 0.0, pltpu.roll(center, lats - 1, 1))
            donor_y = jnp.where(uy == 0.0, left, right)
            value = center - cx * (center - donor_x) - cy * (center - donor_y)
            moved[l, at, :] = (value * sea_f[l : l + 1, :]).astype(BF16)
        return carry

    lax.fori_loop(0, rows // tile, advect, 0)

    owners_id = iota((owners_count, points), 0)
    hot = [(owner[m][...] == owners_id).astype(F32) for m in range(bins_axis)]
    earlier = (iota((points, points), 0) < iota((points, points), 1)).astype(F32).astype(BF16)
    before = jnp.dot(
        jnp.concatenate(hot, axis=0).astype(BF16), earlier, preferred_element_type=F32
    )
    place_id = iota((points, points), 0)
    for m in range(bins_axis):
        own = owner[m][...]
        count = jnp.sum(hot[m], axis=1, keepdims=True)
        offset = jnp.sum(jnp.where(owners_id < own, count, 0.0), axis=0, keepdims=True)
        mine = before[m * owners_count : (m + 1) * owners_count, :]
        rank = jnp.sum(hot[m] * mine, axis=0, keepdims=True)
        key = (offset + rank).astype(I32)
        place = (key & 1) * half + (key >> 1)
        order = (place_id == place).astype(F32).astype(BF16)
        block = me ^ m
        at = pl.ds(pl.multiple_of(block * LANES, LANES), LANES)
        lhs = jnp.concatenate([moved[l, :, at] for l in range(lon_rows)], axis=1)
        ordered = dot_nt(lhs, order)[:rows_out].astype(BF16)
        for c in range(CHUNKS):
            chunks[c * bins_axis + m][...] = ordered[:, c * half : (c + 1) * half]
        if m == 0:
            first = offset.astype(I32)
            slot = (key - first - (((key & 1) - first) & 1)) >> 1
            weight = jnp.concatenate([sea[l : l + 1, at].astype(F32) for l in range(lon_rows)], axis=1)
            facts = jnp.concatenate(
                [slot.astype(F32), (own ^ me_pts).astype(F32), rank, weight]
                + [jnp.zeros((1, points), F32)] * 4,
                axis=0,
            )
            meta[...] = dot_nt(facts.astype(BF16), order)


def couple_kernel(chunk, bins_axis, owners_count, all_bins, pad_row, slots, *refs):
    blocks = refs[:bins_axis]
    weights, meta = refs[bins_axis : bins_axis + 2]
    outs = refs[bins_axis + 2 : -1]
    values = refs[-1]
    rows, width = blocks[0].shape
    half_rows = values.shape[0] // 2
    me = lax.axis_index("bins")
    for m in range(bins_axis):
        at = pl.ds(pl.multiple_of((me ^ m) * rows, 8), rows)
        values[at, :] = blocks[m][...].astype(F32)
    flat = values[...].astype(BF16)
    energy = jnp.sum(values[...], axis=0, keepdims=True) / all_bins
    facts = meta[:, chunk * width : (chunk + 1) * width]
    scale = facts[3:4, :] / (1.0 + energy)
    slot, towards, rank = facts[0:1, :].astype(I32), facts[1:2, :].astype(I32), facts[2:3, :]
    slot_id = iota((owners_count * slots, width), 0)
    straight = (slot_id == towards * slots + slot).astype(F32).astype(BF16)
    crossed = (slot_id == (towards ^ 1) * slots + slot).astype(F32).astype(BF16)
    is_rank = iota((half_rows, width), 0) == pad_row
    sent = []
    for group in range(2):
        at = slice(group * half_rows, (group + 1) * half_rows)
        coupled = jnp.dot(weights[at, :], flat, preferred_element_type=F32)
        updated = (values[at, :] + coupled) * scale
        updated = jnp.where(is_rank, rank, updated).astype(BF16)
        sent.append(dot_nt(updated, straight if group == chunk else crossed).astype(BF16))
    even, odd = sent[chunk], sent[1 - chunk]
    is_low = iota((half_rows, LANES), 1) < slots
    for t in range(owners_count // 2):
        at = slice(t * LANES, (t + 1) * LANES)
        outs[t][0] = jnp.where(is_low, even[:, at], odd[:, at])
        outs[t][1] = jnp.where(is_low, odd[:, at], even[:, at])


def place_kernel(owners_count, rows, real, slots, *refs):
    pairs = owners_count // 2
    arrivals = refs[: CHUNKS * pairs]
    swapped = refs[CHUNKS * pairs : CHUNKS * pairs + CHUNKS]
    out = refs[CHUNKS * pairs + CHUNKS]
    staged, sems = refs[-2:]
    me = lax.axis_index("pts")
    half_rows = arrivals[0].shape[1]
    is_low = iota((half_rows, LANES), 1) < slots
    slot_id = iota((LANES, LANES), 0)
    copies = []
    for x in range(owners_count):
        t = x // 2
        if x % 2 == 0:
            first, second = arrivals[t][0], arrivals[pairs + t][0]
        else:
            second, first = swapped[0][t], swapped[1][t]
        pieces = []
        for lhs in (jnp.where(is_low, first, second), jnp.where(is_low, second, first)):
            rank = lhs[real : real + 16 - real % 16, :].astype(F32)[0:1, :].astype(I32)
            place = (slot_id == rank).astype(F32).astype(BF16)
            rows_f = dot_nt(lhs, place)
            for at in range(0, half_rows, rows):
                pieces.append(rows_f[at : at + real, :])
        staged[x] = jnp.concatenate(pieces, axis=0).astype(BF16)
        at = pl.ds(pl.multiple_of((me ^ x) * LANES, LANES), LANES)
        copy = pltpu.make_async_copy(staged.at[x], out.at[:, at], sems.at[x])
        copy.start()
        copies.append(copy)
    for copy in copies:
        copy.wait()


def gate_kernel(count, after, *refs):
    del count, after, refs


def gate(arrays, after):
    count = len(arrays)
    return pl.pallas_call(
        functools.partial(gate_kernel, count, len(after)),
        out_shape=[jax.ShapeDtypeStruct(a.shape, a.dtype) for a in arrays],
        in_specs=[pl.BlockSpec(memory_space=pl.ANY)] * (count + len(after)),
        out_specs=[pl.BlockSpec(memory_space=pl.ANY)] * count,
        input_output_aliases={i: i for i in range(count)},
        name="gate",
    )(*arrays, *after)


def params(mib):
    return pltpu.CompilerParams(vmem_limit_bytes=mib << 20)


def vmem(count):
    return [pl.BlockSpec(memory_space=pltpu.VMEM)] * count


def cost(flops, bytes_accessed):
    return pl.CostEstimate(flops=int(flops), bytes_accessed=int(bytes_accessed), transcendentals=0)


def exchange(array, axis, offset):
    return lax.ppermute(array, axis, [(i, i ^ offset) for i in range(lax.axis_size(axis))])


def chunked(spectrum, courant, upwind, coupling, sea, owner):
    local_bins, lon_rows, lats = spectrum.shape
    all_bins = courant.shape[0]
    bins_axis = lax.axis_size("bins")
    owners_count = lax.axis_size("pts")
    points = lon_rows * LANES
    half = points // CHUNKS
    slots = 2 * points // owners_count // CHUNKS
    tall = round_up(local_bins, 16)
    rows = round_up(local_bins + 1, 8)
    half_rows = bins_axis * rows // 2
    first_bin = lax.axis_index("bins") * local_bins

    masked = spectrum * sea.astype(BF16)[None]
    planes = jnp.pad(jnp.transpose(masked, (1, 0, 2)), ((0, 0), (0, tall - local_bins), (0, 0)))
    up = [(i, i + 1) for i in range(owners_count - 1)]
    down = [(i + 1, i) for i in range(owners_count - 1)]
    low = lax.ppermute(planes[lon_rows - 1], "pts", up)
    high = lax.ppermute(planes[0], "pts", down)
    own = owner.reshape(1, points)
    owners = [own] + [exchange(own, "bins", m) for m in range(1, bins_axis)]
    coef = jnp.concatenate([courant, upwind.astype(F32)], axis=1)
    coef = lax.dynamic_slice_in_dim(coef, first_bin, local_bins, 0)
    coef = jnp.pad(coef, ((0, tall - local_bins), (0, 0)))

    weights = jnp.transpose(coupling).reshape(bins_axis, local_bins, bins_axis, local_bins)
    extra = rows - local_bins
    weights = jnp.pad(weights, ((0, 0), (0, extra), (0, 0), (0, extra)))
    weights = weights.reshape(bins_axis * rows, bins_axis * rows)

    packed = pl.pallas_call(
        functools.partial(pack_kernel, rows, bins_axis, owners_count, half),
        out_shape=[jax.ShapeDtypeStruct((rows, half), BF16)] * (CHUNKS * bins_axis)
        + [jax.ShapeDtypeStruct((8, points), F32)],
        in_specs=vmem(5 + bins_axis),
        out_specs=vmem(CHUNKS * bins_axis + 1),
        scratch_shapes=[pltpu.VMEM((lon_rows, tall, lats), BF16)],
        compiler_params=params(24),
        cost_estimate=cost(2 * bins_axis * tall * points * points, 4e6),
        name="pack",
    )(planes, low, high, coef, sea, *owners)
    meta = packed[-1]

    arrivals, swaps, got = [], [], None
    for c in range(CHUNKS):
        blocks = packed[c * bins_axis : (c + 1) * bins_axis]
        if got is not None:
            blocks = gate(blocks, got)
        got = [exchange(blocks[m], "bins", m) for m in range(1, bins_axis)]
        pays = pl.pallas_call(
            functools.partial(
                couple_kernel, c, bins_axis, owners_count, all_bins, local_bins, slots
            ),
            out_shape=[jax.ShapeDtypeStruct((2, half_rows, LANES), BF16)] * (owners_count // 2),
            in_specs=vmem(bins_axis + 2),
            out_specs=vmem(owners_count // 2),
            scratch_shapes=[pltpu.VMEM((bins_axis * rows, half), F32)],
            compiler_params=params(32),
            cost_estimate=cost(2 * all_bins * all_bins * half + 4 * all_bins * half * 512, 6e6),
            name="couple",
        )(blocks[0], *got, weights, meta)
        came = [pays[0]]
        came += [exchange(pays[t], "pts", 2 * t) for t in range(1, owners_count // 2)]
        swaps.append(exchange(jnp.stack([a[1] for a in came]), "pts", 1))
        arrivals += came

    placed = pl.pallas_call(
        functools.partial(place_kernel, owners_count, rows, local_bins, slots),
        out_shape=jax.ShapeDtypeStruct((all_bins, owners_count * LANES), BF16),
        in_specs=vmem(len(arrivals) + CHUNKS),
        out_specs=pl.BlockSpec(memory_space=pl.ANY),
        scratch_shapes=[
            pltpu.VMEM((owners_count, all_bins, LANES), BF16),
            pltpu.SemaphoreType.DMA((owners_count,)),
        ],
        compiler_params=params(32),
        cost_estimate=cost(4 * all_bins * LANES * LANES * owners_count, 8e6),
        name="place",
    )(*arrivals, *swaps)
    return jnp.transpose(placed).reshape(1, 1, owners_count * LANES, all_bins)


def padded_2(block, sides, width):
    for axis, dim in sides:
        count = lax.axis_size(axis)
        forward = [(i, i + 1) for i in range(count - 1)]
        backward = [(target, source) for source, target in forward]
        low = lax.ppermute(
            lax.slice_in_dim(block, block.shape[dim] - width, None, axis=dim), axis, forward
        )
        high = lax.ppermute(lax.slice_in_dim(block, 0, width, axis=dim), axis, backward)
        block = jnp.concatenate([low, block, high], axis=dim)
    return block


def advect(padded, sea_mask, courant, upwind):
    center = padded[:, 1:-1, 1:-1]
    donor_x = jnp.where(upwind[:, 0][:, None, None] == 0, padded[:, :-2, 1:-1], padded[:, 2:, 1:-1])
    donor_y = jnp.where(upwind[:, 1][:, None, None] == 0, padded[:, 1:-1, :-2], padded[:, 1:-1, 2:])
    moved = (
        center
        - courant[:, 0][:, None, None] * (center - donor_x)
        - courant[:, 1][:, None, None] * (center - donor_y)
    )
    return (moved * sea_mask[None]).astype(jnp.bfloat16)


def whole(spectrum, courant, upwind, coupling, sea, owner):
    local_bins = spectrum.shape[0]
    lon_rows = spectrum.shape[1]
    bins_count = lax.axis_size("bins")
    lat_cells = spectrum.shape[2] // bins_count
    masked = spectrum * sea.astype(jnp.bfloat16)[None]
    local_sea = lax.dynamic_slice_in_dim(
        sea, lax.axis_index("bins") * lat_cells, lat_cells, 1
    ).astype(jnp.float32)
    first_bin = lax.axis_index("bins") * local_bins
    my_courant = lax.dynamic_slice_in_dim(courant, first_bin, local_bins, 0)
    my_upwind = lax.dynamic_slice_in_dim(upwind, first_bin, local_bins, 0)
    extended = padded_2(masked, (("pts", 1),), 1)
    extended = jnp.pad(extended.astype(jnp.float32), ((0, 0), (0, 0), (1, 1)))
    moved = advect(extended, sea.astype(jnp.float32), my_courant, my_upwind)
    columns = lax.all_to_all(moved, "bins", split_axis=2, concat_axis=0, tiled=True)
    all_bins = columns.shape[0]
    points = lon_rows * lat_cells
    flat = columns.reshape(all_bins, points)
    energy = jnp.mean(flat.astype(jnp.float32), axis=0)
    coupled = jnp.einsum("bp,bc->pc", flat, coupling, preferred_element_type=jnp.float32)
    weights = local_sea.reshape(points)
    updated = (
        weights[:, None] * (flat.astype(jnp.float32).T + coupled) / (1.0 + energy)[:, None]
    ).astype(jnp.bfloat16)
    owners_count = lax.axis_size("pts")
    capacity = max(2, (2 * points + owners_count - 1) // owners_count)
    target = owner.reshape(points)
    onehot = (target[:, None] == jnp.arange(owners_count, dtype=jnp.int32)[None, :]).astype(
        jnp.int32
    )
    slot_rank = jnp.sum(jnp.cumsum(onehot, axis=0) * onehot, axis=1) - 1
    slot_index = target * capacity + slot_rank
    selector = (
        slot_index[None, :] == jnp.arange(owners_count * capacity, dtype=jnp.int32)[:, None]
    ).astype(jnp.bfloat16)
    outgoing = jnp.dot(selector, updated, preferred_element_type=jnp.float32).astype(jnp.bfloat16)
    outgoing = outgoing.reshape(owners_count, capacity, all_bins)
    received = lax.all_to_all(outgoing, "pts", split_axis=0, concat_axis=0, tiled=True)
    return received.reshape(1, 1, owners_count * capacity, all_bins)


def local(spectrum, courant, upwind, coupling, sea, owner):
    bins_axis, owners_count = lax.axis_size("bins"), lax.axis_size("pts")
    points = owner.shape[2]
    suits = (
        spectrum.shape[2] == bins_axis * LANES
        and points % (2 * LANES) == 0
        and 2 * points == owners_count * LANES
        and bins_axis & (bins_axis - 1) == 0
        and owners_count & (owners_count - 1) == 0
        and bins_axis % 2 == 0
        and owners_count <= 8
    )
    form = chunked if suits else whole
    return form(spectrum, courant, upwind, coupling, sea, owner)


def solution(mesh):
    placed = (P("bins", "pts", None), P(), P(), P(), P("pts", None), P("pts", "bins", None, None))
    return jax.shard_map(
        local, mesh=mesh, in_specs=placed, out_specs=P("pts", "bins", None, None), check_vma=False
    )
```

```python
import functools

import jax
import jax.numpy as jnp
from jax import lax
from jax.experimental import pallas as pl
from jax.experimental.pallas import tpu as pltpu
from jax.sharding import PartitionSpec as P

F32 = jnp.float32
BF16 = jnp.bfloat16
I32 = jnp.int32
LANES = 128
CHUNKS = 2
NT = (((1,), (1,)), ((), ()))


def round_up(size, unit):
    return -(-size // unit) * unit


def iota(shape, axis):
    return lax.broadcasted_iota(I32, shape, axis)


def dot_nt(lhs, rhs):
    return lax.dot_general(lhs, rhs, NT, preferred_element_type=F32)


def pack_kernel(rows_out, bins_axis, owners_count, half, *refs):
    planes, low, high, coef, sea = refs[:5]
    owner = refs[5 : 5 + bins_axis]
    chunks = refs[5 + bins_axis : 5 + bins_axis + CHUNKS * bins_axis]
    meta = refs[5 + bins_axis + CHUNKS * bins_axis]
    moved = refs[-1]
    lon_rows, rows, lats = planes.shape
    points = lon_rows * LANES
    me = lax.axis_index("bins")
    me_pts = lax.axis_index("pts")

    tile = 16
    lane = iota((tile, lats), 1)
    sea_f = sea[...].astype(F32)

    def advect(step, carry):
        at = pl.ds(pl.multiple_of(step * tile, tile), tile)
        c = coef[at, :]
        cx, cy, ux, uy = c[:, 0:1], c[:, 1:2], c[:, 2:3], c[:, 3:4]
        masked = [low[at, :].astype(F32)]
        masked += [planes[l, at, :].astype(F32) for l in range(lon_rows)]
        masked += [high[at, :].astype(F32)]
        for l in range(lon_rows):
            center = masked[l + 1]
            donor_x = jnp.where(ux == 0.0, masked[l], masked[l + 2])
            left = jnp.where(lane == 0, 0.0, pltpu.roll(center, 1, 1))
            right = jnp.where(lane == lats - 1, 0.0, pltpu.roll(center, lats - 1, 1))
            donor_y = jnp.where(uy == 0.0, left, right)
            value = center - cx * (center - donor_x) - cy * (center - donor_y)
            moved[l, at, :] = (value * sea_f[l : l + 1, :]).astype(BF16)
        return carry

    lax.fori_loop(0, rows // tile, advect, 0)

    owners_id = iota((owners_count, points), 0)
    hot = [(owner[m][...] == owners_id).astype(F32) for m in range(bins_axis)]
    earlier = (iota((points, points), 0) < iota((points, points), 1)).astype(F32).astype(BF16)
    before = jnp.dot(
        jnp.concatenate(hot, axis=0).astype(BF16), earlier, preferred_element_type=F32
    )
    place_id = iota((points, points), 0)
    for m in range(bins_axis):
        own = owner[m][...]
        count = jnp.sum(hot[m], axis=1, keepdims=True)
        offset = jnp.sum(jnp.where(owners_id < own, count, 0.0), axis=0, keepdims=True)
        mine = before[m * owners_count : (m + 1) * owners_count, :]
        rank = jnp.sum(hot[m] * mine, axis=0, keepdims=True)
        key = (offset + rank).astype(I32)
        place = (key & 1) * half + (key >> 1)
        order = (place_id == place).astype(F32).astype(BF16)
        block = me ^ m
        at = pl.ds(pl.multiple_of(block * LANES, LANES), LANES)
        lhs = jnp.concatenate([moved[l, :, at] for l in range(lon_rows)], axis=1)
        ordered = dot_nt(lhs, order)[:rows_out]
        ordered = jnp.where((me & 1) == 1, pltpu.roll(ordered, 4, 0), ordered).astype(BF16)
        for c in range(CHUNKS):
            chunks[c * bins_axis + m][...] = ordered[:, c * half : (c + 1) * half]
        if m == 0:
            first = offset.astype(I32)
            slot = (key - first - (((key & 1) - first) & 1)) >> 1
            weight = jnp.concatenate([sea[l : l + 1, at].astype(F32) for l in range(lon_rows)], axis=1)
            facts = jnp.concatenate(
                [slot.astype(F32), (own ^ me_pts).astype(F32), rank, weight]
                + [jnp.zeros((1, points), F32)] * 4,
                axis=0,
            )
            meta[...] = dot_nt(facts.astype(BF16), order)


def transpose_kernel(coupling, out):
    bins = coupling.shape[0]
    for start in range(0, bins, 256):
        size = min(256, bins - start)
        eye = (iota((size, size), 0) == iota((size, size), 1)).astype(F32).astype(BF16)
        out[start : start + size, :] = dot_nt(eye, coupling[:, start : start + size]).astype(BF16)


def couple_kernel(chunk, bins_axis, owners_count, local_bins, slots, paired, *refs):
    blocks = refs[:bins_axis]
    weights, meta = refs[bins_axis : bins_axis + 2]
    outs = refs[-1 - (owners_count // 2 if paired else owners_count) : -1]
    values = refs[-1]
    rows, width = blocks[0].shape
    all_bins = values.shape[0]
    half_bins = all_bins // 2
    me = lax.axis_index("bins")
    values[...] = jnp.zeros_like(values)
    for m in range(bins_axis):
        block = me ^ m
        at = pl.ds(pl.multiple_of(block * local_bins - 4 * (block & 1), 8), rows)
        values[at, :] += blocks[m][...].astype(F32)
    flat = values[...].astype(BF16)
    energy = jnp.sum(values[...], axis=0, keepdims=True) / all_bins
    facts = meta[:, chunk * width : (chunk + 1) * width]
    scale = facts[3:4, :] / (1.0 + energy)
    slot, towards, rank = facts[0:1, :].astype(I32), facts[1:2, :].astype(I32), facts[2:3, :]
    slot_id = iota((owners_count * slots, width), 0)
    straight = (slot_id == towards * slots + slot).astype(F32).astype(BF16)
    crossed = (slot_id == (towards ^ 1) * slots + slot).astype(F32).astype(BF16)
    step = all_bins // 3
    for start in range(0, all_bins, step):
        at = slice(start, start + step)
        coupled = jnp.dot(weights[at, :], flat, preferred_element_type=F32)
        values[at, :] = (values[at, :] + coupled) * scale
    spare = jnp.zeros((7, width), F32)
    sent = []
    for group in range(2):
        updated = values[group * half_bins : (group + 1) * half_bins, :]
        updated = jnp.concatenate([updated, rank, spare], axis=0).astype(BF16)
        sent.append(dot_nt(updated, straight if group == chunk else crossed).astype(BF16))
    even, odd = sent[chunk], sent[1 - chunk]
    is_low = iota((half_bins + 8, LANES), 1) < slots
    for t in range(owners_count // 2):
        at = slice(t * LANES, (t + 1) * LANES)
        first = jnp.where(is_low, even[:, at], odd[:, at])
        second = jnp.where(is_low, odd[:, at], even[:, at])
        if paired:
            outs[t][0] = first
            outs[t][1] = second
        else:
            outs[2 * t][...] = first
            outs[2 * t + 1][...] = second


def place_kernel(owners_count, slots, *refs):
    pairs = owners_count // 2
    paired, swapped = refs[:pairs], refs[pairs]
    direct = refs[pairs + 1 : pairs + 1 + owners_count]
    out, staged, sems = refs[-3:]
    me = lax.axis_index("pts")
    tall = direct[0].shape[0]
    half_bins = tall - 8
    is_low = iota((tall, LANES), 1) < slots
    slot_id = iota((LANES, LANES), 0)
    copies = []
    for x in range(owners_count):
        early = paired[x // 2][0] if x % 2 == 0 else swapped[x // 2]
        first, second = (early, direct[x][...]) if x % 2 == 0 else (direct[x][...], early)
        pieces = []
        for lhs in (jnp.where(is_low, first, second), jnp.where(is_low, second, first)):
            rank = lhs[tall - 16 :, :].astype(F32)[8:9, :].astype(I32)
            place = (slot_id == rank).astype(F32).astype(BF16)
            pieces.append(dot_nt(lhs, place)[:half_bins])
        staged[x] = jnp.concatenate(pieces, axis=0).astype(BF16)
        at = pl.ds(pl.multiple_of((me ^ x) * LANES, LANES), LANES)
        copy = pltpu.make_async_copy(staged.at[x], out.at[:, at], sems.at[x])
        copy.start()
        copies.append(copy)
    for copy in copies:
        copy.wait()


def gate_kernel(array, after, out):
    del after
    out[...] = array[...]


def gate(array, after):
    return pl.pallas_call(
        gate_kernel,
        out_shape=jax.ShapeDtypeStruct(array.shape, array.dtype),
        in_specs=vmem(2),
        out_specs=vmem(1)[0],
        compiler_params=params(8),
        cost_estimate=cost(0, 4 * array.size),
        name="gate",
    )(array, after)


def stack_kernel(count, *refs):
    for t in range(count):
        refs[-1][t] = refs[t][1]


def stack(pairs, after):
    return pl.pallas_call(
        functools.partial(stack_kernel, len(pairs)),
        out_shape=jax.ShapeDtypeStruct((len(pairs),) + pairs[0].shape[1:], pairs[0].dtype),
        in_specs=vmem(len(pairs) + 1),
        out_specs=vmem(1)[0],
        compiler_params=params(8),
        cost_estimate=cost(0, 4 * sum(a.size for a in pairs)),
        name="stack",
    )(*pairs, after)


def params(mib):
    return pltpu.CompilerParams(vmem_limit_bytes=mib << 20)


def vmem(count):
    return [pl.BlockSpec(memory_space=pltpu.VMEM)] * count


def cost(flops, bytes_accessed):
    return pl.CostEstimate(flops=int(flops), bytes_accessed=int(bytes_accessed), transcendentals=0)


def exchange(array, axis, offset):
    return lax.ppermute(array, axis, [(i, i ^ offset) for i in range(lax.axis_size(axis))])


def chunked(spectrum, courant, upwind, coupling, sea, owner):
    local_bins, lon_rows, lats = spectrum.shape
    all_bins = courant.shape[0]
    bins_axis = lax.axis_size("bins")
    owners_count = lax.axis_size("pts")
    points = lon_rows * LANES
    half = points // CHUNKS
    slots = 2 * points // owners_count // CHUNKS
    tall = round_up(local_bins, 16)
    rows = round_up(local_bins + 1, 8)
    half_rows = all_bins // 2 + 8
    first_bin = lax.axis_index("bins") * local_bins

    masked = spectrum * sea.astype(BF16)[None]
    planes = jnp.pad(jnp.transpose(masked, (1, 0, 2)), ((0, 0), (0, tall - local_bins), (0, 0)))
    up = [(i, i + 1) for i in range(owners_count - 1)]
    down = [(i + 1, i) for i in range(owners_count - 1)]
    low = lax.ppermute(planes[lon_rows - 1], "pts", up)
    high = lax.ppermute(planes[0], "pts", down)
    own = owner.reshape(1, points)
    owners = [own] + [exchange(own, "bins", m) for m in range(1, bins_axis)]
    coef = jnp.concatenate([courant, upwind.astype(F32)], axis=1)
    coef = lax.dynamic_slice_in_dim(coef, first_bin, local_bins, 0)
    coef = jnp.pad(coef, ((0, tall - local_bins), (0, 0)))

    weights = pl.pallas_call(
        transpose_kernel,
        out_shape=jax.ShapeDtypeStruct(coupling.shape, BF16),
        in_specs=vmem(1),
        out_specs=vmem(1)[0],
        compiler_params=params(16),
        cost_estimate=cost(2 * 256 * all_bins * all_bins, 7e6),
        name="transpose",
    )(coupling)

    packed = pl.pallas_call(
        functools.partial(pack_kernel, rows, bins_axis, owners_count, half),
        out_shape=[jax.ShapeDtypeStruct((rows, half), BF16)] * (CHUNKS * bins_axis)
        + [jax.ShapeDtypeStruct((8, points), F32)],
        in_specs=vmem(5 + bins_axis),
        out_specs=vmem(CHUNKS * bins_axis + 1),
        scratch_shapes=[pltpu.VMEM((lon_rows, tall, lats), BF16)],
        compiler_params=params(16),
        cost_estimate=cost(2 * bins_axis * tall * points * points, 4e6),
        name="pack",
    )(planes, low, high, coef, sea, *owners)
    meta = packed[-1]

    def couple(c, blocks, ready, paired):
        shape, count = ((half_rows, LANES), owners_count)
        if paired:
            shape, count = (2,) + shape, count // 2
        return pl.pallas_call(
            functools.partial(
                couple_kernel, c, bins_axis, owners_count, local_bins, slots, paired
            ),
            out_shape=[jax.ShapeDtypeStruct(shape, BF16)] * count,
            in_specs=vmem(len(blocks) + 2 + len(ready)),
            out_specs=vmem(count),
            scratch_shapes=[pltpu.VMEM((all_bins, half), F32)],
            compiler_params=params(16),
            cost_estimate=cost(2 * all_bins * all_bins * half + 4 * all_bins * half * 512, 6e6),
            name="couple",
        )(*blocks, weights, meta, *ready)

    early, late = packed[:bins_axis], packed[bins_axis : 2 * bins_axis]
    first = [exchange(early[m], "bins", m) for m in range(1, bins_axis)]
    late = [late[0]] + [gate(b, after) for b, after in zip(late[1:], first)]
    second = [exchange(late[m], "bins", m) for m in range(1, bins_axis)]
    pays = couple(0, [early[0], *first], late[1:], True)
    pairs = [pays[0]] + [exchange(pays[t], "pts", 2 * t) for t in range(1, owners_count // 2)]
    pays = couple(1, [late[0], *second], [], False)
    direct = [pays[0]] + [exchange(pays[x], "pts", x) for x in range(1, owners_count)]
    arrivals = [*pairs, exchange(stack(pairs, pays[0]), "pts", 1), *direct]

    placed = pl.pallas_call(
        functools.partial(place_kernel, owners_count, slots),
        out_shape=jax.ShapeDtypeStruct((all_bins, owners_count * LANES), BF16),
        in_specs=vmem(len(arrivals)),
        out_specs=pl.BlockSpec(memory_space=pl.ANY),
        scratch_shapes=[
            pltpu.VMEM((owners_count, all_bins, LANES), BF16),
            pltpu.SemaphoreType.DMA((owners_count,)),
        ],
        compiler_params=params(16),
        cost_estimate=cost(4 * all_bins * LANES * LANES * owners_count, 8e6),
        name="place",
    )(*arrivals)
    return jnp.transpose(placed).reshape(1, 1, owners_count * LANES, all_bins)


def padded_2(block, sides, width):
    for axis, dim in sides:
        count = lax.axis_size(axis)
        forward = [(i, i + 1) for i in range(count - 1)]
        backward = [(target, source) for source, target in forward]
        low = lax.ppermute(
            lax.slice_in_dim(block, block.shape[dim] - width, None, axis=dim), axis, forward
        )
        high = lax.ppermute(lax.slice_in_dim(block, 0, width, axis=dim), axis, backward)
        block = jnp.concatenate([low, block, high], axis=dim)
    return block


def advect(padded, sea_mask, courant, upwind):
    center = padded[:, 1:-1, 1:-1]
    donor_x = jnp.where(upwind[:, 0][:, None, None] == 0, padded[:, :-2, 1:-1], padded[:, 2:, 1:-1])
    donor_y = jnp.where(upwind[:, 1][:, None, None] == 0, padded[:, 1:-1, :-2], padded[:, 1:-1, 2:])
    moved = (
        center
        - courant[:, 0][:, None, None] * (center - donor_x)
        - courant[:, 1][:, None, None] * (center - donor_y)
    )
    return (moved * sea_mask[None]).astype(jnp.bfloat16)


def whole(spectrum, courant, upwind, coupling, sea, owner):
    local_bins = spectrum.shape[0]
    lon_rows = spectrum.shape[1]
    bins_count = lax.axis_size("bins")
    lat_cells = spectrum.shape[2] // bins_count
    masked = spectrum * sea.astype(jnp.bfloat16)[None]
    local_sea = lax.dynamic_slice_in_dim(
        sea, lax.axis_index("bins") * lat_cells, lat_cells, 1
    ).astype(jnp.float32)
    first_bin = lax.axis_index("bins") * local_bins
    my_courant = lax.dynamic_slice_in_dim(courant, first_bin, local_bins, 0)
    my_upwind = lax.dynamic_slice_in_dim(upwind, first_bin, local_bins, 0)
    extended = padded_2(masked, (("pts", 1),), 1)
    extended = jnp.pad(extended.astype(jnp.float32), ((0, 0), (0, 0), (1, 1)))
    moved = advect(extended, sea.astype(jnp.float32), my_courant, my_upwind)
    columns = lax.all_to_all(moved, "bins", split_axis=2, concat_axis=0, tiled=True)
    all_bins = columns.shape[0]
    points = lon_rows * lat_cells
    flat = columns.reshape(all_bins, points)
    energy = jnp.mean(flat.astype(jnp.float32), axis=0)
    coupled = jnp.einsum("bp,bc->pc", flat, coupling, preferred_element_type=jnp.float32)
    weights = local_sea.reshape(points)
    updated = (
        weights[:, None] * (flat.astype(jnp.float32).T + coupled) / (1.0 + energy)[:, None]
    ).astype(jnp.bfloat16)
    owners_count = lax.axis_size("pts")
    capacity = max(2, (2 * points + owners_count - 1) // owners_count)
    target = owner.reshape(points)
    onehot = (target[:, None] == jnp.arange(owners_count, dtype=jnp.int32)[None, :]).astype(
        jnp.int32
    )
    slot_rank = jnp.sum(jnp.cumsum(onehot, axis=0) * onehot, axis=1) - 1
    slot_index = target * capacity + slot_rank
    selector = (
        slot_index[None, :] == jnp.arange(owners_count * capacity, dtype=jnp.int32)[:, None]
    ).astype(jnp.bfloat16)
    outgoing = jnp.dot(selector, updated, preferred_element_type=jnp.float32).astype(jnp.bfloat16)
    outgoing = outgoing.reshape(owners_count, capacity, all_bins)
    received = lax.all_to_all(outgoing, "pts", split_axis=0, concat_axis=0, tiled=True)
    return received.reshape(1, 1, owners_count * capacity, all_bins)


def local(spectrum, courant, upwind, coupling, sea, owner):
    bins_axis, owners_count = lax.axis_size("bins"), lax.axis_size("pts")
    points = owner.shape[2]
    suits = (
        spectrum.shape[2] == bins_axis * LANES
        and points % (2 * LANES) == 0
        and 2 * points == owners_count * LANES
        and bins_axis & (bins_axis - 1) == 0
        and owners_count & (owners_count - 1) == 0
        and bins_axis % 2 == 0
        and spectrum.shape[0] % 8 == 4
        and courant.shape[0] % 48 == 0
        and owners_count <= 8
    )
    form = chunked if suits else whole
    return form(spectrum, courant, upwind, coupling, sea, owner)


def solution(mesh):
    placed = (P("bins", "pts", None), P(), P(), P(), P("pts", None), P("pts", "bins", None, None))
    return jax.shard_map(
        local, mesh=mesh, in_specs=placed, out_specs=P("pts", "bins", None, None), check_vma=False
    )
```

```python
import functools

import jax
import jax.numpy as jnp
from jax import lax
from jax.experimental import pallas as pl
from jax.experimental.pallas import tpu as pltpu
from jax.sharding import PartitionSpec as P

F32 = jnp.float32
BF16 = jnp.bfloat16
I32 = jnp.int32
LANES = 128
CHUNKS = 2
NT = (((1,), (1,)), ((), ()))


def round_up(size, unit):
    return -(-size // unit) * unit


def iota(shape, axis):
    return lax.broadcasted_iota(I32, shape, axis)


def dot_nt(lhs, rhs):
    return lax.dot_general(lhs, rhs, NT, preferred_element_type=F32)


def upwind_row(at, speed, side, before, center, after, sea_row):
    lats = center.shape[1]
    lane = iota(center.shape, 1)
    wide = lats // LANES
    cx, cy = [jnp.concatenate([speed[k, at, :]] * wide, axis=1) for k in range(2)]
    ux, uy = [jnp.concatenate([side[k, at, :]] * wide, axis=1) for k in range(2)]
    donor_x = jnp.where(ux == 0, before, after).astype(F32)
    left = jnp.where(lane == 0, 0, pltpu.roll(center, 1, 1))
    right = jnp.where(lane == lats - 1, 0, pltpu.roll(center, lats - 1, 1))
    donor_y = jnp.where(uy == 0, left, right).astype(F32)
    center = center.astype(F32)
    value = center - cx * (center - donor_x) - cy * (center - donor_y)
    return (value * sea_row).astype(BF16)


def columns(moved, block):
    at = pl.ds(pl.multiple_of(block * LANES, LANES), LANES)
    return jnp.concatenate([moved[l, :, at] for l in range(moved.shape[0])], axis=1)


def inner_kernel(bins_axis, owners_count, half, *refs):
    planes, speed, side, sea = refs[:4]
    owner = refs[4 : 4 + bins_axis]
    inner, rim_order, meta, moved = refs[4 + bins_axis :]
    lon_rows, rows, _ = planes.shape
    points = lon_rows * LANES
    me = lax.axis_index("bins")
    me_pts = lax.axis_index("pts")
    sea_f = sea[...].astype(F32)
    sea_b = sea_f.astype(BF16)

    def step(index, carry):
        at = pl.ds(pl.multiple_of(index * 16, 16), 16)
        masked = [planes[l, at, :] * sea_b[l : l + 1, :] for l in range(lon_rows)]
        for l in range(1, lon_rows - 1):
            moved[l - 1, at, :] = upwind_row(
                at, speed, side, masked[l - 1], masked[l], masked[l + 1], sea_f[l : l + 1, :]
            )
        return carry

    lax.fori_loop(0, rows // 16, step, 0, unroll=7)

    owners_id = iota((owners_count, points), 0)
    hot = [(owner[m][...] == owners_id).astype(F32) for m in range(bins_axis)]
    earlier = (iota((points, points), 0) < iota((points, points), 1)).astype(F32).astype(BF16)
    before = jnp.dot(
        jnp.concatenate(hot, axis=0).astype(BF16), earlier, preferred_element_type=F32
    )
    place_id = iota((points, points), 0)
    last = (lon_rows - 1) * LANES
    for m in range(bins_axis):
        own = owner[m][...]
        count = jnp.sum(hot[m], axis=1, keepdims=True)
        offset = jnp.sum(jnp.where(owners_id < own, count, 0.0), axis=0, keepdims=True)
        mine = before[m * owners_count : (m + 1) * owners_count, :]
        rank = jnp.sum(hot[m] * mine, axis=0, keepdims=True)
        key = (offset + rank).astype(I32)
        place = (key & 1) * half + (key >> 1)
        order = (place_id == place).astype(F32).astype(BF16)
        inner[m] = dot_nt(columns(moved, me ^ m), order[:, LANES:last]).astype(BF16)
        rim_order[m, :, :LANES] = order[:, :LANES]
        rim_order[m, :, LANES:] = order[:, last:]
        if m == 0:
            first = offset.astype(I32)
            slot = (key - first - (((key & 1) - first) & 1)) >> 1
            at = pl.ds(pl.multiple_of(me * LANES, LANES), LANES)
            weight = jnp.concatenate([sea[l : l + 1, at].astype(F32) for l in range(lon_rows)], axis=1)
            facts = jnp.concatenate(
                [slot.astype(F32), (own ^ me_pts).astype(F32), rank, weight]
                + [jnp.zeros((1, points), F32)] * 4,
                axis=0,
            )
            meta[...] = dot_nt(facts.astype(BF16), order)


def pack_kernel(rows_out, bins_axis, half, *refs):
    planes, low, high, speed, side, sea, inner, rim_order = refs[:8]
    chunks, moved = refs[8:-1], refs[-1]
    lon_rows, rows, _ = planes.shape
    me = lax.axis_index("bins")
    sea_f = sea[...].astype(F32)
    sea_b = sea_f.astype(BF16)

    top = lon_rows - 1

    def rim(at, below, above):
        masked = [planes[l, at, :] * sea_b[l : l + 1, :] for l in (0, 1, top - 1, top)]
        moved[0, at, :] = upwind_row(
            at, speed, side, below, masked[0], masked[1], sea_f[0:1, :]
        )
        moved[1, at, :] = upwind_row(
            at, speed, side, masked[2], masked[3], above, sea_f[top : top + 1, :]
        )

    def step(index, carry):
        at = pl.ds(pl.multiple_of(index * 16, 16), 16)
        rim(at, low[at, :], high[at, :])
        return carry

    held = low.shape[0]
    full = held // 16 * 16
    lax.fori_loop(0, full // 16, step, 0, unroll=5)
    if full < rows:
        spare = jnp.zeros((rows - held, low.shape[1]), F32)
        ends = [
            jnp.concatenate([h[full:, :].astype(F32), spare], axis=0).astype(BF16) for h in (low, high)
        ]
        rim(pl.ds(full, 16), *ends)
    for m in range(bins_axis):
        ordered = dot_nt(columns(moved, me ^ m), rim_order[m]) + inner[m].astype(F32)
        ordered = ordered[:rows_out]
        ordered = jnp.where((me & 1) == 1, pltpu.roll(ordered, 4, 0), ordered).astype(BF16)
        for c in range(CHUNKS):
            chunks[c * bins_axis + m][...] = ordered[:, c * half : (c + 1) * half]


def transpose_kernel(coupling, out):
    bins = coupling.shape[0]
    for start in range(0, bins, 256):
        size = min(256, bins - start)
        eye = (iota((size, size), 0) == iota((size, size), 1)).astype(F32).astype(BF16)
        out[start : start + size, :] = dot_nt(eye, coupling[:, start : start + size]).astype(BF16)


def couple_kernel(chunk, bins_axis, local_bins, slots, paired, *refs):
    blocks = refs[:bins_axis]
    weights, meta = refs[bins_axis : bins_axis + 2]
    values = refs[-1]
    owners_count = 2 * len(paired)
    outs = list(refs[-1 - sum(1 if pair else 2 for pair in paired) : -1])
    rows, width = blocks[0].shape
    all_bins = values.shape[0]
    half_bins = all_bins // 2
    me = lax.axis_index("bins")
    values[...] = jnp.zeros_like(values)
    for m in range(bins_axis):
        block = me ^ m
        at = pl.ds(pl.multiple_of(block * local_bins - 4 * (block & 1), 8), rows)
        values[at, :] += blocks[m][...].astype(F32)
    flat = values[...].astype(BF16)
    energy = jnp.sum(values[...], axis=0, keepdims=True) / all_bins
    facts = meta[:, chunk * width : (chunk + 1) * width]
    scale = facts[3:4, :] / (1.0 + energy)
    slot, towards, rank = facts[0:1, :].astype(I32), facts[1:2, :].astype(I32), facts[2:3, :]
    slot_id = iota((owners_count * slots, width), 0)
    straight = (slot_id == towards * slots + slot).astype(F32).astype(BF16)
    crossed = (slot_id == (towards ^ 1) * slots + slot).astype(F32).astype(BF16)
    step = all_bins // 3
    for start in range(0, all_bins, step):
        at = slice(start, start + step)
        coupled = jnp.dot(weights[at, :], flat, preferred_element_type=F32)
        values[at, :] = (values[at, :] + coupled) * scale
    spare = jnp.zeros((7, width), F32)
    sent = []
    for group in range(2):
        updated = values[group * half_bins : (group + 1) * half_bins, :]
        updated = jnp.concatenate([updated, rank, spare], axis=0).astype(BF16)
        sent.append(dot_nt(updated, straight if group == chunk else crossed).astype(BF16))
    even, odd = sent[chunk], sent[1 - chunk]
    is_low = iota((half_bins + 8, LANES), 1) < slots
    for t in range(owners_count // 2):
        at = slice(t * LANES, (t + 1) * LANES)
        first = jnp.where(is_low, even[:, at], odd[:, at])
        second = jnp.where(is_low, odd[:, at], even[:, at])
        if paired[t]:
            out = outs.pop(0)
            out[0], out[1] = first, second
        else:
            outs.pop(0)[...] = first
            outs.pop(0)[...] = second


def place_kernel(slots, sources, picks, *refs):
    out, staged, sems = refs[-3:]
    me = lax.axis_index("pts")
    tall = refs[0].shape[-2]
    half_bins = tall - 8
    is_low = iota((tall, LANES), 1) < slots
    slot_id = iota((LANES, LANES), 0)

    def block(pick):
        ref, index = refs[pick[0]], pick[1]
        return ref[...] if index is None else ref[index]

    copies = []
    for number, x in enumerate(sources):
        first, second = [block(picks[number][c]) for c in range(CHUNKS)]
        if x % 2 == 1:
            first, second = second, first
        pieces = []
        for lhs in (jnp.where(is_low, first, second), jnp.where(is_low, second, first)):
            rank = lhs[tall - 16 :, :].astype(F32)[8:9, :].astype(I32)
            place = (slot_id == rank).astype(F32).astype(BF16)
            pieces.append(dot_nt(lhs, place)[:half_bins])
        staged[number] = jnp.concatenate(pieces, axis=0).astype(BF16)
        at = pl.ds(pl.multiple_of((me ^ x) * LANES, LANES), LANES)
        copy = pltpu.make_async_copy(staged.at[number], out.at[:, at], sems.at[number])
        copy.start()
        copies.append(copy)
    for copy in copies:
        copy.wait()


def place(out, slots, owners_count, all_bins, sources):
    arrays, picks = [], []
    for x in sorted(sources):
        mine = []
        for array, index in sources[x]:
            known = [n for n, a in enumerate(arrays) if a is array]
            if not known:
                arrays.append(array)
                known = [len(arrays) - 1]
            mine.append((known[0], index))
        picks.append(tuple(mine))
    held = [] if out is None else [out]
    return pl.pallas_call(
        functools.partial(place_kernel, slots, tuple(sorted(sources)), tuple(picks)),
        out_shape=jax.ShapeDtypeStruct((all_bins, owners_count * LANES), BF16),
        in_specs=vmem(len(arrays)) + [pl.BlockSpec(memory_space=pl.ANY)] * len(held),
        out_specs=pl.BlockSpec(memory_space=pl.ANY),
        scratch_shapes=[
            pltpu.VMEM((len(sources), all_bins, LANES), BF16),
            pltpu.SemaphoreType.DMA((len(sources),)),
        ],
        input_output_aliases={len(arrays): 0} if held else {},
        compiler_params=params(16),
        cost_estimate=cost(4 * all_bins * LANES * LANES * len(sources), 1e6 * len(sources)),
        name="place",
    )(*arrays, *held)


def gate_kernel(array, after, out):
    del after
    out[...] = array[...]


def gate(array, after):
    return pl.pallas_call(
        gate_kernel,
        out_shape=jax.ShapeDtypeStruct(array.shape, array.dtype),
        in_specs=vmem(2),
        out_specs=vmem(1)[0],
        compiler_params=params(8),
        cost_estimate=cost(0, 4 * array.size),
        name="gate",
    )(array, after)


def stack_kernel(count, *refs):
    for t in range(count):
        refs[-1][t] = refs[t][1]


def stack(pairs, after):
    return pl.pallas_call(
        functools.partial(stack_kernel, len(pairs)),
        out_shape=jax.ShapeDtypeStruct((len(pairs),) + pairs[0].shape[1:], pairs[0].dtype),
        in_specs=vmem(len(pairs) + 1),
        out_specs=vmem(1)[0],
        compiler_params=params(8),
        cost_estimate=cost(0, 4 * sum(a.size for a in pairs)),
        name="stack",
    )(*pairs, after)


def params(mib):
    return pltpu.CompilerParams(vmem_limit_bytes=mib << 20)


def vmem(count):
    return [pl.BlockSpec(memory_space=pltpu.VMEM)] * count


def cost(flops, bytes_accessed):
    del flops, bytes_accessed
    return pl.CostEstimate(flops=1, bytes_accessed=1, transcendentals=0)


def exchange(array, axis, offset):
    return lax.ppermute(array, axis, [(i, i ^ offset) for i in range(lax.axis_size(axis))])


def chunked(spectrum, courant, upwind, coupling, sea, owner):
    local_bins, lon_rows, lats = spectrum.shape
    all_bins = courant.shape[0]
    bins_axis = lax.axis_size("bins")
    owners_count = lax.axis_size("pts")
    points = lon_rows * LANES
    half = points // CHUNKS
    slots = 2 * points // owners_count // CHUNKS
    tall = round_up(local_bins, 16)
    rows = round_up(local_bins + 1, 8)
    half_rows = all_bins // 2 + 8
    first_bin = lax.axis_index("bins") * local_bins

    planes = jnp.pad(jnp.transpose(spectrum, (1, 0, 2)), ((0, 0), (0, tall - local_bins), (0, 0)))
    edges = [planes[r, :local_bins] * sea[r].astype(BF16)[None] for r in (0, lon_rows - 1)]
    up = [(i, i + 1) for i in range(owners_count - 1)]
    down = [(i + 1, i) for i in range(owners_count - 1)]
    low = lax.ppermute(edges[1], "pts", up)
    high = lax.ppermute(edges[0], "pts", down)
    own = owner.reshape(1, points)
    owners = [own] + [exchange(own, "bins", m) for m in range(1, bins_axis)]
    def wide(table, dtype):
        mine = lax.dynamic_slice_in_dim(table.T, first_bin, local_bins, 1).astype(dtype)
        mine = jnp.pad(mine, ((0, 0), (0, tall - local_bins)))
        return jnp.broadcast_to(mine[:, :, None], (2, tall, LANES))

    speed, side = wide(courant, F32), wide(upwind, BF16)

    weights = pl.pallas_call(
        transpose_kernel,
        out_shape=jax.ShapeDtypeStruct(coupling.shape, BF16),
        in_specs=vmem(1),
        out_specs=vmem(1)[0],
        compiler_params=params(16),
        cost_estimate=cost(2 * 256 * all_bins * all_bins, 7e6),
        name="transpose",
    )(coupling)

    inner, rim_order, meta = pl.pallas_call(
        functools.partial(inner_kernel, bins_axis, owners_count, half),
        out_shape=[
            jax.ShapeDtypeStruct((bins_axis, tall, points), BF16),
            jax.ShapeDtypeStruct((bins_axis, points, 2 * LANES), BF16),
            jax.ShapeDtypeStruct((8, points), F32),
        ],
        in_specs=vmem(4 + bins_axis),
        out_specs=vmem(3),
        scratch_shapes=[pltpu.VMEM((lon_rows - 2, tall, lats), BF16)],
        compiler_params=params(16),
        cost_estimate=cost(bins_axis * tall * points * points, 4e6),
        name="inner",
    )(planes, speed, side, sea, *owners)
    packed = pl.pallas_call(
        functools.partial(pack_kernel, rows, bins_axis, half),
        out_shape=[jax.ShapeDtypeStruct((rows, half), BF16)] * (CHUNKS * bins_axis),
        in_specs=vmem(8),
        out_specs=vmem(CHUNKS * bins_axis),
        scratch_shapes=[pltpu.VMEM((2, tall, lats), BF16)],
        compiler_params=params(16),
        cost_estimate=cost(bins_axis * tall * points * points, 4e6),
        name="pack",
    )(planes, low, high, speed, side, sea, inner, rim_order)

    def couple(c, blocks, ready, paired):
        shapes = [[(2, half_rows, LANES)] if pair else [(half_rows, LANES)] * 2 for pair in paired]
        shapes = sum(shapes, [])
        return list(pl.pallas_call(
            functools.partial(couple_kernel, c, bins_axis, local_bins, slots, paired),
            out_shape=[jax.ShapeDtypeStruct(shape, BF16) for shape in shapes],
            in_specs=vmem(len(blocks) + 2 + len(ready)),
            out_specs=vmem(len(shapes)),
            scratch_shapes=[pltpu.VMEM((all_bins, half), F32)],
            compiler_params=params(16),
            cost_estimate=cost(2 * all_bins * all_bins * half + 4 * all_bins * half * 512, 6e6),
            name="couple",
        )(*blocks, weights, meta, *ready))

    pairs = owners_count // 2
    early, late = packed[:bins_axis], packed[bins_axis : 2 * bins_axis]
    first = [exchange(early[m], "bins", m) for m in range(1, bins_axis)]
    late = [late[0]] + [gate(b, after) for b, after in zip(late[1:], first)]
    second = [exchange(late[m], "bins", m) for m in range(1, bins_axis)]
    pays = couple(0, [early[0], *first], [*late[2:], second[0]], (True,) * pairs)
    came = {0: pays[0]}
    for t in range(pairs - 1, 0, -1):
        came[t] = exchange(pays[t], "pts", 2 * t)
    pays = couple(1, [late[0], *second], [], (True,) * pairs)
    last = {0: pays[0]}
    for t in range(pairs - 1, 0, -1):
        last[t] = exchange(pays[t], "pts", 2 * t)
    swapped = exchange(stack([came[t] for t in range(pairs)], last[pairs - 1]), "pts", 1)
    swapped_late = exchange(stack([last[t] for t in range(pairs)], last[0]), "pts", 1)

    shape = (slots, owners_count, all_bins)
    placed = place(None, *shape, {2 * t: [(came[t], 0), (last[t], 0)] for t in range(pairs)})
    placed = place(
        placed, *shape, {2 * t + 1: [(swapped, t), (swapped_late, t)] for t in range(pairs)}
    )
    return jnp.transpose(placed).reshape(1, 1, owners_count * LANES, all_bins)


def padded_2(block, sides, width):
    for axis, dim in sides:
        count = lax.axis_size(axis)
        forward = [(i, i + 1) for i in range(count - 1)]
        backward = [(target, source) for source, target in forward]
        low = lax.ppermute(
            lax.slice_in_dim(block, block.shape[dim] - width, None, axis=dim), axis, forward
        )
        high = lax.ppermute(lax.slice_in_dim(block, 0, width, axis=dim), axis, backward)
        block = jnp.concatenate([low, block, high], axis=dim)
    return block


def advect(padded, sea_mask, courant, upwind):
    center = padded[:, 1:-1, 1:-1]
    donor_x = jnp.where(upwind[:, 0][:, None, None] == 0, padded[:, :-2, 1:-1], padded[:, 2:, 1:-1])
    donor_y = jnp.where(upwind[:, 1][:, None, None] == 0, padded[:, 1:-1, :-2], padded[:, 1:-1, 2:])
    moved = (
        center
        - courant[:, 0][:, None, None] * (center - donor_x)
        - courant[:, 1][:, None, None] * (center - donor_y)
    )
    return (moved * sea_mask[None]).astype(jnp.bfloat16)


def whole(spectrum, courant, upwind, coupling, sea, owner):
    local_bins = spectrum.shape[0]
    lon_rows = spectrum.shape[1]
    bins_count = lax.axis_size("bins")
    lat_cells = spectrum.shape[2] // bins_count
    masked = spectrum * sea.astype(jnp.bfloat16)[None]
    local_sea = lax.dynamic_slice_in_dim(
        sea, lax.axis_index("bins") * lat_cells, lat_cells, 1
    ).astype(jnp.float32)
    first_bin = lax.axis_index("bins") * local_bins
    my_courant = lax.dynamic_slice_in_dim(courant, first_bin, local_bins, 0)
    my_upwind = lax.dynamic_slice_in_dim(upwind, first_bin, local_bins, 0)
    extended = padded_2(masked, (("pts", 1),), 1)
    extended = jnp.pad(extended.astype(jnp.float32), ((0, 0), (0, 0), (1, 1)))
    moved = advect(extended, sea.astype(jnp.float32), my_courant, my_upwind)
    columns = lax.all_to_all(moved, "bins", split_axis=2, concat_axis=0, tiled=True)
    all_bins = columns.shape[0]
    points = lon_rows * lat_cells
    flat = columns.reshape(all_bins, points)
    energy = jnp.mean(flat.astype(jnp.float32), axis=0)
    coupled = jnp.einsum("bp,bc->pc", flat, coupling, preferred_element_type=jnp.float32)
    weights = local_sea.reshape(points)
    updated = (
        weights[:, None] * (flat.astype(jnp.float32).T + coupled) / (1.0 + energy)[:, None]
    ).astype(jnp.bfloat16)
    owners_count = lax.axis_size("pts")
    capacity = max(2, (2 * points + owners_count - 1) // owners_count)
    target = owner.reshape(points)
    onehot = (target[:, None] == jnp.arange(owners_count, dtype=jnp.int32)[None, :]).astype(
        jnp.int32
    )
    slot_rank = jnp.sum(jnp.cumsum(onehot, axis=0) * onehot, axis=1) - 1
    slot_index = target * capacity + slot_rank
    selector = (
        slot_index[None, :] == jnp.arange(owners_count * capacity, dtype=jnp.int32)[:, None]
    ).astype(jnp.bfloat16)
    outgoing = jnp.dot(selector, updated, preferred_element_type=jnp.float32).astype(jnp.bfloat16)
    outgoing = outgoing.reshape(owners_count, capacity, all_bins)
    received = lax.all_to_all(outgoing, "pts", split_axis=0, concat_axis=0, tiled=True)
    return received.reshape(1, 1, owners_count * capacity, all_bins)


def local(spectrum, courant, upwind, coupling, sea, owner):
    bins_axis, owners_count = lax.axis_size("bins"), lax.axis_size("pts")
    points = owner.shape[2]
    suits = (
        spectrum.shape[2] == bins_axis * LANES
        and points % (2 * LANES) == 0
        and 2 * points == owners_count * LANES
        and bins_axis & (bins_axis - 1) == 0
        and owners_count & (owners_count - 1) == 0
        and bins_axis % 2 == 0
        and spectrum.shape[0] % 8 == 4
        and courant.shape[0] % 48 == 0
        and owners_count == 8
        and spectrum.shape[1] >= 3
    )
    form = chunked if suits else whole
    return form(spectrum, courant, upwind, coupling, sea, owner)


def solution(mesh):
    placed = (P("bins", "pts", None), P(), P(), P(), P("pts", None), P("pts", "bins", None, None))
    return jax.shard_map(
        local, mesh=mesh, in_specs=placed, out_specs=P("pts", "bins", None, None), check_vma=False
    )
```

```python
import functools

import jax
import jax.numpy as jnp
from jax import lax
from jax.experimental import pallas as pl
from jax.experimental.pallas import tpu as pltpu
from jax.sharding import PartitionSpec as P

F32 = jnp.float32
BF16 = jnp.bfloat16
I32 = jnp.int32
LANES = 128
CHUNKS = 2
NT = (((1,), (1,)), ((), ()))


def round_up(size, unit):
    return -(-size // unit) * unit


def iota(shape, axis):
    return lax.broadcasted_iota(I32, shape, axis)


def dot_nt(lhs, rhs):
    return lax.dot_general(lhs, rhs, NT, preferred_element_type=F32)


def upwind_row(at, speed, side, before, center, after, sea_row):
    lats = center.shape[1]
    lane = iota(center.shape, 1)
    wide = lats // LANES
    cx, cy = [jnp.concatenate([speed[k, at, :]] * wide, axis=1) for k in range(2)]
    ux, uy = [jnp.concatenate([side[k, at, :]] * wide, axis=1) for k in range(2)]
    donor_x = jnp.where(ux == 0, before, after).astype(F32)
    left = jnp.where(lane == 0, 0, pltpu.roll(center, 1, 1))
    right = jnp.where(lane == lats - 1, 0, pltpu.roll(center, lats - 1, 1))
    donor_y = jnp.where(uy == 0, left, right).astype(F32)
    center = center.astype(F32)
    value = center - cx * (center - donor_x) - cy * (center - donor_y)
    return (value * sea_row).astype(BF16)


def columns(moved, block):
    at = pl.ds(pl.multiple_of(block * LANES, LANES), LANES)
    return jnp.concatenate([moved[l, :, at] for l in range(moved.shape[0])], axis=1)


def inner_kernel(bins_axis, owners_count, half, *refs):
    planes, speed, side, sea = refs[:4]
    owner = refs[4 : 4 + bins_axis]
    inner, rim_order, meta, moved = refs[4 + bins_axis :]
    lon_rows, rows, _ = planes.shape
    points = lon_rows * LANES
    me = lax.axis_index("bins")
    me_pts = lax.axis_index("pts")
    sea_f = sea[...].astype(F32)
    sea_b = sea_f.astype(BF16)

    def step(index, carry):
        at = pl.ds(pl.multiple_of(index * 16, 16), 16)
        masked = [planes[l, at, :] * sea_b[l : l + 1, :] for l in range(lon_rows)]
        for l in range(1, lon_rows - 1):
            moved[l - 1, at, :] = upwind_row(
                at, speed, side, masked[l - 1], masked[l], masked[l + 1], sea_f[l : l + 1, :]
            )
        return carry

    lax.fori_loop(0, rows // 16, step, 0, unroll=7)

    owners_id = iota((owners_count, points), 0)
    hot = [(owner[m][...] == owners_id).astype(F32) for m in range(bins_axis)]
    earlier = (iota((points, points), 0) < iota((points, points), 1)).astype(F32).astype(BF16)
    before = jnp.dot(
        jnp.concatenate(hot, axis=0).astype(BF16), earlier, preferred_element_type=F32
    )
    place_id = iota((points, points), 0)
    last = (lon_rows - 1) * LANES
    for m in range(bins_axis):
        own = owner[m][...]
        count = jnp.sum(hot[m], axis=1, keepdims=True)
        offset = jnp.sum(jnp.where(owners_id < own, count, 0.0), axis=0, keepdims=True)
        mine = before[m * owners_count : (m + 1) * owners_count, :]
        rank = jnp.sum(hot[m] * mine, axis=0, keepdims=True)
        key = (offset + rank).astype(I32)
        place = (key & 1) * half + (key >> 1)
        order = (place_id == place).astype(F32).astype(BF16)
        inner[m] = dot_nt(columns(moved, me ^ m), order[:, LANES:last]).astype(BF16)
        rim_order[m, :, :LANES] = order[:, :LANES]
        rim_order[m, :, LANES:] = order[:, last:]
        if m == 0:
            first = offset.astype(I32)
            slot = (key - first - (((key & 1) - first) & 1)) >> 1
            at = pl.ds(pl.multiple_of(me * LANES, LANES), LANES)
            weight = jnp.concatenate([sea[l : l + 1, at].astype(F32) for l in range(lon_rows)], axis=1)
            facts = jnp.concatenate(
                [slot.astype(F32), (own ^ me_pts).astype(F32), rank, weight]
                + [jnp.zeros((1, points), F32)] * 4,
                axis=0,
            )
            meta[...] = dot_nt(facts.astype(BF16), order)


def pack_kernel(rows_out, bins_axis, half, *refs):
    planes, low, high, speed, side, sea, inner, rim_order = refs[:8]
    chunks, moved = refs[8:-1], refs[-1]
    lon_rows, rows, _ = planes.shape
    me = lax.axis_index("bins")
    sea_f = sea[...].astype(F32)
    sea_b = sea_f.astype(BF16)

    top = lon_rows - 1

    def rim(at, below, above):
        masked = [planes[l, at, :] * sea_b[l : l + 1, :] for l in (0, 1, top - 1, top)]
        moved[0, at, :] = upwind_row(
            at, speed, side, below, masked[0], masked[1], sea_f[0:1, :]
        )
        moved[1, at, :] = upwind_row(
            at, speed, side, masked[2], masked[3], above, sea_f[top : top + 1, :]
        )

    def step(index, carry):
        at = pl.ds(pl.multiple_of(index * 16, 16), 16)
        rim(at, low[at, :], high[at, :])
        return carry

    held = low.shape[0]
    full = held // 16 * 16
    lax.fori_loop(0, full // 16, step, 0, unroll=5)
    if full < rows:
        spare = jnp.zeros((rows - held, low.shape[1]), F32)
        ends = [
            jnp.concatenate([h[full:, :].astype(F32), spare], axis=0).astype(BF16) for h in (low, high)
        ]
        rim(pl.ds(full, 16), *ends)
    for m in range(bins_axis):
        ordered = dot_nt(columns(moved, me ^ m), rim_order[m]) + inner[m].astype(F32)
        ordered = ordered[:rows_out]
        ordered = jnp.where((me & 1) == 1, pltpu.roll(ordered, 4, 0), ordered).astype(BF16)
        for c in range(CHUNKS):
            chunks[c * bins_axis + m][...] = ordered[:, c * half : (c + 1) * half]


def transpose_kernel(coupling, out):
    bins = coupling.shape[0]
    for start in range(0, bins, 256):
        size = min(256, bins - start)
        eye = (iota((size, size), 0) == iota((size, size), 1)).astype(F32).astype(BF16)
        out[start : start + size, :] = dot_nt(eye, coupling[:, start : start + size]).astype(BF16)


def couple_kernel(chunk, bins_axis, local_bins, slots, paired, *refs):
    blocks = refs[:bins_axis]
    weights, meta = refs[bins_axis : bins_axis + 2]
    values = refs[-1]
    owners_count = 2 * len(paired)
    outs = list(refs[-1 - sum(1 if pair else 2 for pair in paired) : -1])
    rows, width = blocks[0].shape
    all_bins = values.shape[0]
    half_bins = all_bins // 2
    me = lax.axis_index("bins")
    values[...] = jnp.zeros_like(values)
    for m in range(bins_axis):
        block = me ^ m
        at = pl.ds(pl.multiple_of(block * local_bins - 4 * (block & 1), 8), rows)
        values[at, :] += blocks[m][...].astype(F32)
    flat = values[...].astype(BF16)
    energy = jnp.sum(values[...], axis=0, keepdims=True) / all_bins
    facts = meta[:, chunk * width : (chunk + 1) * width]
    scale = facts[3:4, :] / (1.0 + energy)
    slot, towards, rank = facts[0:1, :].astype(I32), facts[1:2, :].astype(I32), facts[2:3, :]
    slot_id = iota((owners_count * slots, width), 0)
    straight = (slot_id == towards * slots + slot).astype(F32).astype(BF16)
    crossed = (slot_id == (towards ^ 1) * slots + slot).astype(F32).astype(BF16)
    step = all_bins // 3
    for start in range(0, all_bins, step):
        at = slice(start, start + step)
        coupled = jnp.dot(weights[at, :], flat, preferred_element_type=F32)
        values[at, :] = (values[at, :] + coupled) * scale
    spare = jnp.zeros((7, width), F32)
    sent = []
    for group in range(2):
        updated = values[group * half_bins : (group + 1) * half_bins, :]
        updated = jnp.concatenate([updated, rank, spare], axis=0).astype(BF16)
        sent.append(dot_nt(updated, straight if group == chunk else crossed).astype(BF16))
    even, odd = sent[chunk], sent[1 - chunk]
    is_low = iota((half_bins + 8, LANES), 1) < slots
    for t in range(owners_count // 2):
        at = slice(t * LANES, (t + 1) * LANES)
        first = jnp.where(is_low, even[:, at], odd[:, at])
        second = jnp.where(is_low, odd[:, at], even[:, at])
        if paired[t]:
            out = outs.pop(0)
            out[0], out[1] = first, second
        else:
            outs.pop(0)[...] = first
            outs.pop(0)[...] = second


def place_kernel(slots, sources, picks, *refs):
    out, staged, sems = refs[-3:]
    me = lax.axis_index("pts")
    tall = refs[0].shape[-2]
    half_bins = tall - 8
    is_low = iota((tall, LANES), 1) < slots
    slot_id = iota((LANES, LANES), 0)

    def block(pick):
        ref, index = refs[pick[0]], pick[1]
        return ref[...] if index is None else ref[index]

    copies = []
    for number, x in enumerate(sources):
        first, second = [block(picks[number][c]) for c in range(CHUNKS)]
        if x % 2 == 1:
            first, second = second, first
        pieces = []
        for lhs in (jnp.where(is_low, first, second), jnp.where(is_low, second, first)):
            rank = lhs[tall - 16 :, :].astype(F32)[8:9, :].astype(I32)
            place = (slot_id == rank).astype(F32).astype(BF16)
            pieces.append(dot_nt(lhs, place)[:half_bins])
        staged[number] = jnp.concatenate(pieces, axis=0).astype(BF16)
        at = pl.ds(pl.multiple_of((me ^ x) * LANES, LANES), LANES)
        copy = pltpu.make_async_copy(staged.at[number], out.at[:, at], sems.at[number])
        copy.start()
        copies.append(copy)
    for copy in copies:
        copy.wait()


def place(out, slots, owners_count, all_bins, sources):
    arrays, picks = [], []
    for x in sorted(sources):
        mine = []
        for array, index in sources[x]:
            known = [n for n, a in enumerate(arrays) if a is array]
            if not known:
                arrays.append(array)
                known = [len(arrays) - 1]
            mine.append((known[0], index))
        picks.append(tuple(mine))
    held = [] if out is None else [out]
    return pl.pallas_call(
        functools.partial(place_kernel, slots, tuple(sorted(sources)), tuple(picks)),
        out_shape=jax.ShapeDtypeStruct((all_bins, owners_count * LANES), BF16),
        in_specs=vmem(len(arrays)) + [pl.BlockSpec(memory_space=pl.ANY)] * len(held),
        out_specs=pl.BlockSpec(memory_space=pl.ANY),
        scratch_shapes=[
            pltpu.VMEM((len(sources), all_bins, LANES), BF16),
            pltpu.SemaphoreType.DMA((len(sources),)),
        ],
        input_output_aliases={len(arrays): 0} if held else {},
        compiler_params=params(16),
        cost_estimate=cost(1, 1),
        name="place",
    )(*arrays, *held)


def gate_kernel(array, *refs):
    refs[-1][...] = array[...]


def gate(array, *after):
    return pl.pallas_call(
        gate_kernel,
        out_shape=jax.ShapeDtypeStruct(array.shape, array.dtype),
        in_specs=vmem(1 + len(after)),
        out_specs=vmem(1)[0],
        compiler_params=params(16),
        cost_estimate=cost(1, 1),
        name="gate",
    )(array, *after)


def stack_kernel(count, *refs):
    for t in range(count):
        refs[-1][t] = refs[t][1]


def stack(pairs, after):
    return pl.pallas_call(
        functools.partial(stack_kernel, len(pairs)),
        out_shape=jax.ShapeDtypeStruct((len(pairs),) + pairs[0].shape[1:], pairs[0].dtype),
        in_specs=vmem(len(pairs) + 1),
        out_specs=vmem(1)[0],
        compiler_params=params(8),
        cost_estimate=cost(1, 1),
        name="stack",
    )(*pairs, after)


def params(mib):
    return pltpu.CompilerParams(vmem_limit_bytes=mib << 20)


def vmem(count):
    return [pl.BlockSpec(memory_space=pltpu.VMEM)] * count


def cost(flops, bytes_accessed):
    del bytes_accessed
    return pl.CostEstimate(flops=int(flops), bytes_accessed=1, transcendentals=0)


def exchange(array, axis, offset):
    return lax.ppermute(array, axis, [(i, i ^ offset) for i in range(lax.axis_size(axis))])


def chunked(spectrum, courant, upwind, coupling, sea, owner):
    local_bins, lon_rows, lats = spectrum.shape
    all_bins = courant.shape[0]
    bins_axis = lax.axis_size("bins")
    owners_count = lax.axis_size("pts")
    points = lon_rows * LANES
    half = points // CHUNKS
    slots = 2 * points // owners_count // CHUNKS
    tall = round_up(local_bins, 16)
    rows = round_up(local_bins + 1, 8)
    half_rows = all_bins // 2 + 8
    first_bin = lax.axis_index("bins") * local_bins

    planes = jnp.pad(jnp.transpose(spectrum, (1, 0, 2)), ((0, 0), (0, tall - local_bins), (0, 0)))
    edges = [planes[r, :local_bins] * sea[r].astype(BF16)[None] for r in (0, lon_rows - 1)]
    up = [(i, i + 1) for i in range(owners_count - 1)]
    down = [(i + 1, i) for i in range(owners_count - 1)]
    low = lax.ppermute(edges[1], "pts", up)
    high = lax.ppermute(edges[0], "pts", down)
    own = owner.reshape(1, points)
    owners = [own] + [exchange(own, "bins", m) for m in range(1, bins_axis)]
    def wide(table, dtype):
        mine = lax.dynamic_slice_in_dim(table.T, first_bin, local_bins, 1).astype(dtype)
        mine = jnp.pad(mine, ((0, 0), (0, tall - local_bins)))
        return jnp.broadcast_to(mine[:, :, None], (2, tall, LANES))

    speed, side = wide(courant, F32), wide(upwind, BF16)

    weights = pl.pallas_call(
        transpose_kernel,
        out_shape=jax.ShapeDtypeStruct(coupling.shape, BF16),
        in_specs=vmem(1),
        out_specs=vmem(1)[0],
        compiler_params=params(16),
        cost_estimate=cost(1, 1),
        name="transpose",
    )(coupling)

    inner, rim_order, meta = pl.pallas_call(
        functools.partial(inner_kernel, bins_axis, owners_count, half),
        out_shape=[
            jax.ShapeDtypeStruct((bins_axis, tall, points), BF16),
            jax.ShapeDtypeStruct((bins_axis, points, 2 * LANES), BF16),
            jax.ShapeDtypeStruct((8, points), F32),
        ],
        in_specs=vmem(4 + bins_axis),
        out_specs=vmem(3),
        scratch_shapes=[pltpu.VMEM((lon_rows - 2, tall, lats), BF16)],
        compiler_params=params(16),
        cost_estimate=cost(1, 1),
        name="inner",
    )(planes, speed, side, sea, *owners)
    packed = pl.pallas_call(
        functools.partial(pack_kernel, rows, bins_axis, half),
        out_shape=[jax.ShapeDtypeStruct((rows, half), BF16)] * (CHUNKS * bins_axis),
        in_specs=vmem(8),
        out_specs=vmem(CHUNKS * bins_axis),
        scratch_shapes=[pltpu.VMEM((2, tall, lats), BF16)],
        compiler_params=params(16),
        cost_estimate=cost(1, 1),
        name="pack",
    )(planes, low, high, speed, side, sea, inner, rim_order)

    def couple(c, blocks, ready, paired):
        shapes = [[(2, half_rows, LANES)] if pair else [(half_rows, LANES)] * 2 for pair in paired]
        shapes = sum(shapes, [])
        return list(pl.pallas_call(
            functools.partial(couple_kernel, c, bins_axis, local_bins, slots, paired),
            out_shape=[jax.ShapeDtypeStruct(shape, BF16) for shape in shapes],
            in_specs=vmem(len(blocks) + 2 + len(ready)),
            out_specs=vmem(len(shapes)),
            scratch_shapes=[pltpu.VMEM((all_bins, half), F32)],
            compiler_params=params(16),
            cost_estimate=cost(1 + c * 3e10, 1),
            name="couple",
        )(*blocks, weights, meta, *ready))

    pairs = owners_count // 2
    early, late = packed[:bins_axis], packed[bins_axis : 2 * bins_axis]
    first = [exchange(early[m], "bins", m) for m in range(1, bins_axis)]
    late = [late[0], gate(late[1], first[0], weights)] + [gate(b, *first) for b in late[2:]]
    second = [exchange(late[m], "bins", m) for m in range(1, bins_axis)]
    pays = couple(0, [early[0], *first], late[1:], (True,) * pairs)
    came = {0: pays[0]}
    for t in range(pairs - 1, 0, -1):
        came[t] = exchange(pays[t], "pts", 2 * t)
    pays = couple(1, [late[0], *second], [], (True,) * pairs)
    last = {0: pays[0]}
    for t in range(pairs - 1, 0, -1):
        last[t] = exchange(pays[t], "pts", 2 * t)
    swapped = exchange(stack([came[t] for t in range(pairs)], last[pairs - 1]), "pts", 1)
    swapped_late = exchange(stack([last[t] for t in range(pairs)], last[0]), "pts", 1)

    shape = (slots, owners_count, all_bins)
    placed = place(None, *shape, {2 * t: [(came[t], 0), (last[t], 0)] for t in range(pairs)})
    placed = place(
        placed, *shape, {2 * t + 1: [(swapped, t), (swapped_late, t)] for t in range(pairs)}
    )
    return jnp.transpose(placed).reshape(1, 1, owners_count * LANES, all_bins)


def padded_2(block, sides, width):
    for axis, dim in sides:
        count = lax.axis_size(axis)
        forward = [(i, i + 1) for i in range(count - 1)]
        backward = [(target, source) for source, target in forward]
        low = lax.ppermute(
            lax.slice_in_dim(block, block.shape[dim] - width, None, axis=dim), axis, forward
        )
        high = lax.ppermute(lax.slice_in_dim(block, 0, width, axis=dim), axis, backward)
        block = jnp.concatenate([low, block, high], axis=dim)
    return block


def advect(padded, sea_mask, courant, upwind):
    center = padded[:, 1:-1, 1:-1]
    donor_x = jnp.where(upwind[:, 0][:, None, None] == 0, padded[:, :-2, 1:-1], padded[:, 2:, 1:-1])
    donor_y = jnp.where(upwind[:, 1][:, None, None] == 0, padded[:, 1:-1, :-2], padded[:, 1:-1, 2:])
    moved = (
        center
        - courant[:, 0][:, None, None] * (center - donor_x)
        - courant[:, 1][:, None, None] * (center - donor_y)
    )
    return (moved * sea_mask[None]).astype(jnp.bfloat16)


def whole(spectrum, courant, upwind, coupling, sea, owner):
    local_bins = spectrum.shape[0]
    lon_rows = spectrum.shape[1]
    bins_count = lax.axis_size("bins")
    lat_cells = spectrum.shape[2] // bins_count
    masked = spectrum * sea.astype(jnp.bfloat16)[None]
    local_sea = lax.dynamic_slice_in_dim(
        sea, lax.axis_index("bins") * lat_cells, lat_cells, 1
    ).astype(jnp.float32)
    first_bin = lax.axis_index("bins") * local_bins
    my_courant = lax.dynamic_slice_in_dim(courant, first_bin, local_bins, 0)
    my_upwind = lax.dynamic_slice_in_dim(upwind, first_bin, local_bins, 0)
    extended = padded_2(masked, (("pts", 1),), 1)
    extended = jnp.pad(extended.astype(jnp.float32), ((0, 0), (0, 0), (1, 1)))
    moved = advect(extended, sea.astype(jnp.float32), my_courant, my_upwind)
    columns = lax.all_to_all(moved, "bins", split_axis=2, concat_axis=0, tiled=True)
    all_bins = columns.shape[0]
    points = lon_rows * lat_cells
    flat = columns.reshape(all_bins, points)
    energy = jnp.mean(flat.astype(jnp.float32), axis=0)
    coupled = jnp.einsum("bp,bc->pc", flat, coupling, preferred_element_type=jnp.float32)
    weights = local_sea.reshape(points)
    updated = (
        weights[:, None] * (flat.astype(jnp.float32).T + coupled) / (1.0 + energy)[:, None]
    ).astype(jnp.bfloat16)
    owners_count = lax.axis_size("pts")
    capacity = max(2, (2 * points + owners_count - 1) // owners_count)
    target = owner.reshape(points)
    onehot = (target[:, None] == jnp.arange(owners_count, dtype=jnp.int32)[None, :]).astype(
        jnp.int32
    )
    slot_rank = jnp.sum(jnp.cumsum(onehot, axis=0) * onehot, axis=1) - 1
    slot_index = target * capacity + slot_rank
    selector = (
        slot_index[None, :] == jnp.arange(owners_count * capacity, dtype=jnp.int32)[:, None]
    ).astype(jnp.bfloat16)
    outgoing = jnp.dot(selector, updated, preferred_element_type=jnp.float32).astype(jnp.bfloat16)
    outgoing = outgoing.reshape(owners_count, capacity, all_bins)
    received = lax.all_to_all(outgoing, "pts", split_axis=0, concat_axis=0, tiled=True)
    return received.reshape(1, 1, owners_count * capacity, all_bins)


def local(spectrum, courant, upwind, coupling, sea, owner):
    bins_axis, owners_count = lax.axis_size("bins"), lax.axis_size("pts")
    points = owner.shape[2]
    suits = (
        spectrum.shape[2] == bins_axis * LANES
        and points % (2 * LANES) == 0
        and 2 * points == owners_count * LANES
        and bins_axis & (bins_axis - 1) == 0
        and owners_count & (owners_count - 1) == 0
        and bins_axis % 2 == 0
        and spectrum.shape[0] % 8 == 4
        and courant.shape[0] % 48 == 0
        and owners_count == 8
        and spectrum.shape[1] >= 3
    )
    form = chunked if suits else whole
    return form(spectrum, courant, upwind, coupling, sea, owner)


def solution(mesh):
    placed = (P("bins", "pts", None), P(), P(), P(), P("pts", None), P("pts", "bins", None, None))
    return jax.shard_map(
        local, mesh=mesh, in_specs=placed, out_specs=P("pts", "bins", None, None), check_vma=False
    )
```

```python
import functools

import jax
import jax.numpy as jnp
from jax import lax
from jax.experimental import pallas as pl
from jax.experimental.pallas import tpu as pltpu
from jax.sharding import PartitionSpec as P

F32 = jnp.float32
BF16 = jnp.bfloat16
I32 = jnp.int32
LANES = 128
CHUNKS = 2
NT = (((1,), (1,)), ((), ()))


def round_up(size, unit):
    return -(-size // unit) * unit


def iota(shape, axis):
    return lax.broadcasted_iota(I32, shape, axis)


def dot_nt(lhs, rhs):
    return lax.dot_general(lhs, rhs, NT, preferred_element_type=F32)


def upwind_row(at, speed, side, before, center, after, sea_row):
    lats = center.shape[1]
    lane = iota(center.shape, 1)
    wide = lats // LANES
    cx, cy = [jnp.concatenate([speed[k, at, :]] * wide, axis=1) for k in range(2)]
    ux, uy = [jnp.concatenate([side[k, at, :]] * wide, axis=1) for k in range(2)]
    donor_x = jnp.where(ux == 0, before, after).astype(F32)
    left = jnp.where(lane == 0, 0, pltpu.roll(center, 1, 1))
    right = jnp.where(lane == lats - 1, 0, pltpu.roll(center, lats - 1, 1))
    donor_y = jnp.where(uy == 0, left, right).astype(F32)
    center = center.astype(F32)
    value = center - cx * (center - donor_x) - cy * (center - donor_y)
    return (value * sea_row).astype(BF16)


def inner_kernel(planes, near, speed, side, sea, moved):
    lon_rows, rows, _ = planes.shape
    top = lon_rows - 1
    even = lax.axis_index("pts") % 2 == 0
    sea_f = sea[...].astype(F32)
    sea_b = sea_f.astype(BF16)

    def tile(at, close):
        masked = [planes[l, at, :] * sea_b[l : l + 1, :] for l in range(lon_rows)]
        for l in range(1, top):
            moved[l - 1, at, :] = upwind_row(
                at, speed, side, masked[l - 1], masked[l], masked[l + 1], sea_f[l : l + 1, :]
            )
        center = jnp.where(even, masked[top], masked[0])
        below = jnp.where(even, masked[top - 1], close)
        above = jnp.where(even, close, masked[1])
        weight = jnp.where(even, sea_f[top : top + 1, :], sea_f[0:1, :])
        moved[top - 1, at, :] = upwind_row(at, speed, side, below, center, above, weight)

    over_rows(tile, rows, near)


def over_rows(tile, rows, halo):
    held = halo.shape[0]
    full = held // 16 * 16

    def step(index, carry):
        at = pl.ds(pl.multiple_of(index * 16, 16), 16)
        tile(at, halo[at, :])
        return carry

    lax.fori_loop(0, full // 16, step, 0, unroll=5)
    if full < rows:
        spare = jnp.zeros((rows - held, halo.shape[1]), F32)
        end = jnp.concatenate([halo[full:, :].astype(F32), spare], axis=0).astype(BF16)
        tile(pl.ds(full, 16), end)


def order_kernel(bins_axis, owners_count, half, *refs):
    inner, sea = refs[:2]
    owner = refs[2 : 2 + bins_axis]
    part, far_order, meta, order = refs[2 + bins_axis :]
    lon_rows = inner.shape[0] + 1
    points = lon_rows * LANES
    me = lax.axis_index("bins")
    me_pts = lax.axis_index("pts")
    even = me_pts % 2 == 0
    last = (lon_rows - 1) * LANES
    near_at = pl.ds(pl.multiple_of(jnp.where(even, last, 0), LANES), LANES)
    far_at = pl.ds(pl.multiple_of(jnp.where(even, 0, last), LANES), LANES)
    owners_id = iota((owners_count, points), 0)
    hot = [(owner[m][...] == owners_id).astype(F32) for m in range(bins_axis)]
    earlier = (iota((points, points), 0) < iota((points, points), 1)).astype(F32).astype(BF16)
    before = jnp.dot(
        jnp.concatenate(hot, axis=0).astype(BF16), earlier, preferred_element_type=F32
    )
    place_id = iota((points, points), 0)
    for m in range(bins_axis):
        own = owner[m][...]
        count = jnp.sum(hot[m], axis=1, keepdims=True)
        offset = jnp.sum(jnp.where(owners_id < own, count, 0.0), axis=0, keepdims=True)
        mine = before[m * owners_count : (m + 1) * owners_count, :]
        rank = jnp.sum(hot[m] * mine, axis=0, keepdims=True)
        key = (offset + rank).astype(I32)
        place = (key & 1) * half + (key >> 1)
        order[...] = (place_id == place).astype(F32).astype(BF16)
        far_order[m] = order[:, far_at]
        at = pl.ds(pl.multiple_of((me ^ m) * LANES, LANES), LANES)
        cells = jnp.concatenate([inner[l, :, at] for l in range(lon_rows - 1)], axis=1)
        columns = jnp.concatenate([order[:, LANES:last], order[:, near_at]], axis=1)
        part[m] = dot_nt(cells, columns).astype(BF16)
        if m == 0:
            first = offset.astype(I32)
            slot = (key - first - (((key & 1) - first) & 1)) >> 1
            weight = jnp.concatenate([sea[l : l + 1, at].astype(F32) for l in range(lon_rows)], axis=1)
            facts = jnp.concatenate(
                [slot.astype(F32), (own ^ me_pts).astype(F32), rank, weight]
                + [jnp.zeros((1, points), F32)] * 4,
                axis=0,
            )
            meta[...] = dot_nt(facts.astype(BF16), order[...])


def pack_kernel(rows_out, bins_axis, half, *refs):
    planes, far, speed, side, sea, part, far_order = refs[:7]
    chunks, moved = refs[7:-1], refs[-1]
    lon_rows, rows, _ = planes.shape
    top = lon_rows - 1
    me = lax.axis_index("bins")
    even = lax.axis_index("pts") % 2 == 0
    center_row, next_row = jnp.where(even, 0, top), jnp.where(even, 1, top - 1)
    sea_f = sea[...].astype(F32)
    center_sea = jnp.where(even, sea_f[0:1, :], sea_f[top : top + 1, :])
    next_sea = jnp.where(even, sea_f[1:2, :], sea_f[top - 1 : top, :]).astype(BF16)

    def tile(at, distant):
        center = planes[center_row, at, :] * center_sea.astype(BF16)
        beside = planes[next_row, at, :] * next_sea
        below, above = jnp.where(even, distant, beside), jnp.where(even, beside, distant)
        moved[at, :] = upwind_row(at, speed, side, below, center, above, center_sea)

    over_rows(tile, rows, far)
    for m in range(bins_axis):
        at = pl.ds(pl.multiple_of((me ^ m) * LANES, LANES), LANES)
        ordered = dot_nt(moved[:, at], far_order[m]) + part[m].astype(F32)
        ordered = ordered[:rows_out]
        ordered = jnp.where((me & 1) == 1, pltpu.roll(ordered, 4, 0), ordered).astype(BF16)
        for c in range(CHUNKS):
            chunks[c * bins_axis + m][...] = ordered[:, c * half : (c + 1) * half]


def transpose_kernel(coupling, out):
    bins = coupling.shape[0]
    for start in range(0, bins, 256):
        size = min(256, bins - start)
        eye = (iota((size, size), 0) == iota((size, size), 1)).astype(F32).astype(BF16)
        out[start : start + size, :] = dot_nt(eye, coupling[:, start : start + size]).astype(BF16)


def couple_kernel(chunk, bins_axis, local_bins, slots, paired, *refs):
    blocks = refs[:bins_axis]
    weights, meta = refs[bins_axis : bins_axis + 2]
    values = refs[-1]
    owners_count = 2 * len(paired)
    outs = list(refs[-1 - sum(1 if pair else 2 for pair in paired) : -1])
    rows, width = blocks[0].shape
    all_bins = values.shape[0]
    half_bins = all_bins // 2
    me = lax.axis_index("bins")
    values[...] = jnp.zeros_like(values)
    for m in range(bins_axis):
        block = me ^ m
        at = pl.ds(pl.multiple_of(block * local_bins - 4 * (block & 1), 8), rows)
        values[at, :] += blocks[m][...].astype(F32)
    flat = values[...].astype(BF16)
    energy = jnp.sum(values[...], axis=0, keepdims=True) / all_bins
    facts = meta[:, chunk * width : (chunk + 1) * width]
    scale = facts[3:4, :] / (1.0 + energy)
    slot, towards, rank = facts[0:1, :].astype(I32), facts[1:2, :].astype(I32), facts[2:3, :]
    slot_id = iota((owners_count * slots, width), 0)
    straight = (slot_id == towards * slots + slot).astype(F32).astype(BF16)
    crossed = (slot_id == (towards ^ 1) * slots + slot).astype(F32).astype(BF16)
    step = all_bins // 9
    for start in range(0, all_bins, step):
        at = slice(start, start + step)
        coupled = jnp.dot(weights[at, :], flat, preferred_element_type=F32)
        values[at, :] = (values[at, :] + coupled) * scale
    spare = jnp.zeros((7, width), F32)
    sent = []
    for group in range(2):
        updated = values[group * half_bins : (group + 1) * half_bins, :]
        updated = jnp.concatenate([updated, rank, spare], axis=0).astype(BF16)
        sent.append(dot_nt(updated, straight if group == chunk else crossed).astype(BF16))
    even, odd = sent[chunk], sent[1 - chunk]
    is_low = iota((half_bins + 8, LANES), 1) < slots
    for t in range(owners_count // 2):
        at = slice(t * LANES, (t + 1) * LANES)
        first = jnp.where(is_low, even[:, at], odd[:, at])
        second = jnp.where(is_low, odd[:, at], even[:, at])
        if paired[t]:
            out = outs.pop(0)
            out[0], out[1] = first, second
        else:
            outs.pop(0)[...] = first
            outs.pop(0)[...] = second


def place_kernel(slots, sources, picks, *refs):
    out, staged, sems = refs[-3:]
    me = lax.axis_index("pts")
    tall = refs[0].shape[-2]
    half_bins = tall - 8
    is_low = iota((tall, LANES), 1) < slots
    slot_id = iota((LANES, LANES), 0)

    def block(pick):
        ref, index = refs[pick[0]], pick[1]
        return ref[...] if index is None else ref[index]

    copies = []
    for number, x in enumerate(sources):
        first, second = [block(picks[number][c]) for c in range(CHUNKS)]
        if x % 2 == 1:
            first, second = second, first
        pieces = []
        for lhs in (jnp.where(is_low, first, second), jnp.where(is_low, second, first)):
            rank = lhs[tall - 16 :, :].astype(F32)[8:9, :].astype(I32)
            place = (slot_id == rank).astype(F32).astype(BF16)
            pieces.append(dot_nt(lhs, place)[:half_bins])
        staged[number] = jnp.concatenate(pieces, axis=0).astype(BF16)
        at = pl.ds(pl.multiple_of((me ^ x) * LANES, LANES), LANES)
        copy = pltpu.make_async_copy(staged.at[number], out.at[:, at], sems.at[number])
        copy.start()
        copies.append(copy)
    for copy in copies:
        copy.wait()


def place(out, slots, owners_count, all_bins, sources):
    arrays, picks = [], []
    for x in sorted(sources):
        mine = []
        for array, index in sources[x]:
            known = [n for n, a in enumerate(arrays) if a is array]
            if not known:
                arrays.append(array)
                known = [len(arrays) - 1]
            mine.append((known[0], index))
        picks.append(tuple(mine))
    held = [] if out is None else [out]
    return pl.pallas_call(
        functools.partial(place_kernel, slots, tuple(sorted(sources)), tuple(picks)),
        out_shape=jax.ShapeDtypeStruct((all_bins, owners_count * LANES), BF16),
        in_specs=vmem(len(arrays)) + [pl.BlockSpec(memory_space=pl.ANY)] * len(held),
        out_specs=pl.BlockSpec(memory_space=pl.ANY),
        scratch_shapes=[
            pltpu.VMEM((len(sources), all_bins, LANES), BF16),
            pltpu.SemaphoreType.DMA((len(sources),)),
        ],
        input_output_aliases={len(arrays): 0} if held else {},
        compiler_params=params(16),
        cost_estimate=cost(1, 1),
        name="place",
    )(*arrays, *held)


def gate_kernel(array, *refs):
    refs[-1][...] = array[...]


def gate(array, *after):
    return pl.pallas_call(
        gate_kernel,
        out_shape=jax.ShapeDtypeStruct(array.shape, array.dtype),
        in_specs=vmem(1 + len(after)),
        out_specs=vmem(1)[0],
        compiler_params=params(16),
        cost_estimate=cost(1, 1),
        name="gate",
    )(array, *after)


def stack_kernel(count, *refs):
    for t in range(count):
        refs[-1][t] = refs[t][1]


def stack(pairs, after):
    return pl.pallas_call(
        functools.partial(stack_kernel, len(pairs)),
        out_shape=jax.ShapeDtypeStruct((len(pairs),) + pairs[0].shape[1:], pairs[0].dtype),
        in_specs=vmem(len(pairs) + 1),
        out_specs=vmem(1)[0],
        compiler_params=params(8),
        cost_estimate=cost(1, 1),
        name="stack",
    )(*pairs, after)


def params(mib):
    return pltpu.CompilerParams(vmem_limit_bytes=mib << 20)


def vmem(count):
    return [pl.BlockSpec(memory_space=pltpu.VMEM)] * count


def cost(flops, bytes_accessed):
    del bytes_accessed
    return pl.CostEstimate(flops=int(flops), bytes_accessed=1, transcendentals=0)


def exchange(array, axis, offset):
    return lax.ppermute(array, axis, [(i, i ^ offset) for i in range(lax.axis_size(axis))])


def chunked(spectrum, courant, upwind, coupling, sea, owner):
    local_bins, lon_rows, lats = spectrum.shape
    all_bins = courant.shape[0]
    bins_axis = lax.axis_size("bins")
    owners_count = lax.axis_size("pts")
    points = lon_rows * LANES
    half = points // CHUNKS
    slots = 2 * points // owners_count // CHUNKS
    tall = round_up(local_bins, 16)
    rows = round_up(local_bins + 1, 8)
    half_rows = all_bins // 2 + 8
    first_bin = lax.axis_index("bins") * local_bins

    planes = jnp.pad(jnp.transpose(spectrum, (1, 0, 2)), ((0, 0), (0, tall - local_bins), (0, 0)))
    even = lax.axis_index("pts") % 2 == 0
    rows_at = [jnp.where(even, 0, lon_rows - 1), jnp.where(even, lon_rows - 1, 0)]
    edges = [
        lax.dynamic_index_in_dim(planes, r, 0, False)[:local_bins]
        * lax.dynamic_index_in_dim(sea, r, 0, False).astype(BF16)[None]
        for r in rows_at
    ]
    between = [(i, i + 1) for i in range(1, owners_count - 1, 2)]
    far = lax.ppermute(edges[0], "pts", between + [(b, a) for a, b in between])
    near = exchange(edges[1], "pts", 1)
    own = owner.reshape(1, points)
    owners = [own, *reversed([exchange(own, "bins", m) for m in range(bins_axis - 1, 0, -1)])]

    def wide(table, dtype):
        mine = lax.dynamic_slice_in_dim(table.T, first_bin, local_bins, 1).astype(dtype)
        mine = jnp.pad(mine, ((0, 0), (0, tall - local_bins)))
        return jnp.broadcast_to(mine[:, :, None], (2, tall, LANES))

    speed, side = wide(courant, F32), wide(upwind, BF16)

    weights = pl.pallas_call(
        transpose_kernel,
        out_shape=jax.ShapeDtypeStruct(coupling.shape, BF16),
        in_specs=vmem(1),
        out_specs=vmem(1)[0],
        compiler_params=params(16),
        cost_estimate=cost(1, 1),
        name="transpose",
    )(coupling)

    inner = pl.pallas_call(
        inner_kernel,
        out_shape=jax.ShapeDtypeStruct((lon_rows - 1, tall, lats), BF16),
        in_specs=vmem(5),
        out_specs=vmem(1)[0],
        compiler_params=params(16),
        cost_estimate=cost(1, 1),
        name="inner",
    )(planes, near, speed, side, sea)
    part, far_order, meta = pl.pallas_call(
        functools.partial(order_kernel, bins_axis, owners_count, half),
        out_shape=[
            jax.ShapeDtypeStruct((bins_axis, tall, points), BF16),
            jax.ShapeDtypeStruct((bins_axis, points, LANES), BF16),
            jax.ShapeDtypeStruct((8, points), F32),
        ],
        in_specs=vmem(2 + bins_axis),
        out_specs=vmem(3),
        scratch_shapes=[pltpu.VMEM((points, points), BF16)],
        compiler_params=params(16),
        cost_estimate=cost(1, 1),
        name="order",
    )(inner, sea, *owners)
    packed = pl.pallas_call(
        functools.partial(pack_kernel, rows, bins_axis, half),
        out_shape=[jax.ShapeDtypeStruct((rows, half), BF16)] * (CHUNKS * bins_axis),
        in_specs=vmem(7),
        out_specs=vmem(CHUNKS * bins_axis),
        scratch_shapes=[pltpu.VMEM((tall, lats), BF16)],
        compiler_params=params(16),
        cost_estimate=cost(1, 1),
        name="pack",
    )(planes, far, speed, side, sea, part, far_order)

    def couple(c, blocks, ready, paired):
        shapes = [[(2, half_rows, LANES)] if pair else [(half_rows, LANES)] * 2 for pair in paired]
        shapes = sum(shapes, [])
        return list(pl.pallas_call(
            functools.partial(couple_kernel, c, bins_axis, local_bins, slots, paired),
            out_shape=[jax.ShapeDtypeStruct(shape, BF16) for shape in shapes],
            in_specs=vmem(len(blocks) + 2 + len(ready)),
            out_specs=vmem(len(shapes)),
            scratch_shapes=[pltpu.VMEM((all_bins, half), F32)],
            compiler_params=params(16),
            cost_estimate=cost(1 + c * 3e10, 1),
            name="couple",
        )(*blocks, weights, meta, *ready))

    pairs = owners_count // 2
    early, late = packed[:bins_axis], packed[bins_axis : 2 * bins_axis]
    first = [exchange(early[m], "bins", m) for m in range(1, bins_axis)]
    late = [late[0], gate(late[1], first[0], weights)] + [gate(b, *first) for b in late[2:]]
    second = [exchange(late[m], "bins", m) for m in range(1, bins_axis)]
    pays = couple(0, [early[0], *first], late[1:], (True,) * pairs)
    came = {0: pays[0]}
    for t in range(pairs - 1, 0, -1):
        came[t] = exchange(pays[t], "pts", 2 * t)
    pays = couple(1, [late[0], *second], [], (True,) * pairs)
    last = {0: pays[0]}
    for t in range(pairs - 1, 0, -1):
        last[t] = exchange(pays[t], "pts", 2 * t)
    swapped = exchange(stack([came[t] for t in range(pairs)], last[pairs - 1]), "pts", 1)
    swapped_late = exchange(stack([last[t] for t in range(pairs)], last[0]), "pts", 1)

    shape = (slots, owners_count, all_bins)
    placed = place(None, *shape, {2 * t: [(came[t], 0), (last[t], 0)] for t in range(pairs)})
    placed = place(
        placed, *shape, {2 * t + 1: [(swapped, t), (swapped_late, t)] for t in range(pairs)}
    )
    return jnp.transpose(placed).reshape(1, 1, owners_count * LANES, all_bins)


def padded_2(block, sides, width):
    for axis, dim in sides:
        count = lax.axis_size(axis)
        forward = [(i, i + 1) for i in range(count - 1)]
        backward = [(target, source) for source, target in forward]
        low = lax.ppermute(
            lax.slice_in_dim(block, block.shape[dim] - width, None, axis=dim), axis, forward
        )
        high = lax.ppermute(lax.slice_in_dim(block, 0, width, axis=dim), axis, backward)
        block = jnp.concatenate([low, block, high], axis=dim)
    return block


def advect(padded, sea_mask, courant, upwind):
    center = padded[:, 1:-1, 1:-1]
    donor_x = jnp.where(upwind[:, 0][:, None, None] == 0, padded[:, :-2, 1:-1], padded[:, 2:, 1:-1])
    donor_y = jnp.where(upwind[:, 1][:, None, None] == 0, padded[:, 1:-1, :-2], padded[:, 1:-1, 2:])
    moved = (
        center
        - courant[:, 0][:, None, None] * (center - donor_x)
        - courant[:, 1][:, None, None] * (center - donor_y)
    )
    return (moved * sea_mask[None]).astype(jnp.bfloat16)


def whole(spectrum, courant, upwind, coupling, sea, owner):
    local_bins = spectrum.shape[0]
    lon_rows = spectrum.shape[1]
    bins_count = lax.axis_size("bins")
    lat_cells = spectrum.shape[2] // bins_count
    masked = spectrum * sea.astype(jnp.bfloat16)[None]
    local_sea = lax.dynamic_slice_in_dim(
        sea, lax.axis_index("bins") * lat_cells, lat_cells, 1
    ).astype(jnp.float32)
    first_bin = lax.axis_index("bins") * local_bins
    my_courant = lax.dynamic_slice_in_dim(courant, first_bin, local_bins, 0)
    my_upwind = lax.dynamic_slice_in_dim(upwind, first_bin, local_bins, 0)
    extended = padded_2(masked, (("pts", 1),), 1)
    extended = jnp.pad(extended.astype(jnp.float32), ((0, 0), (0, 0), (1, 1)))
    moved = advect(extended, sea.astype(jnp.float32), my_courant, my_upwind)
    columns = lax.all_to_all(moved, "bins", split_axis=2, concat_axis=0, tiled=True)
    all_bins = columns.shape[0]
    points = lon_rows * lat_cells
    flat = columns.reshape(all_bins, points)
    energy = jnp.mean(flat.astype(jnp.float32), axis=0)
    coupled = jnp.einsum("bp,bc->pc", flat, coupling, preferred_element_type=jnp.float32)
    weights = local_sea.reshape(points)
    updated = (
        weights[:, None] * (flat.astype(jnp.float32).T + coupled) / (1.0 + energy)[:, None]
    ).astype(jnp.bfloat16)
    owners_count = lax.axis_size("pts")
    capacity = max(2, (2 * points + owners_count - 1) // owners_count)
    target = owner.reshape(points)
    onehot = (target[:, None] == jnp.arange(owners_count, dtype=jnp.int32)[None, :]).astype(
        jnp.int32
    )
    slot_rank = jnp.sum(jnp.cumsum(onehot, axis=0) * onehot, axis=1) - 1
    slot_index = target * capacity + slot_rank
    selector = (
        slot_index[None, :] == jnp.arange(owners_count * capacity, dtype=jnp.int32)[:, None]
    ).astype(jnp.bfloat16)
    outgoing = jnp.dot(selector, updated, preferred_element_type=jnp.float32).astype(jnp.bfloat16)
    outgoing = outgoing.reshape(owners_count, capacity, all_bins)
    received = lax.all_to_all(outgoing, "pts", split_axis=0, concat_axis=0, tiled=True)
    return received.reshape(1, 1, owners_count * capacity, all_bins)


def local(spectrum, courant, upwind, coupling, sea, owner):
    bins_axis, owners_count = lax.axis_size("bins"), lax.axis_size("pts")
    points = owner.shape[2]
    suits = (
        spectrum.shape[2] == bins_axis * LANES
        and points % (2 * LANES) == 0
        and 2 * points == owners_count * LANES
        and bins_axis & (bins_axis - 1) == 0
        and owners_count & (owners_count - 1) == 0
        and bins_axis % 2 == 0
        and spectrum.shape[0] % 8 == 4
        and courant.shape[0] % 144 == 0
        and owners_count == 8
        and spectrum.shape[1] >= 3
    )
    form = chunked if suits else whole
    return form(spectrum, courant, upwind, coupling, sea, owner)


def solution(mesh):
    placed = (P("bins", "pts", None), P(), P(), P(), P("pts", None), P("pts", "bins", None, None))
    return jax.shard_map(
        local, mesh=mesh, in_specs=placed, out_specs=P("pts", "bins", None, None), check_vma=False
    )
```

```python
import functools

import jax
import jax.numpy as jnp
from jax import lax
from jax.experimental import pallas as pl
from jax.experimental.pallas import tpu as pltpu
from jax.sharding import PartitionSpec as P

F32 = jnp.float32
BF16 = jnp.bfloat16
I32 = jnp.int32
LANES = 128
CHUNKS = 4
MAIN = ((0, 1), (2,))
NT = (((1,), (1,)), ((), ()))


def round_up(size, unit):
    return -(-size // unit) * unit


def iota(shape, axis):
    return lax.broadcasted_iota(I32, shape, axis)


def dot_nt(lhs, rhs):
    return lax.dot_general(lhs, rhs, NT, preferred_element_type=F32)


def upwind_row(at, speed, side, before, center, after, sea_row):
    lats = center.shape[1]
    lane = iota(center.shape, 1)
    wide = lats // LANES
    cx, cy = [jnp.concatenate([speed[k, at, :]] * wide, axis=1) for k in range(2)]
    ux, uy = [jnp.concatenate([side[k, at, :]] * wide, axis=1) for k in range(2)]
    donor_x = jnp.where(ux == 0, before, after).astype(F32)
    left = jnp.where(lane == 0, 0, pltpu.roll(center, 1, 1))
    right = jnp.where(lane == lats - 1, 0, pltpu.roll(center, lats - 1, 1))
    donor_y = jnp.where(uy == 0, left, right).astype(F32)
    center = center.astype(F32)
    value = center - cx * (center - donor_x) - cy * (center - donor_y)
    return (value * sea_row).astype(BF16)


def inner_kernel(planes, near, speed, side, sea, moved):
    lon_rows, rows, _ = planes.shape
    top = lon_rows - 1
    even = lax.axis_index("pts") % 2 == 0
    sea_f = sea[...].astype(F32)
    sea_b = sea_f.astype(BF16)

    def tile(at, close):
        masked = [planes[l, at, :] * sea_b[l : l + 1, :] for l in range(lon_rows)]
        for l in range(1, top):
            moved[l - 1, at, :] = upwind_row(
                at, speed, side, masked[l - 1], masked[l], masked[l + 1], sea_f[l : l + 1, :]
            )
        center = jnp.where(even, masked[top], masked[0])
        below = jnp.where(even, masked[top - 1], close)
        above = jnp.where(even, close, masked[1])
        weight = jnp.where(even, sea_f[top : top + 1, :], sea_f[0:1, :])
        moved[top - 1, at, :] = upwind_row(at, speed, side, below, center, above, weight)

    over_rows(tile, rows, near)


def over_rows(tile, rows, halo):
    held = halo.shape[0]
    full = held // 16 * 16

    def step(index, carry):
        at = pl.ds(pl.multiple_of(index * 16, 16), 16)
        tile(at, halo[at, :])
        return carry

    lax.fori_loop(0, full // 16, step, 0, unroll=5)
    if full < rows:
        spare = jnp.zeros((rows - held, halo.shape[1]), F32)
        end = jnp.concatenate([halo[full:, :].astype(F32), spare], axis=0).astype(BF16)
        tile(pl.ds(full, 16), end)


def order_kernel(bins_axis, owners_count, width, slots, *refs):
    inner, sea = refs[:2]
    owner = refs[2 : 2 + bins_axis]
    part, far_order, meta, order = refs[2 + bins_axis :]
    lon_rows, rows = inner.shape[0] + 1, inner.shape[1]
    points = lon_rows * LANES
    me = lax.axis_index("bins")
    me_pts = lax.axis_index("pts")
    even = me_pts % 2 == 0
    last = (lon_rows - 1) * LANES
    near_at = pl.ds(pl.multiple_of(jnp.where(even, last, 0), LANES), LANES)
    far_at = pl.ds(pl.multiple_of(jnp.where(even, 0, last), LANES), LANES)
    owners_id = iota((owners_count, points), 0)
    hot = [(owner[m][...] == owners_id).astype(F32) for m in range(bins_axis)]
    earlier = (iota((points, points), 0) < iota((points, points), 1)).astype(F32).astype(BF16)
    before = jnp.dot(
        jnp.concatenate(hot, axis=0).astype(BF16), earlier, preferred_element_type=F32
    )
    main = (CHUNKS - 1) * width
    place_id = iota(order.shape, 0)
    none = [jnp.zeros((1, points), F32)]
    for m in range(bins_axis):
        own = owner[m][...]
        count = jnp.sum(hot[m], axis=1, keepdims=True)
        offset = jnp.sum(jnp.where(owners_id < own, count, 0.0), axis=0, keepdims=True)
        mine = before[m * owners_count : (m + 1) * owners_count, :]
        rank = jnp.sum(hot[m] * mine, axis=0, keepdims=True)
        key, first = (offset + rank).astype(I32), offset.astype(I32)
        quarter = key & (CHUNKS - 1)
        slot = (key - first - ((quarter - first) & (CHUNKS - 1))) // CHUNKS
        towards = own ^ me_pts
        block = me ^ m
        group = (towards & (CHUNKS - 1)) ^ block
        spread = main + towards // CHUNKS * LANES + group * slots + slot
        place = jnp.where(quarter < CHUNKS - 1, quarter * width + key // CHUNKS, spread)
        order[...] = (place_id == place).astype(F32).astype(BF16)
        far_order[m] = order[:, far_at]
        at = pl.ds(pl.multiple_of(block * LANES, LANES), LANES)
        cells = jnp.concatenate([inner[l, :, at] for l in range(lon_rows - 1)], axis=1)
        columns = jnp.concatenate([order[:, LANES:last], order[:, near_at]], axis=1)
        part[m] = dot_nt(cells, columns).astype(BF16)
        weight = jnp.concatenate([sea[l : l + 1, at].astype(F32) for l in range(lon_rows)], axis=1)
        facts = jnp.concatenate(none * 4 + [weight, rank] + none * 10, axis=0).astype(BF16)
        end = slice(rows - 16, rows)
        spare = part[m, end, main:].astype(F32) + dot_nt(facts, order[main:, :])
        part[m, end, main:] = spare.astype(BF16)
        if m == 0:
            facts = [slot.astype(F32), towards.astype(F32), rank, weight] + none * 4
            meta[...] = dot_nt(jnp.concatenate(facts, axis=0).astype(BF16), order[:main, :])


def pack_kernel(rows_out, bins_axis, width, pairs, *refs):
    planes, far, speed, side, sea, part, far_order = refs[:7]
    chunks, moved = refs[7:-1], refs[-1]
    direct = chunks[len(MAIN) * bins_axis :]
    lon_rows, rows, _ = planes.shape
    top = lon_rows - 1
    me = lax.axis_index("bins")
    even = lax.axis_index("pts") % 2 == 0
    center_row, next_row = jnp.where(even, 0, top), jnp.where(even, 1, top - 1)
    sea_f = sea[...].astype(F32)
    center_sea = jnp.where(even, sea_f[0:1, :], sea_f[top : top + 1, :])
    next_sea = jnp.where(even, sea_f[1:2, :], sea_f[top - 1 : top, :]).astype(BF16)

    def tile(at, distant):
        center = planes[center_row, at, :] * center_sea.astype(BF16)
        beside = planes[next_row, at, :] * next_sea
        below, above = jnp.where(even, distant, beside), jnp.where(even, beside, distant)
        moved[at, :] = upwind_row(at, speed, side, below, center, above, center_sea)

    over_rows(tile, rows, far)
    spread = []
    for m in range(bins_axis):
        at = pl.ds(pl.multiple_of((me ^ m) * LANES, LANES), LANES)
        ordered = dot_nt(moved[:, at], far_order[m]) + part[m].astype(F32)
        ordered = ordered[:rows_out]
        ordered = jnp.where((me & 1) == 1, pltpu.roll(ordered, 4, 0), ordered).astype(BF16)
        for c, quarters in enumerate(MAIN):
            at = slice(quarters[0] * width, (quarters[-1] + 1) * width)
            chunks[c * bins_axis + m][...] = ordered[:, at]
        spread.append(ordered[:, (CHUNKS - 1) * width :])
    group = iota((rows_out, LANES), 1) // (LANES // CHUNKS)
    for x in range(2 * pairs):
        at = slice(x // CHUNKS * LANES, (x // CHUNKS + 1) * LANES)
        mixed = spread[0][:, at]
        for m in range(1, bins_axis):
            mixed = jnp.where(group == ((me ^ m) ^ (x % CHUNKS)), spread[m][:, at], mixed)
        direct[x // 2][x % 2, 0] = mixed


def regroup_kernel(bins_axis, pairs, *refs):
    came, swapped, outs = refs[:pairs], refs[pairs], refs[pairs + 1 :]
    me = lax.axis_index("bins")
    sources = [swapped[x // 2, 0] if x % 2 else came[x // 2][0, 0] for x in range(2 * pairs)]
    group = iota(sources[0].shape, 1) // (LANES // CHUNKS)
    for m in range(bins_axis):
        for u in range(2 * pairs // CHUNKS):
            mixed = sources[u * CHUNKS]
            for k in range(1, CHUNKS):
                mixed = jnp.where(group == ((me ^ m) ^ k), sources[u * CHUNKS + k], mixed)
            outs[m][:, u * LANES : (u + 1) * LANES] = mixed


def transpose_kernel(coupling, out):
    bins = coupling.shape[0]
    for start in range(0, bins, 256):
        size = min(256, bins - start)
        eye = (iota((size, size), 0) == iota((size, size), 1)).astype(F32).astype(BF16)
        out[start : start + size, :] = dot_nt(eye, coupling[:, start : start + size]).astype(BF16)


def lane_groups(blocks, shift):
    group = iota(blocks[0].shape, 1) // (LANES // CHUNKS)
    mixed = blocks[shift]
    for q in range(1, CHUNKS):
        mixed = jnp.where(group == q, blocks[q ^ shift], mixed)
    return mixed


def couple_kernel(quarters, bins_axis, local_bins, slots, pairs, *refs):
    blocks = refs[:bins_axis]
    weights, meta = refs[bins_axis : bins_axis + 2]
    values, outs = refs[-1], refs[-1 - pairs : -1]
    rows, columns = blocks[0].shape
    all_bins = values.shape[0]
    held = all_bins // CHUNKS
    tall = outs[0].shape[2]
    at_owner = quarters[0] == CHUNKS - 1
    me = lax.axis_index("bins")
    values[...] = jnp.zeros_like(values)
    row = iota((rows, columns), 0)
    for m in range(bins_axis):
        block = me ^ m
        at = pl.ds(pl.multiple_of(block * local_bins - 4 * (block & 1), 8), rows)
        arrived = blocks[m][...].astype(F32)
        if at_owner:
            lead = 4 * (block & 1)
            arrived = jnp.where((row >= lead) & (row < local_bins + lead), arrived, 0.0)
        values[at, :] += arrived
    flat = values[...].astype(BF16)
    energy = jnp.sum(values[...], axis=0, keepdims=True) / all_bins
    if at_owner:
        own = blocks[0][...].astype(F32)
        spare = jnp.where((me & 1) == 1, own[0:4, :], own[local_bins : local_bins + 4, :])
        weight, rank = spare[0:1, :], spare[1:2, :]
        lane = iota((1, columns), 1)
        slot = lane & (slots - 1)
        low = ((lane // slots) & (CHUNKS - 1)) ^ me
        towards = lane // LANES * CHUNKS + low
    else:
        facts = meta[:, quarters[0] * LANES : (quarters[-1] + 1) * LANES]
        slot, towards = facts[0:1, :].astype(I32), facts[1:2, :].astype(I32)
        rank, weight = facts[2:3, :], facts[3:4, :]
    scale = weight / (1.0 + energy)
    step = all_bins // 9
    for start in range(0, all_bins, step):
        at = slice(start, start + step)
        coupled = jnp.dot(weights[at, :], flat, preferred_element_type=F32)
        values[at, :] = (values[at, :] + coupled) * scale
    width = columns // len(quarters)
    slot_id = iota((2 * pairs * slots, width), 0)
    row_id = iota((tall, width), 0)
    for n, quarter in enumerate(quarters):
        cut = slice(n * width, (n + 1) * width)
        sent = []
        for v in range(CHUNKS):
            start = (v ^ quarter) * held
            lead = start % 8
            updated = values[start - lead : start - lead + tall, cut]
            if lead:
                updated = pltpu.roll(updated, tall - lead, 0)
            updated = jnp.where(row_id < held, updated, jnp.where(row_id == held, rank[:, cut], 0.0))
            group = (towards[:, cut] & (CHUNKS - 1)) ^ v
            column = towards[:, cut] // CHUNKS * LANES + group * slots + slot[:, cut]
            route = (slot_id == column).astype(F32).astype(BF16)
            sent.append(dot_nt(updated.astype(BF16), route).astype(BF16))
        for x in range(2 * pairs):
            at = slice(x // CHUNKS * LANES, (x // CHUNKS + 1) * LANES)
            outs[x // 2][x % 2, n] = lane_groups([rows_v[:, at] for rows_v in sent], x % CHUNKS)


def place_kernel(held, sources, picks, *refs):
    out, staged, sems = refs[-3:]
    me = lax.axis_index("pts")
    tall = refs[0].shape[-2]
    slot_id = iota((LANES, LANES), 0)
    copies = []
    for number, x in enumerate(sources):
        blocks = [refs[n][index] for n, index in picks[number]]
        pieces = []
        for g in range(CHUNKS):
            lhs = lane_groups(blocks, (x % CHUNKS) ^ g)
            rank = lhs[tall - 8 :, :].astype(F32)[held - tall + 8 : held - tall + 9, :].astype(I32)
            spots = (slot_id == rank).astype(F32).astype(BF16)
            pieces.append(dot_nt(lhs, spots)[:held])
        staged[number] = jnp.concatenate(pieces, axis=0).astype(BF16)
        at = pl.ds(pl.multiple_of((me ^ x) * LANES, LANES), LANES)
        copy = pltpu.make_async_copy(staged.at[number], out.at[:, at], sems.at[number])
        copy.start()
        copies.append(copy)
    for copy in copies:
        copy.wait()


def place(out, owners_count, all_bins, sources):
    arrays, picks = [], []
    for x in sorted(sources):
        mine = []
        for array, index in sources[x]:
            known = [n for n, a in enumerate(arrays) if a is array]
            if not known:
                arrays.append(array)
                known = [len(arrays) - 1]
            mine.append((known[0], index))
        picks.append(tuple(mine))
    held = [] if out is None else [out]
    return pl.pallas_call(
        functools.partial(place_kernel, all_bins // CHUNKS, tuple(sorted(sources)), tuple(picks)),
        out_shape=jax.ShapeDtypeStruct((all_bins, owners_count * LANES), BF16),
        in_specs=vmem(len(arrays)) + [pl.BlockSpec(memory_space=pl.ANY)] * len(held),
        out_specs=pl.BlockSpec(memory_space=pl.ANY),
        scratch_shapes=[
            pltpu.VMEM((len(sources), all_bins, LANES), BF16),
            pltpu.SemaphoreType.DMA((len(sources),)),
        ],
        input_output_aliases={len(arrays): 0} if held else {},
        compiler_params=params(16),
        cost_estimate=cost(1, 1),
        name="place",
    )(*arrays, *held)


def gate_kernel(array, *refs):
    refs[-1][...] = array[...]


def gate(array, *after):
    return pl.pallas_call(
        gate_kernel,
        out_shape=jax.ShapeDtypeStruct(array.shape, array.dtype),
        in_specs=vmem(1 + len(after)),
        out_specs=vmem(1)[0],
        compiler_params=params(16),
        cost_estimate=cost(1, 1),
        name="gate",
    )(array, *after)


def stack_kernel(count, *refs):
    for t in range(count):
        refs[-1][t] = refs[t][1]


def stack(pairs, *after):
    return pl.pallas_call(
        functools.partial(stack_kernel, len(pairs)),
        out_shape=jax.ShapeDtypeStruct((len(pairs),) + pairs[0].shape[1:], pairs[0].dtype),
        in_specs=vmem(len(pairs) + len(after)),
        out_specs=vmem(1)[0],
        compiler_params=params(8),
        cost_estimate=cost(1, 1),
        name="stack",
    )(*pairs, *after)


def params(mib):
    return pltpu.CompilerParams(vmem_limit_bytes=mib << 20)


def vmem(count):
    return [pl.BlockSpec(memory_space=pltpu.VMEM)] * count


def cost(flops, bytes_accessed):
    del bytes_accessed
    return pl.CostEstimate(flops=int(flops), bytes_accessed=1, transcendentals=0)


def exchange(array, axis, offset):
    return lax.ppermute(array, axis, [(i, i ^ offset) for i in range(lax.axis_size(axis))])


def chunked(spectrum, courant, upwind, coupling, sea, owner):
    local_bins, lon_rows, lats = spectrum.shape
    all_bins = courant.shape[0]
    bins_axis = lax.axis_size("bins")
    owners_count = lax.axis_size("pts")
    points = lon_rows * LANES
    width = points // CHUNKS
    slots = 2 * points // owners_count // CHUNKS
    tall = round_up(local_bins, 16)
    rows = round_up(local_bins + 1, 8)
    order_columns = (CHUNKS - 1) * width + owners_count * slots
    pairs = owners_count // 2
    quarter_rows = round_up(all_bins // CHUNKS + 1, 8)
    first_bin = lax.axis_index("bins") * local_bins

    planes = jnp.pad(jnp.transpose(spectrum, (1, 0, 2)), ((0, 0), (0, tall - local_bins), (0, 0)))
    even = lax.axis_index("pts") % 2 == 0
    rows_at = [jnp.where(even, 0, lon_rows - 1), jnp.where(even, lon_rows - 1, 0)]
    edges = [
        lax.dynamic_index_in_dim(planes, r, 0, False)[:local_bins]
        * lax.dynamic_index_in_dim(sea, r, 0, False).astype(BF16)[None]
        for r in rows_at
    ]
    between = [(i, i + 1) for i in range(1, owners_count - 1, 2)]
    far = lax.ppermute(edges[0], "pts", between + [(b, a) for a, b in between])
    near = exchange(edges[1], "pts", 1)
    own = owner.reshape(1, points)
    owners = [own, *reversed([exchange(own, "bins", m) for m in range(bins_axis - 1, 0, -1)])]

    def wide(table, dtype):
        mine = lax.dynamic_slice_in_dim(table.T, first_bin, local_bins, 1).astype(dtype)
        mine = jnp.pad(mine, ((0, 0), (0, tall - local_bins)))
        return jnp.broadcast_to(mine[:, :, None], (2, tall, LANES))

    speed, side = wide(courant, F32), wide(upwind, BF16)

    weights = pl.pallas_call(
        transpose_kernel,
        out_shape=jax.ShapeDtypeStruct(coupling.shape, BF16),
        in_specs=vmem(1),
        out_specs=vmem(1)[0],
        compiler_params=params(16),
        cost_estimate=cost(1, 1),
        name="transpose",
    )(coupling)

    inner = pl.pallas_call(
        inner_kernel,
        out_shape=jax.ShapeDtypeStruct((lon_rows - 1, tall, lats), BF16),
        in_specs=vmem(5),
        out_specs=vmem(1)[0],
        compiler_params=params(16),
        cost_estimate=cost(1, 1),
        name="inner",
    )(planes, near, speed, side, sea)
    part, far_order, meta = pl.pallas_call(
        functools.partial(order_kernel, bins_axis, owners_count, width, slots),
        out_shape=[
            jax.ShapeDtypeStruct((bins_axis, tall, order_columns), BF16),
            jax.ShapeDtypeStruct((bins_axis, order_columns, LANES), BF16),
            jax.ShapeDtypeStruct((8, (CHUNKS - 1) * width), F32),
        ],
        in_specs=vmem(2 + bins_axis),
        out_specs=vmem(3),
        scratch_shapes=[pltpu.VMEM((order_columns, points), BF16)],
        compiler_params=params(16),
        cost_estimate=cost(1, 1),
        name="order",
    )(inner, sea, *owners)
    packed = pl.pallas_call(
        functools.partial(pack_kernel, rows, bins_axis, width, pairs),
        out_shape=[
            jax.ShapeDtypeStruct((rows, len(quarters) * width), BF16)
            for quarters in MAIN
            for _ in range(bins_axis)
        ]
        + [jax.ShapeDtypeStruct((2, 1, rows, LANES), BF16)] * pairs,
        in_specs=vmem(7),
        out_specs=vmem(len(MAIN) * bins_axis + pairs),
        scratch_shapes=[pltpu.VMEM((tall, lats), BF16)],
        compiler_params=params(16),
        cost_estimate=cost(1, 1),
        name="pack",
    )(planes, far, speed, side, sea, part, far_order)

    def couple(quarters, blocks, ready):
        shape = (2, len(quarters), quarter_rows, LANES)
        return pl.pallas_call(
            functools.partial(couple_kernel, quarters, bins_axis, local_bins, slots, pairs),
            out_shape=[jax.ShapeDtypeStruct(shape, BF16)] * pairs,
            in_specs=vmem(len(blocks) + 2 + len(ready)),
            out_specs=vmem(pairs),
            scratch_shapes=[pltpu.VMEM((all_bins, blocks[0].shape[1]), F32)],
            compiler_params=params(16),
            cost_estimate=cost((3e9, 1, 3e10, 3e10)[quarters[0]], 1),
            name="couple",
        )(*blocks, weights, meta, *ready)

    def over_bins(blocks):
        return [blocks[0]] + [exchange(blocks[m], "bins", m) for m in range(1, bins_axis)]

    def over_pts(pays):
        sent = {0: pays[0]}
        for t in range(pairs - 1, 0, -1):
            sent[t] = exchange(pays[t], "pts", 2 * t)
        return [sent[t] for t in range(pairs)]

    def held_back(blocks, *after):
        return [blocks[0]] + [gate(b, *after) for b in blocks[1:]]

    early, late = packed[:bins_axis], packed[bins_axis : 2 * bins_axis]
    direct = packed[2 * bins_axis :]
    first = over_bins(early)
    direct = over_pts(direct)
    late = [late[0], gate(late[1], first[1], weights), *[gate(b, *first[1:]) for b in late[2:]]]
    second = over_bins(late)
    came = [over_pts(couple(MAIN[0], first, late[1:]))]
    regrouped = pl.pallas_call(
        functools.partial(regroup_kernel, bins_axis, pairs),
        out_shape=[jax.ShapeDtypeStruct((rows, owners_count * slots), BF16)] * bins_axis,
        in_specs=vmem(pairs + 1),
        out_specs=vmem(bins_axis),
        compiler_params=params(16),
        cost_estimate=cost(1, 1),
        name="regroup",
    )(*direct, exchange(stack(direct, came[0][0]), "pts", 1))
    regrouped = [
        regrouped[0],
        gate(regrouped[1], *second[1:], came[0][0], came[0][pairs - 1]),
        *[gate(b, *second[1:], came[0][0]) for b in regrouped[2:]],
    ]
    third = over_bins(regrouped)
    came.append(over_pts(couple(MAIN[1], second, regrouped[2:])))
    last = came[-1]
    here = couple((CHUNKS - 1,), third, [])
    swapped = [exchange(stack(came[0], *third[2:]), "pts", 1), exchange(stack(last, here[0]), "pts", 1)]

    shape = (owners_count, all_bins)
    cuts = [(c, n) for c, quarters in enumerate(MAIN) for n in range(len(quarters))]
    near_side = {
        2 * t: [(came[c][t], (0, n)) for c, n in cuts] + [(here[t], (0, 0))] for t in range(pairs)
    }
    far_side = {
        2 * t + 1: [(swapped[c], (t, n)) for c, n in cuts] + [(here[t], (1, 0))] for t in range(pairs)
    }
    placed = place(place(None, *shape, near_side), *shape, far_side)
    return jnp.transpose(placed).reshape(1, 1, owners_count * LANES, all_bins)


def padded_2(block, sides, width):
    for axis, dim in sides:
        count = lax.axis_size(axis)
        forward = [(i, i + 1) for i in range(count - 1)]
        backward = [(target, source) for source, target in forward]
        low = lax.ppermute(
            lax.slice_in_dim(block, block.shape[dim] - width, None, axis=dim), axis, forward
        )
        high = lax.ppermute(lax.slice_in_dim(block, 0, width, axis=dim), axis, backward)
        block = jnp.concatenate([low, block, high], axis=dim)
    return block


def advect(padded, sea_mask, courant, upwind):
    center = padded[:, 1:-1, 1:-1]
    donor_x = jnp.where(upwind[:, 0][:, None, None] == 0, padded[:, :-2, 1:-1], padded[:, 2:, 1:-1])
    donor_y = jnp.where(upwind[:, 1][:, None, None] == 0, padded[:, 1:-1, :-2], padded[:, 1:-1, 2:])
    moved = (
        center
        - courant[:, 0][:, None, None] * (center - donor_x)
        - courant[:, 1][:, None, None] * (center - donor_y)
    )
    return (moved * sea_mask[None]).astype(jnp.bfloat16)


def whole(spectrum, courant, upwind, coupling, sea, owner):
    local_bins = spectrum.shape[0]
    lon_rows = spectrum.shape[1]
    bins_count = lax.axis_size("bins")
    lat_cells = spectrum.shape[2] // bins_count
    masked = spectrum * sea.astype(jnp.bfloat16)[None]
    local_sea = lax.dynamic_slice_in_dim(
        sea, lax.axis_index("bins") * lat_cells, lat_cells, 1
    ).astype(jnp.float32)
    first_bin = lax.axis_index("bins") * local_bins
    my_courant = lax.dynamic_slice_in_dim(courant, first_bin, local_bins, 0)
    my_upwind = lax.dynamic_slice_in_dim(upwind, first_bin, local_bins, 0)
    extended = padded_2(masked, (("pts", 1),), 1)
    extended = jnp.pad(extended.astype(jnp.float32), ((0, 0), (0, 0), (1, 1)))
    moved = advect(extended, sea.astype(jnp.float32), my_courant, my_upwind)
    columns = lax.all_to_all(moved, "bins", split_axis=2, concat_axis=0, tiled=True)
    all_bins = columns.shape[0]
    points = lon_rows * lat_cells
    flat = columns.reshape(all_bins, points)
    energy = jnp.mean(flat.astype(jnp.float32), axis=0)
    coupled = jnp.einsum("bp,bc->pc", flat, coupling, preferred_element_type=jnp.float32)
    weights = local_sea.reshape(points)
    updated = (
        weights[:, None] * (flat.astype(jnp.float32).T + coupled) / (1.0 + energy)[:, None]
    ).astype(jnp.bfloat16)
    owners_count = lax.axis_size("pts")
    capacity = max(2, (2 * points + owners_count - 1) // owners_count)
    target = owner.reshape(points)
    onehot = (target[:, None] == jnp.arange(owners_count, dtype=jnp.int32)[None, :]).astype(
        jnp.int32
    )
    slot_rank = jnp.sum(jnp.cumsum(onehot, axis=0) * onehot, axis=1) - 1
    slot_index = target * capacity + slot_rank
    selector = (
        slot_index[None, :] == jnp.arange(owners_count * capacity, dtype=jnp.int32)[:, None]
    ).astype(jnp.bfloat16)
    outgoing = jnp.dot(selector, updated, preferred_element_type=jnp.float32).astype(jnp.bfloat16)
    outgoing = outgoing.reshape(owners_count, capacity, all_bins)
    received = lax.all_to_all(outgoing, "pts", split_axis=0, concat_axis=0, tiled=True)
    return received.reshape(1, 1, owners_count * capacity, all_bins)


def local(spectrum, courant, upwind, coupling, sea, owner):
    bins_axis, owners_count = lax.axis_size("bins"), lax.axis_size("pts")
    points = owner.shape[2]
    suits = (
        spectrum.shape[2] == bins_axis * LANES
        and points % (2 * LANES) == 0
        and 2 * points == owners_count * LANES
        and bins_axis & (bins_axis - 1) == 0
        and owners_count & (owners_count - 1) == 0
        and bins_axis % 2 == 0
        and spectrum.shape[0] % 8 == 4
        and courant.shape[0] % 144 == 0
        and courant.shape[0] // CHUNKS % 8 == 4
        and points == CHUNKS * LANES
        and bins_axis == CHUNKS
        and owners_count == 8
        and spectrum.shape[1] >= 3
    )
    form = chunked if suits else whole
    return form(spectrum, courant, upwind, coupling, sea, owner)


def solution(mesh):
    placed = (P("bins", "pts", None), P(), P(), P(), P("pts", None), P("pts", "bins", None, None))
    return jax.shard_map(
        local, mesh=mesh, in_specs=placed, out_specs=P("pts", "bins", None, None), check_vma=False
    )
```

```python
import functools

import jax
import jax.numpy as jnp
from jax import lax
from jax.experimental import pallas as pl
from jax.experimental.pallas import tpu as pltpu
from jax.sharding import PartitionSpec as P

F32 = jnp.float32
BF16 = jnp.bfloat16
I32 = jnp.int32
LANES = 128
CHUNKS = 4
MAIN = ((0, 1), (2,))
NT = (((1,), (1,)), ((), ()))


def round_up(size, unit):
    return -(-size // unit) * unit


def iota(shape, axis):
    return lax.broadcasted_iota(I32, shape, axis)


def dot_nt(lhs, rhs):
    return lax.dot_general(lhs, rhs, NT, preferred_element_type=F32)


def upwind_row(at, speed, side, before, center, after, sea_row):
    lats = center.shape[1]
    lane = iota(center.shape, 1)
    wide = lats // LANES
    cx, cy = [jnp.concatenate([speed[k, at, :]] * wide, axis=1) for k in range(2)]
    ux, uy = [jnp.concatenate([side[k, at, :]] * wide, axis=1) for k in range(2)]
    donor_x = jnp.where(ux == 0, before, after).astype(F32)
    left = jnp.where(lane == 0, 0, pltpu.roll(center, 1, 1))
    right = jnp.where(lane == lats - 1, 0, pltpu.roll(center, lats - 1, 1))
    donor_y = jnp.where(uy == 0, left, right).astype(F32)
    center = center.astype(F32)
    value = center - cx * (center - donor_x) - cy * (center - donor_y)
    return (value * sea_row).astype(BF16)


def inner_kernel(planes, near, speed, side, sea, moved):
    lon_rows, rows, _ = planes.shape
    top = lon_rows - 1
    even = lax.axis_index("pts") % 2 == 0
    sea_f = sea[...].astype(F32)
    sea_b = sea_f.astype(BF16)

    def tile(at, close):
        masked = [planes[l, at, :] * sea_b[l : l + 1, :] for l in range(lon_rows)]
        for l in range(1, top):
            moved[l - 1, at, :] = upwind_row(
                at, speed, side, masked[l - 1], masked[l], masked[l + 1], sea_f[l : l + 1, :]
            )
        center = jnp.where(even, masked[top], masked[0])
        below = jnp.where(even, masked[top - 1], close)
        above = jnp.where(even, close, masked[1])
        weight = jnp.where(even, sea_f[top : top + 1, :], sea_f[0:1, :])
        moved[top - 1, at, :] = upwind_row(at, speed, side, below, center, above, weight)

    over_rows(tile, rows, near)


def over_rows(tile, rows, halo):
    held = halo.shape[0]
    full = held // 16 * 16

    def step(index, carry):
        at = pl.ds(pl.multiple_of(index * 16, 16), 16)
        tile(at, halo[at, :])
        return carry

    lax.fori_loop(0, full // 16, step, 0, unroll=5)
    if full < rows:
        spare = jnp.zeros((rows - held, halo.shape[1]), F32)
        end = jnp.concatenate([halo[full:, :].astype(F32), spare], axis=0).astype(BF16)
        tile(pl.ds(full, 16), end)


def order_kernel(bins_axis, owners_count, width, slots, *refs):
    inner, sea = refs[:2]
    owner = refs[2 : 2 + bins_axis]
    part, far_order, meta, order = refs[2 + bins_axis :]
    lon_rows, rows = inner.shape[0] + 1, inner.shape[1]
    points = lon_rows * LANES
    me = lax.axis_index("bins")
    me_pts = lax.axis_index("pts")
    even = me_pts % 2 == 0
    last = (lon_rows - 1) * LANES
    near_at = pl.ds(pl.multiple_of(jnp.where(even, last, 0), LANES), LANES)
    far_at = pl.ds(pl.multiple_of(jnp.where(even, 0, last), LANES), LANES)
    owners_id = iota((owners_count, points), 0)
    hot = [(owner[m][...] == owners_id).astype(F32) for m in range(bins_axis)]
    earlier = (iota((points, points), 0) < iota((points, points), 1)).astype(F32).astype(BF16)
    before = jnp.dot(
        jnp.concatenate(hot, axis=0).astype(BF16), earlier, preferred_element_type=F32
    )
    main = (CHUNKS - 1) * width
    place_id = iota(order.shape, 0)
    none = [jnp.zeros((1, points), F32)]
    for m in range(bins_axis):
        own = owner[m][...]
        count = jnp.sum(hot[m], axis=1, keepdims=True)
        offset = jnp.sum(jnp.where(owners_id < own, count, 0.0), axis=0, keepdims=True)
        mine = before[m * owners_count : (m + 1) * owners_count, :]
        rank = jnp.sum(hot[m] * mine, axis=0, keepdims=True)
        key, first = (offset + rank).astype(I32), offset.astype(I32)
        quarter = key & (CHUNKS - 1)
        slot = (key - first - ((quarter - first) & (CHUNKS - 1))) // CHUNKS
        towards = own ^ me_pts
        block = me ^ m
        group = (towards & (CHUNKS - 1)) ^ block
        spread = main + towards // CHUNKS * LANES + group * slots + slot
        place = jnp.where(quarter < CHUNKS - 1, quarter * width + key // CHUNKS, spread)
        order[...] = (place_id == place).astype(F32).astype(BF16)
        far_order[m] = order[:, far_at]
        at = pl.ds(pl.multiple_of(block * LANES, LANES), LANES)
        cells = jnp.concatenate([inner[l, :, at] for l in range(lon_rows - 1)], axis=1)
        columns = jnp.concatenate([order[:, LANES:last], order[:, near_at]], axis=1)
        part[m] = dot_nt(cells, columns).astype(BF16)
        weight = jnp.concatenate([sea[l : l + 1, at].astype(F32) for l in range(lon_rows)], axis=1)
        facts = jnp.concatenate(none * 4 + [weight, rank] + none * 10, axis=0).astype(BF16)
        end = slice(rows - 16, rows)
        spare = part[m, end, main:].astype(F32) + dot_nt(facts, order[main:, :])
        part[m, end, main:] = spare.astype(BF16)
        if m == 0:
            facts = [slot.astype(F32), towards.astype(F32), rank, weight] + none * 4
            meta[...] = dot_nt(jnp.concatenate(facts, axis=0).astype(BF16), order[:main, :])


def pack_kernel(rows_out, bins_axis, width, pairs, *refs):
    planes, far, speed, side, sea, part, far_order = refs[:7]
    chunks, moved = refs[7:-1], refs[-1]
    direct = chunks[len(MAIN) * bins_axis :]
    lon_rows, rows, _ = planes.shape
    top = lon_rows - 1
    me = lax.axis_index("bins")
    even = lax.axis_index("pts") % 2 == 0
    center_row, next_row = jnp.where(even, 0, top), jnp.where(even, 1, top - 1)
    sea_f = sea[...].astype(F32)
    center_sea = jnp.where(even, sea_f[0:1, :], sea_f[top : top + 1, :])
    next_sea = jnp.where(even, sea_f[1:2, :], sea_f[top - 1 : top, :]).astype(BF16)

    def tile(at, distant):
        center = planes[center_row, at, :] * center_sea.astype(BF16)
        beside = planes[next_row, at, :] * next_sea
        below, above = jnp.where(even, distant, beside), jnp.where(even, beside, distant)
        moved[at, :] = upwind_row(at, speed, side, below, center, above, center_sea)

    over_rows(tile, rows, far)
    spread = []
    for m in range(bins_axis):
        at = pl.ds(pl.multiple_of((me ^ m) * LANES, LANES), LANES)
        ordered = dot_nt(moved[:, at], far_order[m]) + part[m].astype(F32)
        ordered = ordered[:rows_out]
        ordered = jnp.where((me & 1) == 1, pltpu.roll(ordered, 4, 0), ordered).astype(BF16)
        for c, quarters in enumerate(MAIN):
            at = slice(quarters[0] * width, (quarters[-1] + 1) * width)
            chunks[c * bins_axis + m][...] = ordered[:, at]
        spread.append(ordered[:, (CHUNKS - 1) * width :])
    group = iota((rows_out, LANES), 1) // (LANES // CHUNKS)
    for x in range(2 * pairs):
        at = slice(x // CHUNKS * LANES, (x // CHUNKS + 1) * LANES)
        mixed = spread[0][:, at]
        for m in range(1, bins_axis):
            mixed = jnp.where(group == ((me ^ m) ^ (x % CHUNKS)), spread[m][:, at], mixed)
        direct[x // 2][x % 2, 0] = mixed


def regroup_kernel(bins_axis, pairs, *refs):
    came, swapped, outs = refs[:pairs], refs[pairs], refs[pairs + 1 :]
    me = lax.axis_index("bins")
    sources = [swapped[x // 2, 0] if x % 2 else came[x // 2][0, 0] for x in range(2 * pairs)]
    group = iota(sources[0].shape, 1) // (LANES // CHUNKS)
    for m in range(bins_axis):
        for u in range(2 * pairs // CHUNKS):
            mixed = sources[u * CHUNKS]
            for k in range(1, CHUNKS):
                mixed = jnp.where(group == ((me ^ m) ^ k), sources[u * CHUNKS + k], mixed)
            outs[m][:, u * LANES : (u + 1) * LANES] = mixed


def transpose_kernel(coupling, out):
    bins = coupling.shape[0]
    for start in range(0, bins, 256):
        size = min(256, bins - start)
        eye = (iota((size, size), 0) == iota((size, size), 1)).astype(F32).astype(BF16)
        out[start : start + size, :] = dot_nt(eye, coupling[:, start : start + size]).astype(BF16)


def lane_groups(blocks, shift):
    group = iota(blocks[0].shape, 1) // (LANES // CHUNKS)
    mixed = blocks[shift]
    for q in range(1, CHUNKS):
        mixed = jnp.where(group == q, blocks[q ^ shift], mixed)
    return mixed


def couple_kernel(quarters, bins_axis, local_bins, slots, pairs, *refs):
    blocks = refs[:bins_axis]
    weights, meta = refs[bins_axis : bins_axis + 2]
    values, outs = refs[-1], refs[-1 - pairs : -1]
    rows, columns = blocks[0].shape
    all_bins = values.shape[0]
    held = all_bins // CHUNKS
    tall = outs[0].shape[2]
    at_owner = quarters[0] == CHUNKS - 1
    me = lax.axis_index("bins")
    values[...] = jnp.zeros_like(values)
    row = iota((rows, columns), 0)
    for m in range(bins_axis):
        block = me ^ m
        at = pl.ds(pl.multiple_of(block * local_bins - 4 * (block & 1), 8), rows)
        arrived = blocks[m][...].astype(F32)
        if at_owner:
            lead = 4 * (block & 1)
            arrived = jnp.where((row >= lead) & (row < local_bins + lead), arrived, 0.0)
        values[at, :] += arrived
    flat = values[...].astype(BF16)
    energy = jnp.sum(values[...], axis=0, keepdims=True) / all_bins
    if at_owner:
        own = blocks[0][...].astype(F32)
        spare = jnp.where((me & 1) == 1, own[0:4, :], own[local_bins : local_bins + 4, :])
        weight, rank = spare[0:1, :], spare[1:2, :]
        lane = iota((1, columns), 1)
        slot = lane & (slots - 1)
        low = ((lane // slots) & (CHUNKS - 1)) ^ me
        towards = lane // LANES * CHUNKS + low
    else:
        facts = meta[:, quarters[0] * LANES : (quarters[-1] + 1) * LANES]
        slot, towards = facts[0:1, :].astype(I32), facts[1:2, :].astype(I32)
        rank, weight = facts[2:3, :], facts[3:4, :]
    scale = weight / (1.0 + energy)
    step = all_bins // 9
    for start in range(0, all_bins, step):
        at = slice(start, start + step)
        coupled = jnp.dot(weights[at, :], flat, preferred_element_type=F32)
        values[at, :] = (values[at, :] + coupled) * scale
    width = columns // len(quarters)
    slot_id = iota((2 * pairs * slots, width), 0)
    row_id = iota((tall, width), 0)
    for n, quarter in enumerate(quarters):
        cut = slice(n * width, (n + 1) * width)
        sent = []
        for v in range(CHUNKS):
            start = (v ^ quarter) * held
            lead = start % 8
            updated = values[start - lead : start - lead + tall, cut]
            if lead:
                updated = pltpu.roll(updated, tall - lead, 0)
            updated = jnp.where(row_id < held, updated, jnp.where(row_id == held, rank[:, cut], 0.0))
            group = (towards[:, cut] & (CHUNKS - 1)) ^ v
            column = towards[:, cut] // CHUNKS * LANES + group * slots + slot[:, cut]
            route = (slot_id == column).astype(F32).astype(BF16)
            sent.append(dot_nt(updated.astype(BF16), route).astype(BF16))
        for x in range(2 * pairs):
            at = slice(x // CHUNKS * LANES, (x // CHUNKS + 1) * LANES)
            outs[x // 2][x % 2, n] = lane_groups([rows_v[:, at] for rows_v in sent], x % CHUNKS)


def place_kernel(held, sources, picks, *refs):
    out, staged, sems = refs[-3:]
    me = lax.axis_index("pts")
    tall = refs[0].shape[-2]
    slot_id = iota((LANES, LANES), 0)
    copies = []
    for number, x in enumerate(sources):
        blocks = [refs[n][index] for n, index in picks[number]]
        pieces = []
        for g in range(CHUNKS):
            lhs = lane_groups(blocks, (x % CHUNKS) ^ g)
            rank = lhs[tall - 8 :, :].astype(F32)[held - tall + 8 : held - tall + 9, :].astype(I32)
            spots = (slot_id == rank).astype(F32).astype(BF16)
            pieces.append(dot_nt(lhs, spots)[:held])
        staged[number] = jnp.concatenate(pieces, axis=0).astype(BF16)
        at = pl.ds(pl.multiple_of((me ^ x) * LANES, LANES), LANES)
        copy = pltpu.make_async_copy(staged.at[number], out.at[:, at], sems.at[number])
        copy.start()
        copies.append(copy)
    for copy in copies:
        copy.wait()


def place(out, owners_count, all_bins, sources):
    arrays, picks = [], []
    for x in sorted(sources):
        mine = []
        for array, index in sources[x]:
            known = [n for n, a in enumerate(arrays) if a is array]
            if not known:
                arrays.append(array)
                known = [len(arrays) - 1]
            mine.append((known[0], index))
        picks.append(tuple(mine))
    held = [] if out is None else [out]
    return pl.pallas_call(
        functools.partial(place_kernel, all_bins // CHUNKS, tuple(sorted(sources)), tuple(picks)),
        out_shape=jax.ShapeDtypeStruct((all_bins, owners_count * LANES), BF16),
        in_specs=vmem(len(arrays)) + [pl.BlockSpec(memory_space=pl.ANY)] * len(held),
        out_specs=pl.BlockSpec(memory_space=pl.ANY),
        scratch_shapes=[
            pltpu.VMEM((len(sources), all_bins, LANES), BF16),
            pltpu.SemaphoreType.DMA((len(sources),)),
        ],
        input_output_aliases={len(arrays): 0} if held else {},
        compiler_params=params(16),
        cost_estimate=cost(1, 1),
        name="place",
    )(*arrays, *held)


def gate_kernel(array, *refs):
    refs[-1][...] = array[...]


def gate(array, *after):
    return pl.pallas_call(
        gate_kernel,
        out_shape=jax.ShapeDtypeStruct(array.shape, array.dtype),
        in_specs=vmem(1 + len(after)),
        out_specs=vmem(1)[0],
        compiler_params=params(16),
        cost_estimate=cost(1, 1),
        name="gate",
    )(array, *after)


def stack_kernel(count, *refs):
    for t in range(count):
        refs[-1][t] = refs[t][1]


def stack(pairs, *after):
    return pl.pallas_call(
        functools.partial(stack_kernel, len(pairs)),
        out_shape=jax.ShapeDtypeStruct((len(pairs),) + pairs[0].shape[1:], pairs[0].dtype),
        in_specs=vmem(len(pairs) + len(after)),
        out_specs=vmem(1)[0],
        compiler_params=params(8),
        cost_estimate=cost(1, 1),
        name="stack",
    )(*pairs, *after)


def params(mib):
    return pltpu.CompilerParams(vmem_limit_bytes=mib << 20)


def vmem(count):
    return [pl.BlockSpec(memory_space=pltpu.VMEM)] * count


def cost(flops, bytes_accessed):
    del bytes_accessed
    return pl.CostEstimate(flops=int(flops), bytes_accessed=1, transcendentals=0)


def exchange(array, axis, offset):
    return lax.ppermute(array, axis, [(i, i ^ offset) for i in range(lax.axis_size(axis))])


def chunked(spectrum, courant, upwind, coupling, sea, owner):
    local_bins, lon_rows, lats = spectrum.shape
    all_bins = courant.shape[0]
    bins_axis = lax.axis_size("bins")
    owners_count = lax.axis_size("pts")
    points = lon_rows * LANES
    width = points // CHUNKS
    slots = 2 * points // owners_count // CHUNKS
    tall = round_up(local_bins, 16)
    rows = round_up(local_bins + 1, 8)
    order_columns = (CHUNKS - 1) * width + owners_count * slots
    pairs = owners_count // 2
    quarter_rows = round_up(all_bins // CHUNKS + 1, 8)
    first_bin = lax.axis_index("bins") * local_bins

    planes = jnp.pad(jnp.transpose(spectrum, (1, 0, 2)), ((0, 0), (0, tall - local_bins), (0, 0)))
    even = lax.axis_index("pts") % 2 == 0
    rows_at = [jnp.where(even, 0, lon_rows - 1), jnp.where(even, lon_rows - 1, 0)]
    edges = [
        lax.dynamic_index_in_dim(planes, r, 0, False)[:local_bins]
        * lax.dynamic_index_in_dim(sea, r, 0, False).astype(BF16)[None]
        for r in rows_at
    ]
    between = [(i, i + 1) for i in range(1, owners_count - 1, 2)]
    far = lax.ppermute(edges[0], "pts", between + [(b, a) for a, b in between])
    near = exchange(edges[1], "pts", 1)
    own = owner.reshape(1, points)
    owners = [own, *reversed([exchange(own, "bins", m) for m in range(bins_axis - 1, 0, -1)])]

    def wide(table, dtype):
        mine = lax.dynamic_slice_in_dim(table.T, first_bin, local_bins, 1).astype(dtype)
        mine = jnp.pad(mine, ((0, 0), (0, tall - local_bins)))
        return jnp.broadcast_to(mine[:, :, None], (2, tall, LANES))

    speed, side = wide(courant, F32), wide(upwind, BF16)

    weights = pl.pallas_call(
        transpose_kernel,
        out_shape=jax.ShapeDtypeStruct(coupling.shape, BF16),
        in_specs=vmem(1),
        out_specs=vmem(1)[0],
        compiler_params=params(16),
        cost_estimate=cost(1, 1),
        name="transpose",
    )(coupling)

    inner = pl.pallas_call(
        inner_kernel,
        out_shape=jax.ShapeDtypeStruct((lon_rows - 1, tall, lats), BF16),
        in_specs=vmem(5),
        out_specs=vmem(1)[0],
        compiler_params=params(16),
        cost_estimate=cost(1, 1),
        name="inner",
    )(planes, near, speed, side, sea)
    part, far_order, meta = pl.pallas_call(
        functools.partial(order_kernel, bins_axis, owners_count, width, slots),
        out_shape=[
            jax.ShapeDtypeStruct((bins_axis, tall, order_columns), BF16),
            jax.ShapeDtypeStruct((bins_axis, order_columns, LANES), BF16),
            jax.ShapeDtypeStruct((8, (CHUNKS - 1) * width), F32),
        ],
        in_specs=vmem(2 + bins_axis),
        out_specs=vmem(3),
        scratch_shapes=[pltpu.VMEM((order_columns, points), BF16)],
        compiler_params=params(16),
        cost_estimate=cost(1, 1),
        name="order",
    )(inner, sea, *owners)
    packed = pl.pallas_call(
        functools.partial(pack_kernel, rows, bins_axis, width, pairs),
        out_shape=[
            jax.ShapeDtypeStruct((rows, len(quarters) * width), BF16)
            for quarters in MAIN
            for _ in range(bins_axis)
        ]
        + [jax.ShapeDtypeStruct((2, 1, rows, LANES), BF16)] * pairs,
        in_specs=vmem(7),
        out_specs=vmem(len(MAIN) * bins_axis + pairs),
        scratch_shapes=[pltpu.VMEM((tall, lats), BF16)],
        compiler_params=params(16),
        cost_estimate=cost(1, 1),
        name="pack",
    )(planes, far, speed, side, sea, part, far_order)

    def couple(quarters, blocks, ready):
        shape = (2, len(quarters), quarter_rows, LANES)
        return pl.pallas_call(
            functools.partial(couple_kernel, quarters, bins_axis, local_bins, slots, pairs),
            out_shape=[jax.ShapeDtypeStruct(shape, BF16)] * pairs,
            in_specs=vmem(len(blocks) + 2 + len(ready)),
            out_specs=vmem(pairs),
            scratch_shapes=[pltpu.VMEM((all_bins, blocks[0].shape[1]), F32)],
            compiler_params=params(16),
            cost_estimate=cost((3e9, 1, 3e10, 3e10)[quarters[0]], 1),
            name="couple",
        )(*blocks, weights, meta, *ready)

    def over_bins(blocks):
        return [blocks[0]] + [exchange(blocks[m], "bins", m) for m in range(1, bins_axis)]

    def over_pts(pays):
        sent = {0: pays[0]}
        for t in range(pairs - 1, 0, -1):
            sent[t] = exchange(pays[t], "pts", 2 * t)
        return [sent[t] for t in range(pairs)]

    def held_back(blocks, *after):
        return [blocks[0]] + [gate(b, *after) for b in blocks[1:]]

    early, late = packed[:bins_axis], packed[bins_axis : 2 * bins_axis]
    direct = packed[2 * bins_axis :]
    first = over_bins(early)
    direct = over_pts(direct)
    regrouped = pl.pallas_call(
        functools.partial(regroup_kernel, bins_axis, pairs),
        out_shape=[jax.ShapeDtypeStruct((rows, owners_count * slots), BF16)] * bins_axis,
        in_specs=vmem(pairs + 1),
        out_specs=vmem(bins_axis),
        compiler_params=params(16),
        cost_estimate=cost(1, 1),
        name="regroup",
    )(*direct, exchange(stack(direct, first[1], first[2]), "pts", 1))
    late = [late[0], gate(late[1], first[1], weights), *[gate(b, *first[1:]) for b in late[2:]]]
    second = over_bins(late)
    came = [over_pts(couple(MAIN[0], first, late[1:]))]
    regrouped = [
        regrouped[0],
        gate(regrouped[1], *second[1:], came[0][0], came[0][pairs - 1]),
        *[gate(b, *second[1:], came[0][0]) for b in regrouped[2:]],
    ]
    third = over_bins(regrouped)
    came.append(over_pts(couple(MAIN[1], second, regrouped[2:])))
    last = came[-1]
    here = couple((CHUNKS - 1,), third, [])
    swapped = [exchange(stack(came[0], last[0]), "pts", 1), exchange(stack(last, here[0]), "pts", 1)]

    shape = (owners_count, all_bins)
    cuts = [(c, n) for c, quarters in enumerate(MAIN) for n in range(len(quarters))]
    near_side = {
        2 * t: [(came[c][t], (0, n)) for c, n in cuts] + [(here[t], (0, 0))] for t in range(pairs)
    }
    far_side = {
        2 * t + 1: [(swapped[c], (t, n)) for c, n in cuts] + [(here[t], (1, 0))] for t in range(pairs)
    }
    placed = place(place(None, *shape, near_side), *shape, far_side)
    return jnp.transpose(placed).reshape(1, 1, owners_count * LANES, all_bins)


def padded_2(block, sides, width):
    for axis, dim in sides:
        count = lax.axis_size(axis)
        forward = [(i, i + 1) for i in range(count - 1)]
        backward = [(target, source) for source, target in forward]
        low = lax.ppermute(
            lax.slice_in_dim(block, block.shape[dim] - width, None, axis=dim), axis, forward
        )
        high = lax.ppermute(lax.slice_in_dim(block, 0, width, axis=dim), axis, backward)
        block = jnp.concatenate([low, block, high], axis=dim)
    return block


def advect(padded, sea_mask, courant, upwind):
    center = padded[:, 1:-1, 1:-1]
    donor_x = jnp.where(upwind[:, 0][:, None, None] == 0, padded[:, :-2, 1:-1], padded[:, 2:, 1:-1])
    donor_y = jnp.where(upwind[:, 1][:, None, None] == 0, padded[:, 1:-1, :-2], padded[:, 1:-1, 2:])
    moved = (
        center
        - courant[:, 0][:, None, None] * (center - donor_x)
        - courant[:, 1][:, None, None] * (center - donor_y)
    )
    return (moved * sea_mask[None]).astype(jnp.bfloat16)


def whole(spectrum, courant, upwind, coupling, sea, owner):
    local_bins = spectrum.shape[0]
    lon_rows = spectrum.shape[1]
    bins_count = lax.axis_size("bins")
    lat_cells = spectrum.shape[2] // bins_count
    masked = spectrum * sea.astype(jnp.bfloat16)[None]
    local_sea = lax.dynamic_slice_in_dim(
        sea, lax.axis_index("bins") * lat_cells, lat_cells, 1
    ).astype(jnp.float32)
    first_bin = lax.axis_index("bins") * local_bins
    my_courant = lax.dynamic_slice_in_dim(courant, first_bin, local_bins, 0)
    my_upwind = lax.dynamic_slice_in_dim(upwind, first_bin, local_bins, 0)
    extended = padded_2(masked, (("pts", 1),), 1)
    extended = jnp.pad(extended.astype(jnp.float32), ((0, 0), (0, 0), (1, 1)))
    moved = advect(extended, sea.astype(jnp.float32), my_courant, my_upwind)
    columns = lax.all_to_all(moved, "bins", split_axis=2, concat_axis=0, tiled=True)
    all_bins = columns.shape[0]
    points = lon_rows * lat_cells
    flat = columns.reshape(all_bins, points)
    energy = jnp.mean(flat.astype(jnp.float32), axis=0)
    coupled = jnp.einsum("bp,bc->pc", flat, coupling, preferred_element_type=jnp.float32)
    weights = local_sea.reshape(points)
    updated = (
        weights[:, None] * (flat.astype(jnp.float32).T + coupled) / (1.0 + energy)[:, None]
    ).astype(jnp.bfloat16)
    owners_count = lax.axis_size("pts")
    capacity = max(2, (2 * points + owners_count - 1) // owners_count)
    target = owner.reshape(points)
    onehot = (target[:, None] == jnp.arange(owners_count, dtype=jnp.int32)[None, :]).astype(
        jnp.int32
    )
    slot_rank = jnp.sum(jnp.cumsum(onehot, axis=0) * onehot, axis=1) - 1
    slot_index = target * capacity + slot_rank
    selector = (
        slot_index[None, :] == jnp.arange(owners_count * capacity, dtype=jnp.int32)[:, None]
    ).astype(jnp.bfloat16)
    outgoing = jnp.dot(selector, updated, preferred_element_type=jnp.float32).astype(jnp.bfloat16)
    outgoing = outgoing.reshape(owners_count, capacity, all_bins)
    received = lax.all_to_all(outgoing, "pts", split_axis=0, concat_axis=0, tiled=True)
    return received.reshape(1, 1, owners_count * capacity, all_bins)


def local(spectrum, courant, upwind, coupling, sea, owner):
    bins_axis, owners_count = lax.axis_size("bins"), lax.axis_size("pts")
    points = owner.shape[2]
    suits = (
        spectrum.shape[2] == bins_axis * LANES
        and points % (2 * LANES) == 0
        and 2 * points == owners_count * LANES
        and bins_axis & (bins_axis - 1) == 0
        and owners_count & (owners_count - 1) == 0
        and bins_axis % 2 == 0
        and spectrum.shape[0] % 8 == 4
        and courant.shape[0] % 144 == 0
        and courant.shape[0] // CHUNKS % 8 == 4
        and points == CHUNKS * LANES
        and bins_axis == CHUNKS
        and owners_count == 8
        and spectrum.shape[1] >= 3
    )
    form = chunked if suits else whole
    return form(spectrum, courant, upwind, coupling, sea, owner)


def solution(mesh):
    placed = (P("bins", "pts", None), P(), P(), P(), P("pts", None), P("pts", "bins", None, None))
    return jax.shard_map(
        local, mesh=mesh, in_specs=placed, out_specs=P("pts", "bins", None, None), check_vma=False
    )
```

```python
import functools

import jax
import jax.numpy as jnp
from jax import lax
from jax.experimental import pallas as pl
from jax.experimental.pallas import tpu as pltpu
from jax.sharding import PartitionSpec as P

F32 = jnp.float32
BF16 = jnp.bfloat16
I32 = jnp.int32
LANES = 128
CHUNKS = 4
MAIN = ((0, 1), (2,))
NT = (((1,), (1,)), ((), ()))


def round_up(size, unit):
    return -(-size // unit) * unit


def iota(shape, axis):
    return lax.broadcasted_iota(I32, shape, axis)


def dot_nt(lhs, rhs):
    return lax.dot_general(lhs, rhs, NT, preferred_element_type=F32)


def upwind_row(at, speed, side, before, center, after, sea_row):
    lats = center.shape[1]
    lane = iota(center.shape, 1)
    wide = lats // LANES
    cx, cy = [jnp.concatenate([speed[k, at, :]] * wide, axis=1) for k in range(2)]
    ux, uy = [jnp.concatenate([side[k, at, :]] * wide, axis=1) for k in range(2)]
    donor_x = jnp.where(ux == 0, before, after).astype(F32)
    left = jnp.where(lane == 0, 0, pltpu.roll(center, 1, 1))
    right = jnp.where(lane == lats - 1, 0, pltpu.roll(center, lats - 1, 1))
    donor_y = jnp.where(uy == 0, left, right).astype(F32)
    center = center.astype(F32)
    value = center - cx * (center - donor_x) - cy * (center - donor_y)
    return (value * sea_row).astype(BF16)


def inner_kernel(planes, near, speed, side, sea, moved):
    lon_rows, rows, _ = planes.shape
    top = lon_rows - 1
    even = lax.axis_index("pts") % 2 == 0
    sea_f = sea[...].astype(F32)
    sea_b = sea_f.astype(BF16)

    def tile(at, close):
        masked = [planes[l, at, :] * sea_b[l : l + 1, :] for l in range(lon_rows)]
        for l in range(1, top):
            moved[l - 1, at, :] = upwind_row(
                at, speed, side, masked[l - 1], masked[l], masked[l + 1], sea_f[l : l + 1, :]
            )
        center = jnp.where(even, masked[top], masked[0])
        below = jnp.where(even, masked[top - 1], close)
        above = jnp.where(even, close, masked[1])
        weight = jnp.where(even, sea_f[top : top + 1, :], sea_f[0:1, :])
        moved[top - 1, at, :] = upwind_row(at, speed, side, below, center, above, weight)

    over_rows(tile, rows, near)


def over_rows(tile, rows, halo):
    held = halo.shape[0]
    full = held // 16 * 16

    def step(index, carry):
        at = pl.ds(pl.multiple_of(index * 16, 16), 16)
        tile(at, halo[at, :])
        return carry

    lax.fori_loop(0, full // 16, step, 0, unroll=5)
    if full < rows:
        spare = jnp.zeros((rows - held, halo.shape[1]), F32)
        end = jnp.concatenate([halo[full:, :].astype(F32), spare], axis=0).astype(BF16)
        tile(pl.ds(full, 16), end)


def order_kernel(bins_axis, owners_count, width, slots, *refs):
    inner, sea = refs[:2]
    owner = refs[2 : 2 + bins_axis]
    part, far_order, meta, order = refs[2 + bins_axis :]
    lon_rows, rows = inner.shape[0] + 1, inner.shape[1]
    points = lon_rows * LANES
    me = lax.axis_index("bins")
    me_pts = lax.axis_index("pts")
    even = me_pts % 2 == 0
    last = (lon_rows - 1) * LANES
    near_at = pl.ds(pl.multiple_of(jnp.where(even, last, 0), LANES), LANES)
    far_at = pl.ds(pl.multiple_of(jnp.where(even, 0, last), LANES), LANES)
    owners_id = iota((owners_count, points), 0)
    hot = [(owner[m][...] == owners_id).astype(F32) for m in range(bins_axis)]
    earlier = (iota((points, points), 0) < iota((points, points), 1)).astype(F32).astype(BF16)
    before = jnp.dot(
        jnp.concatenate(hot, axis=0).astype(BF16), earlier, preferred_element_type=F32
    )
    main = (CHUNKS - 1) * width
    place_id = iota(order.shape, 0)
    none = [jnp.zeros((1, points), F32)]
    for m in range(bins_axis):
        own = owner[m][...]
        count = jnp.sum(hot[m], axis=1, keepdims=True)
        offset = jnp.sum(jnp.where(owners_id < own, count, 0.0), axis=0, keepdims=True)
        mine = before[m * owners_count : (m + 1) * owners_count, :]
        rank = jnp.sum(hot[m] * mine, axis=0, keepdims=True)
        key, first = (offset + rank).astype(I32), offset.astype(I32)
        quarter = key & (CHUNKS - 1)
        slot = (key - first - ((quarter - first) & (CHUNKS - 1))) // CHUNKS
        towards = own ^ me_pts
        block = me ^ m
        group = (towards & (CHUNKS - 1)) ^ block
        spread = main + towards // CHUNKS * LANES + group * slots + slot
        place = jnp.where(quarter < CHUNKS - 1, quarter * width + key // CHUNKS, spread)
        order[...] = (place_id == place).astype(F32).astype(BF16)
        far_order[m] = order[:, far_at]
        at = pl.ds(pl.multiple_of(block * LANES, LANES), LANES)
        cells = jnp.concatenate([inner[l, :, at] for l in range(lon_rows - 1)], axis=1)
        columns = jnp.concatenate([order[:, LANES:last], order[:, near_at]], axis=1)
        part[m] = dot_nt(cells, columns).astype(BF16)
        weight = jnp.concatenate([sea[l : l + 1, at].astype(F32) for l in range(lon_rows)], axis=1)
        facts = jnp.concatenate(none * 4 + [weight, rank] + none * 10, axis=0).astype(BF16)
        end = slice(rows - 16, rows)
        spare = part[m, end, main:].astype(F32) + dot_nt(facts, order[main:, :])
        part[m, end, main:] = spare.astype(BF16)
        if m == 0:
            facts = [slot.astype(F32), towards.astype(F32), rank, weight] + none * 4
            meta[...] = dot_nt(jnp.concatenate(facts, axis=0).astype(BF16), order[:main, :])


def pack_kernel(rows_out, bins_axis, width, pairs, *refs):
    planes, far, speed, side, sea, part, far_order = refs[:7]
    chunks, moved = refs[7:-1], refs[-1]
    direct = chunks[len(MAIN) * bins_axis :]
    lon_rows, rows, _ = planes.shape
    top = lon_rows - 1
    me = lax.axis_index("bins")
    even = lax.axis_index("pts") % 2 == 0
    center_row, next_row = jnp.where(even, 0, top), jnp.where(even, 1, top - 1)
    sea_f = sea[...].astype(F32)
    center_sea = jnp.where(even, sea_f[0:1, :], sea_f[top : top + 1, :])
    next_sea = jnp.where(even, sea_f[1:2, :], sea_f[top - 1 : top, :]).astype(BF16)

    def tile(at, distant):
        center = planes[center_row, at, :] * center_sea.astype(BF16)
        beside = planes[next_row, at, :] * next_sea
        below, above = jnp.where(even, distant, beside), jnp.where(even, beside, distant)
        moved[at, :] = upwind_row(at, speed, side, below, center, above, center_sea)

    over_rows(tile, rows, far)
    spread = []
    for m in range(bins_axis):
        at = pl.ds(pl.multiple_of((me ^ m) * LANES, LANES), LANES)
        ordered = dot_nt(moved[:, at], far_order[m]) + part[m].astype(F32)
        ordered = ordered[:rows_out]
        ordered = jnp.where((me & 1) == 1, pltpu.roll(ordered, 4, 0), ordered).astype(BF16)
        for c, quarters in enumerate(MAIN):
            at = slice(quarters[0] * width, (quarters[-1] + 1) * width)
            chunks[c * bins_axis + m][...] = ordered[:, at]
        spread.append(ordered[:, (CHUNKS - 1) * width :])
    group = iota((rows_out, LANES), 1) // (LANES // CHUNKS)
    for x in range(2 * pairs):
        at = slice(x // CHUNKS * LANES, (x // CHUNKS + 1) * LANES)
        mixed = spread[0][:, at]
        for m in range(1, bins_axis):
            mixed = jnp.where(group == ((me ^ m) ^ (x % CHUNKS)), spread[m][:, at], mixed)
        direct[x // 2][x % 2, 0] = mixed


def regroup_kernel(bins_axis, pairs, *refs):
    came, swapped, outs = refs[:pairs], refs[pairs], refs[pairs + 1 :]
    me = lax.axis_index("bins")
    sources = [swapped[x // 2, 0] if x % 2 else came[x // 2][0, 0] for x in range(2 * pairs)]
    group = iota(sources[0].shape, 1) // (LANES // CHUNKS)
    for m in range(bins_axis):
        for u in range(2 * pairs // CHUNKS):
            mixed = sources[u * CHUNKS]
            for k in range(1, CHUNKS):
                mixed = jnp.where(group == ((me ^ m) ^ k), sources[u * CHUNKS + k], mixed)
            outs[m][:, u * LANES : (u + 1) * LANES] = mixed


def transpose_kernel(coupling, out):
    bins = coupling.shape[0]
    for start in range(0, bins, 256):
        size = min(256, bins - start)
        eye = (iota((size, size), 0) == iota((size, size), 1)).astype(F32).astype(BF16)
        out[start : start + size, :] = dot_nt(eye, coupling[:, start : start + size]).astype(BF16)


def lane_groups(blocks, shift):
    group = iota(blocks[0].shape, 1) // (LANES // CHUNKS)
    mixed = blocks[shift]
    for q in range(1, CHUNKS):
        mixed = jnp.where(group == q, blocks[q ^ shift], mixed)
    return mixed


def couple_kernel(quarters, bins_axis, local_bins, slots, pairs, *refs):
    blocks = refs[:bins_axis]
    weights, meta = refs[bins_axis : bins_axis + 2]
    values, outs = refs[-1], refs[-1 - pairs : -1]
    rows, columns = blocks[0].shape
    all_bins = values.shape[0]
    held = all_bins // CHUNKS
    tall = outs[0].shape[2]
    at_owner = quarters[0] == CHUNKS - 1
    me = lax.axis_index("bins")
    values[...] = jnp.zeros_like(values)
    row = iota((rows, columns), 0)
    for m in range(bins_axis):
        block = me ^ m
        at = pl.ds(pl.multiple_of(block * local_bins - 4 * (block & 1), 8), rows)
        arrived = blocks[m][...].astype(F32)
        if at_owner:
            lead = 4 * (block & 1)
            arrived = jnp.where((row >= lead) & (row < local_bins + lead), arrived, 0.0)
        values[at, :] += arrived
    flat = values[...].astype(BF16)
    energy = jnp.sum(values[...], axis=0, keepdims=True) / all_bins
    if at_owner:
        own = blocks[0][...].astype(F32)
        spare = jnp.where((me & 1) == 1, own[0:4, :], own[local_bins : local_bins + 4, :])
        weight, rank = spare[0:1, :], spare[1:2, :]
        lane = iota((1, columns), 1)
        slot = lane & (slots - 1)
        low = ((lane // slots) & (CHUNKS - 1)) ^ me
        towards = lane // LANES * CHUNKS + low
    else:
        facts = meta[:, quarters[0] * LANES : (quarters[-1] + 1) * LANES]
        slot, towards = facts[0:1, :].astype(I32), facts[1:2, :].astype(I32)
        rank, weight = facts[2:3, :], facts[3:4, :]
    scale = weight / (1.0 + energy)
    step = all_bins // 9
    for start in range(0, all_bins, step):
        at = slice(start, start + step)
        coupled = jnp.dot(weights[at, :], flat, preferred_element_type=F32)
        values[at, :] = (values[at, :] + coupled) * scale
    width = columns // len(quarters)
    slot_id = iota((2 * pairs * slots, width), 0)
    row_id = iota((tall, width), 0)
    for n, quarter in enumerate(quarters):
        cut = slice(n * width, (n + 1) * width)
        sent = []
        for v in range(CHUNKS):
            start = (v ^ quarter) * held
            lead = start % 8
            updated = values[start - lead : start - lead + tall, cut]
            if lead:
                updated = pltpu.roll(updated, tall - lead, 0)
            updated = jnp.where(row_id < held, updated, jnp.where(row_id == held, rank[:, cut], 0.0))
            group = (towards[:, cut] & (CHUNKS - 1)) ^ v
            column = towards[:, cut] // CHUNKS * LANES + group * slots + slot[:, cut]
            route = (slot_id == column).astype(F32).astype(BF16)
            sent.append(dot_nt(updated.astype(BF16), route).astype(BF16))
        for x in range(2 * pairs):
            at = slice(x // CHUNKS * LANES, (x // CHUNKS + 1) * LANES)
            outs[x // 2][x % 2, n] = lane_groups([rows_v[:, at] for rows_v in sent], x % CHUNKS)


def place_kernel(held, sources, picks, *refs):
    out, staged, sems = refs[-3:]
    me = lax.axis_index("pts")
    tall = refs[0].shape[-2]
    slot_id = iota((LANES, LANES), 0)
    copies = []
    for number, x in enumerate(sources):
        blocks = [refs[n][index] for n, index in picks[number]]
        pieces = []
        for g in range(CHUNKS):
            lhs = lane_groups(blocks, (x % CHUNKS) ^ g)
            rank = lhs[tall - 8 :, :].astype(F32)[held - tall + 8 : held - tall + 9, :].astype(I32)
            spots = (slot_id == rank).astype(F32).astype(BF16)
            pieces.append(dot_nt(lhs, spots)[:held])
        staged[number] = jnp.concatenate(pieces, axis=0).astype(BF16)
        at = pl.ds(pl.multiple_of((me ^ x) * LANES, LANES), LANES)
        copy = pltpu.make_async_copy(staged.at[number], out.at[:, at], sems.at[number])
        copy.start()
        copies.append(copy)
    for copy in copies:
        copy.wait()


def place(out, owners_count, all_bins, sources):
    arrays, picks = [], []
    for x in sorted(sources):
        mine = []
        for array, index in sources[x]:
            known = [n for n, a in enumerate(arrays) if a is array]
            if not known:
                arrays.append(array)
                known = [len(arrays) - 1]
            mine.append((known[0], index))
        picks.append(tuple(mine))
    held = [] if out is None else [out]
    return pl.pallas_call(
        functools.partial(place_kernel, all_bins // CHUNKS, tuple(sorted(sources)), tuple(picks)),
        out_shape=jax.ShapeDtypeStruct((all_bins, owners_count * LANES), BF16),
        in_specs=vmem(len(arrays)) + [pl.BlockSpec(memory_space=pl.ANY)] * len(held),
        out_specs=pl.BlockSpec(memory_space=pl.ANY),
        scratch_shapes=[
            pltpu.VMEM((len(sources), all_bins, LANES), BF16),
            pltpu.SemaphoreType.DMA((len(sources),)),
        ],
        input_output_aliases={len(arrays): 0} if held else {},
        compiler_params=params(16),
        cost_estimate=cost(1, 1),
        name="place",
    )(*arrays, *held)


def gate_kernel(array, *refs):
    refs[-1][...] = array[...]


def gate(array, *after):
    return pl.pallas_call(
        gate_kernel,
        out_shape=jax.ShapeDtypeStruct(array.shape, array.dtype),
        in_specs=vmem(1 + len(after)),
        out_specs=vmem(1)[0],
        compiler_params=params(16),
        cost_estimate=cost(1, 1),
        name="gate",
    )(array, *after)


def stack_kernel(count, *refs):
    for t in range(count):
        refs[-1][t] = refs[t][1]


def stack(pairs, *after):
    return pl.pallas_call(
        functools.partial(stack_kernel, len(pairs)),
        out_shape=jax.ShapeDtypeStruct((len(pairs),) + pairs[0].shape[1:], pairs[0].dtype),
        in_specs=vmem(len(pairs) + len(after)),
        out_specs=vmem(1)[0],
        compiler_params=params(8),
        cost_estimate=cost(1, 1),
        name="stack",
    )(*pairs, *after)


def params(mib):
    return pltpu.CompilerParams(vmem_limit_bytes=mib << 20)


def vmem(count):
    return [pl.BlockSpec(memory_space=pltpu.VMEM)] * count


def cost(flops, bytes_accessed):
    del bytes_accessed
    return pl.CostEstimate(flops=int(flops), bytes_accessed=1, transcendentals=0)


def exchange(array, axis, offset):
    return lax.ppermute(array, axis, [(i, i ^ offset) for i in range(lax.axis_size(axis))])


def chunked(spectrum, courant, upwind, coupling, sea, owner):
    local_bins, lon_rows, lats = spectrum.shape
    all_bins = courant.shape[0]
    bins_axis = lax.axis_size("bins")
    owners_count = lax.axis_size("pts")
    points = lon_rows * LANES
    width = points // CHUNKS
    slots = 2 * points // owners_count // CHUNKS
    tall = round_up(local_bins, 16)
    rows = round_up(local_bins + 1, 8)
    order_columns = (CHUNKS - 1) * width + owners_count * slots
    pairs = owners_count // 2
    quarter_rows = round_up(all_bins // CHUNKS + 1, 8)
    first_bin = lax.axis_index("bins") * local_bins

    planes = jnp.pad(jnp.transpose(spectrum, (1, 0, 2)), ((0, 0), (0, tall - local_bins), (0, 0)))
    even = lax.axis_index("pts") % 2 == 0
    rows_at = [jnp.where(even, 0, lon_rows - 1), jnp.where(even, lon_rows - 1, 0)]
    edges = [
        lax.dynamic_index_in_dim(planes, r, 0, False)[:local_bins]
        * lax.dynamic_index_in_dim(sea, r, 0, False).astype(BF16)[None]
        for r in rows_at
    ]
    between = [(i, i + 1) for i in range(1, owners_count - 1, 2)]
    far = lax.ppermute(edges[0], "pts", between + [(b, a) for a, b in between])
    near = exchange(edges[1], "pts", 1)
    own = owner.reshape(1, points)
    owners = [own, *reversed([exchange(own, "bins", m) for m in range(bins_axis - 1, 0, -1)])]

    def wide(table, dtype):
        mine = lax.dynamic_slice_in_dim(table.T, first_bin, local_bins, 1).astype(dtype)
        mine = jnp.pad(mine, ((0, 0), (0, tall - local_bins)))
        return jnp.broadcast_to(mine[:, :, None], (2, tall, LANES))

    speed, side = wide(courant, F32), wide(upwind, BF16)

    weights = pl.pallas_call(
        transpose_kernel,
        out_shape=jax.ShapeDtypeStruct(coupling.shape, BF16),
        in_specs=vmem(1),
        out_specs=vmem(1)[0],
        compiler_params=params(16),
        cost_estimate=cost(1, 1),
        name="transpose",
    )(coupling)

    inner = pl.pallas_call(
        inner_kernel,
        out_shape=jax.ShapeDtypeStruct((lon_rows - 1, tall, lats), BF16),
        in_specs=vmem(5),
        out_specs=vmem(1)[0],
        compiler_params=params(16),
        cost_estimate=cost(1, 1),
        name="inner",
    )(planes, near, speed, side, sea)
    part, far_order, meta = pl.pallas_call(
        functools.partial(order_kernel, bins_axis, owners_count, width, slots),
        out_shape=[
            jax.ShapeDtypeStruct((bins_axis, tall, order_columns), BF16),
            jax.ShapeDtypeStruct((bins_axis, order_columns, LANES), BF16),
            jax.ShapeDtypeStruct((8, (CHUNKS - 1) * width), F32),
        ],
        in_specs=vmem(2 + bins_axis),
        out_specs=vmem(3),
        scratch_shapes=[pltpu.VMEM((order_columns, points), BF16)],
        compiler_params=params(16),
        cost_estimate=cost(1, 1),
        name="order",
    )(inner, sea, *owners)
    packed = pl.pallas_call(
        functools.partial(pack_kernel, rows, bins_axis, width, pairs),
        out_shape=[
            jax.ShapeDtypeStruct((rows, len(quarters) * width), BF16)
            for quarters in MAIN
            for _ in range(bins_axis)
        ]
        + [jax.ShapeDtypeStruct((2, 1, rows, LANES), BF16)] * pairs,
        in_specs=vmem(7),
        out_specs=vmem(len(MAIN) * bins_axis + pairs),
        scratch_shapes=[pltpu.VMEM((tall, lats), BF16)],
        compiler_params=params(16),
        cost_estimate=cost(1, 1),
        name="pack",
    )(planes, far, speed, side, sea, part, far_order)

    def couple(quarters, blocks, ready):
        shape = (2, len(quarters), quarter_rows, LANES)
        return pl.pallas_call(
            functools.partial(couple_kernel, quarters, bins_axis, local_bins, slots, pairs),
            out_shape=[jax.ShapeDtypeStruct(shape, BF16)] * pairs,
            in_specs=vmem(len(blocks) + 2 + len(ready)),
            out_specs=vmem(pairs),
            scratch_shapes=[pltpu.VMEM((all_bins, blocks[0].shape[1]), F32)],
            compiler_params=params(16),
            cost_estimate=cost((3e9, 1, 3e10, 3e10)[quarters[0]], 1),
            name="couple",
        )(*blocks, weights, meta, *ready)

    def over_bins(blocks):
        return [blocks[0]] + [exchange(blocks[m], "bins", m) for m in range(1, bins_axis)]

    def over_pts(pays):
        sent = {0: pays[0]}
        for t in range(pairs - 1, 0, -1):
            sent[t] = exchange(pays[t], "pts", 2 * t)
        return [sent[t] for t in range(pairs)]

    def held_back(blocks, *after):
        return [blocks[0]] + [gate(b, *after) for b in blocks[1:]]

    early, late = packed[:bins_axis], packed[bins_axis : 2 * bins_axis]
    direct = packed[2 * bins_axis :]
    first = over_bins(early)
    direct = over_pts(direct)
    regrouped = pl.pallas_call(
        functools.partial(regroup_kernel, bins_axis, pairs),
        out_shape=[jax.ShapeDtypeStruct((rows, owners_count * slots), BF16)] * bins_axis,
        in_specs=vmem(pairs + 1),
        out_specs=vmem(bins_axis),
        compiler_params=params(16),
        cost_estimate=cost(1, 1),
        name="regroup",
    )(*direct, exchange(stack(direct, first[1], first[2]), "pts", 1))
    late = [late[0], gate(late[1], first[1], weights), *[gate(b, *first[1:]) for b in late[2:]]]
    second = over_bins(late)
    came = [over_pts(couple(MAIN[0], first, late[1:]))]
    regrouped = [
        regrouped[0],
        gate(regrouped[1], *second[1:], came[0][0], came[0][pairs - 1]),
        *[gate(b, *second[1:], came[0][0]) for b in regrouped[2:]],
    ]
    third = over_bins(regrouped)
    came.append(over_pts(couple(MAIN[1], second, regrouped[2:])))
    last = came[-1]
    here = couple((CHUNKS - 1,), third, [])
    swapped = [exchange(stack(came[0], last[0]), "pts", 1), exchange(stack(last, here[0]), "pts", 1)]

    shape = (owners_count, all_bins)
    cuts = [(c, n) for c, quarters in enumerate(MAIN) for n in range(len(quarters))]
    near_side = {
        2 * t: [(came[c][t], (0, n)) for c, n in cuts] + [(here[t], (0, 0))] for t in range(pairs)
    }
    far_side = {
        2 * t + 1: [(swapped[c], (t, n)) for c, n in cuts] + [(here[t], (1, 0))] for t in range(pairs)
    }
    placed = place(place(None, *shape, near_side), *shape, far_side)
    return jnp.transpose(placed).reshape(1, 1, owners_count * LANES, all_bins)


def padded_2(block, sides, width):
    for axis, dim in sides:
        count = lax.axis_size(axis)
        forward = [(i, i + 1) for i in range(count - 1)]
        backward = [(target, source) for source, target in forward]
        low = lax.ppermute(
            lax.slice_in_dim(block, block.shape[dim] - width, None, axis=dim), axis, forward
        )
        high = lax.ppermute(lax.slice_in_dim(block, 0, width, axis=dim), axis, backward)
        block = jnp.concatenate([low, block, high], axis=dim)
    return block


def advect(padded, sea_mask, courant, upwind):
    center = padded[:, 1:-1, 1:-1]
    donor_x = jnp.where(upwind[:, 0][:, None, None] == 0, padded[:, :-2, 1:-1], padded[:, 2:, 1:-1])
    donor_y = jnp.where(upwind[:, 1][:, None, None] == 0, padded[:, 1:-1, :-2], padded[:, 1:-1, 2:])
    moved = (
        center
        - courant[:, 0][:, None, None] * (center - donor_x)
        - courant[:, 1][:, None, None] * (center - donor_y)
    )
    return (moved * sea_mask[None]).astype(jnp.bfloat16)


def whole(spectrum, courant, upwind, coupling, sea, owner):
    local_bins = spectrum.shape[0]
    lon_rows = spectrum.shape[1]
    bins_count = lax.axis_size("bins")
    lat_cells = spectrum.shape[2] // bins_count
    masked = spectrum * sea.astype(jnp.bfloat16)[None]
    local_sea = lax.dynamic_slice_in_dim(
        sea, lax.axis_index("bins") * lat_cells, lat_cells, 1
    ).astype(jnp.float32)
    first_bin = lax.axis_index("bins") * local_bins
    my_courant = lax.dynamic_slice_in_dim(courant, first_bin, local_bins, 0)
    my_upwind = lax.dynamic_slice_in_dim(upwind, first_bin, local_bins, 0)
    extended = padded_2(masked, (("pts", 1),), 1)
    extended = jnp.pad(extended.astype(jnp.float32), ((0, 0), (0, 0), (1, 1)))
    moved = advect(extended, sea.astype(jnp.float32), my_courant, my_upwind)
    columns = lax.all_to_all(moved, "bins", split_axis=2, concat_axis=0, tiled=True)
    all_bins = columns.shape[0]
    points = lon_rows * lat_cells
    flat = columns.reshape(all_bins, points)
    energy = jnp.mean(flat.astype(jnp.float32), axis=0)
    coupled = jnp.einsum("bp,bc->pc", flat, coupling, preferred_element_type=jnp.float32)
    weights = local_sea.reshape(points)
    updated = (
        weights[:, None] * (flat.astype(jnp.float32).T + coupled) / (1.0 + energy)[:, None]
    ).astype(jnp.bfloat16)
    owners_count = lax.axis_size("pts")
    capacity = max(2, (2 * points + owners_count - 1) // owners_count)
    target = owner.reshape(points)
    onehot = (target[:, None] == jnp.arange(owners_count, dtype=jnp.int32)[None, :]).astype(
        jnp.int32
    )
    slot_rank = jnp.sum(jnp.cumsum(onehot, axis=0) * onehot, axis=1) - 1
    slot_index = target * capacity + slot_rank
    selector = (
        slot_index[None, :] == jnp.arange(owners_count * capacity, dtype=jnp.int32)[:, None]
    ).astype(jnp.bfloat16)
    outgoing = jnp.dot(selector, updated, preferred_element_type=jnp.float32).astype(jnp.bfloat16)
    outgoing = outgoing.reshape(owners_count, capacity, all_bins)
    received = lax.all_to_all(outgoing, "pts", split_axis=0, concat_axis=0, tiled=True)
    return received.reshape(1, 1, owners_count * capacity, all_bins)


def local(spectrum, courant, upwind, coupling, sea, owner):
    bins_axis, owners_count = lax.axis_size("bins"), lax.axis_size("pts")
    points = owner.shape[2]
    suits = (
        spectrum.shape[2] == bins_axis * LANES
        and points % (2 * LANES) == 0
        and 2 * points == owners_count * LANES
        and bins_axis & (bins_axis - 1) == 0
        and owners_count & (owners_count - 1) == 0
        and bins_axis % 2 == 0
        and spectrum.shape[0] % 16 == 4
        and courant.shape[0] % 144 == 0
        and courant.shape[0] // CHUNKS % 8 == 4
        and points == CHUNKS * LANES
        and bins_axis == CHUNKS
        and owners_count == 8
        and spectrum.shape[1] >= 3
    )
    form = chunked if suits else whole
    return form(spectrum, courant, upwind, coupling, sea, owner)


def solution(mesh):
    placed = (P("bins", "pts", None), P(), P(), P(), P("pts", None), P("pts", "bins", None, None))
    return jax.shard_map(
        local, mesh=mesh, in_specs=placed, out_specs=P("pts", "bins", None, None), check_vma=False
    )
```

```python
import functools

import jax
import jax.numpy as jnp
from jax import lax
from jax.experimental import pallas as pl
from jax.experimental.pallas import tpu as pltpu
from jax.sharding import PartitionSpec as P

F32 = jnp.float32
BF16 = jnp.bfloat16
I32 = jnp.int32
LANES = 128
CHUNKS = 4
MAIN = ((0, 1), (2,))
NT = (((1,), (1,)), ((), ()))


def round_up(size, unit):
    return -(-size // unit) * unit


def iota(shape, axis):
    return lax.broadcasted_iota(I32, shape, axis)


def dot_nt(lhs, rhs):
    return lax.dot_general(lhs, rhs, NT, preferred_element_type=F32)


def upwind_row(at, speed, side, before, center, after, sea_row):
    lats = center.shape[1]
    lane = iota(center.shape, 1)
    wide = lats // LANES
    cx, cy = [jnp.concatenate([speed[k, at, :]] * wide, axis=1) for k in range(2)]
    ux, uy = [jnp.concatenate([side[k, at, :]] * wide, axis=1) for k in range(2)]
    donor_x = jnp.where(ux == 0, before, after).astype(F32)
    left = jnp.where(lane == 0, 0, pltpu.roll(center, 1, 1))
    right = jnp.where(lane == lats - 1, 0, pltpu.roll(center, lats - 1, 1))
    donor_y = jnp.where(uy == 0, left, right).astype(F32)
    center = center.astype(F32)
    value = center - cx * (center - donor_x) - cy * (center - donor_y)
    return (value * sea_row).astype(BF16)


def inner_kernel(planes, near, speed, side, sea, moved):
    lon_rows, rows, _ = planes.shape
    top = lon_rows - 1
    even = lax.axis_index("pts") % 2 == 0
    sea_f = sea[...].astype(F32)
    sea_b = sea_f.astype(BF16)

    def tile(at, close):
        masked = [planes[l, at, :] * sea_b[l : l + 1, :] for l in range(lon_rows)]
        for l in range(1, top):
            moved[l - 1, at, :] = upwind_row(
                at, speed, side, masked[l - 1], masked[l], masked[l + 1], sea_f[l : l + 1, :]
            )
        center = jnp.where(even, masked[top], masked[0])
        below = jnp.where(even, masked[top - 1], close)
        above = jnp.where(even, close, masked[1])
        weight = jnp.where(even, sea_f[top : top + 1, :], sea_f[0:1, :])
        moved[top - 1, at, :] = upwind_row(at, speed, side, below, center, above, weight)

    over_rows(tile, rows, near)


def over_rows(tile, rows, halo):
    held = halo.shape[0]
    full = held // 16 * 16

    def step(index, carry):
        at = pl.ds(pl.multiple_of(index * 16, 16), 16)
        tile(at, halo[at, :])
        return carry

    lax.fori_loop(0, full // 16, step, 0, unroll=5)
    if full < rows:
        spare = jnp.zeros((rows - held, halo.shape[1]), F32)
        end = jnp.concatenate([halo[full:, :].astype(F32), spare], axis=0).astype(BF16)
        tile(pl.ds(full, 16), end)


def order_kernel(blocks, owners_count, width, slots, *refs):
    inner, sea = refs[:2]
    owner = refs[2 : 2 + len(blocks)]
    part, far_order = refs[2 + len(blocks) : 4 + len(blocks)]
    order = refs[-1]
    lon_rows, rows = inner.shape[0] + 1, inner.shape[1]
    points = lon_rows * LANES
    me = lax.axis_index("bins")
    me_pts = lax.axis_index("pts")
    even = me_pts % 2 == 0
    last = (lon_rows - 1) * LANES
    near_at = pl.ds(pl.multiple_of(jnp.where(even, last, 0), LANES), LANES)
    far_at = pl.ds(pl.multiple_of(jnp.where(even, 0, last), LANES), LANES)
    owners_id = iota((owners_count, points), 0)
    hot = [(owner[m][...] == owners_id).astype(F32) for m in range(len(blocks))]
    earlier = (iota((points, points), 0) < iota((points, points), 1)).astype(F32).astype(BF16)
    before = jnp.dot(
        jnp.concatenate(hot, axis=0).astype(BF16), earlier, preferred_element_type=F32
    )
    main = (CHUNKS - 1) * width
    place_id = iota(order.shape, 0)
    none = [jnp.zeros((1, points), F32)]
    for m, offset_of in enumerate(blocks):
        own = owner[m][...]
        count = jnp.sum(hot[m], axis=1, keepdims=True)
        offset = jnp.sum(jnp.where(owners_id < own, count, 0.0), axis=0, keepdims=True)
        mine = before[m * owners_count : (m + 1) * owners_count, :]
        rank = jnp.sum(hot[m] * mine, axis=0, keepdims=True)
        key, first = (offset + rank).astype(I32), offset.astype(I32)
        quarter = key & (CHUNKS - 1)
        slot = (key - first - ((quarter - first) & (CHUNKS - 1))) // CHUNKS
        towards = own ^ me_pts
        block = me ^ offset_of
        group = (towards & (CHUNKS - 1)) ^ block
        spread = main + towards // CHUNKS * LANES + group * slots + slot
        place = jnp.where(quarter < CHUNKS - 1, quarter * width + key // CHUNKS, spread)
        order[...] = (place_id == place).astype(F32).astype(BF16)
        far_order[m] = order[:, far_at]
        at = pl.ds(pl.multiple_of(block * LANES, LANES), LANES)
        cells = jnp.concatenate([inner[l, :, at] for l in range(lon_rows - 1)], axis=1)
        columns = jnp.concatenate([order[:, LANES:last], order[:, near_at]], axis=1)
        part[m] = dot_nt(cells, columns).astype(BF16)
        weight = jnp.concatenate([sea[l : l + 1, at].astype(F32) for l in range(lon_rows)], axis=1)
        facts = jnp.concatenate(none * 4 + [weight, rank] + none * 10, axis=0).astype(BF16)
        end = slice(rows - 16, rows)
        spare = part[m, end, main:].astype(F32) + dot_nt(facts, order[main:, :])
        part[m, end, main:] = spare.astype(BF16)
        if offset_of == 0:
            facts = [slot.astype(F32), towards.astype(F32), rank, weight] + none * 4
            refs[-2][...] = dot_nt(jnp.concatenate(facts, axis=0).astype(BF16), order[:main, :])


def pack_kernel(rows_out, bins_axis, width, pairs, *refs):
    planes, far, speed, side, sea = refs[:5]
    parts, far_orders = refs[5:7], refs[7:9]
    chunks, moved = refs[9:-1], refs[-1]
    direct = chunks[len(MAIN) * bins_axis :]
    lon_rows, rows, _ = planes.shape
    top = lon_rows - 1
    me = lax.axis_index("bins")
    even = lax.axis_index("pts") % 2 == 0
    center_row, next_row = jnp.where(even, 0, top), jnp.where(even, 1, top - 1)
    sea_f = sea[...].astype(F32)
    center_sea = jnp.where(even, sea_f[0:1, :], sea_f[top : top + 1, :])
    next_sea = jnp.where(even, sea_f[1:2, :], sea_f[top - 1 : top, :]).astype(BF16)

    def tile(at, distant):
        center = planes[center_row, at, :] * center_sea.astype(BF16)
        beside = planes[next_row, at, :] * next_sea
        below, above = jnp.where(even, distant, beside), jnp.where(even, beside, distant)
        moved[at, :] = upwind_row(at, speed, side, below, center, above, center_sea)

    over_rows(tile, rows, far)
    spread = []
    for m in range(bins_axis):
        at = pl.ds(pl.multiple_of((me ^ m) * LANES, LANES), LANES)
        late = m == bins_axis - 1
        index = 0 if late else m
        ordered = dot_nt(moved[:, at], far_orders[late][index]) + parts[late][index].astype(F32)
        ordered = ordered[:rows_out]
        ordered = jnp.where((me & 1) == 1, pltpu.roll(ordered, 4, 0), ordered).astype(BF16)
        for c, quarters in enumerate(MAIN):
            at = slice(quarters[0] * width, (quarters[-1] + 1) * width)
            chunks[c * bins_axis + m][...] = ordered[:, at]
        spread.append(ordered[:, (CHUNKS - 1) * width :])
    group = iota((rows_out, LANES), 1) // (LANES // CHUNKS)
    for x in range(2 * pairs):
        at = slice(x // CHUNKS * LANES, (x // CHUNKS + 1) * LANES)
        mixed = spread[0][:, at]
        for m in range(1, bins_axis):
            mixed = jnp.where(group == ((me ^ m) ^ (x % CHUNKS)), spread[m][:, at], mixed)
        direct[x // 2][x % 2, 0] = mixed


def regroup_kernel(bins_axis, pairs, *refs):
    came, swapped, outs = refs[:pairs], refs[pairs], refs[pairs + 1 :]
    me = lax.axis_index("bins")
    sources = [swapped[x // 2, 0] if x % 2 else came[x // 2][0, 0] for x in range(2 * pairs)]
    group = iota(sources[0].shape, 1) // (LANES // CHUNKS)
    for m in range(bins_axis):
        for u in range(2 * pairs // CHUNKS):
            mixed = sources[u * CHUNKS]
            for k in range(1, CHUNKS):
                mixed = jnp.where(group == ((me ^ m) ^ k), sources[u * CHUNKS + k], mixed)
            outs[m][:, u * LANES : (u + 1) * LANES] = mixed


def transpose_kernel(coupling, out):
    bins = coupling.shape[0]
    for start in range(0, bins, 256):
        size = min(256, bins - start)
        eye = (iota((size, size), 0) == iota((size, size), 1)).astype(F32).astype(BF16)
        out[start : start + size, :] = dot_nt(eye, coupling[:, start : start + size]).astype(BF16)


def lane_groups(blocks, shift):
    group = iota(blocks[0].shape, 1) // (LANES // CHUNKS)
    mixed = blocks[shift]
    for q in range(1, CHUNKS):
        mixed = jnp.where(group == q, blocks[q ^ shift], mixed)
    return mixed


def couple_kernel(quarters, bins_axis, local_bins, slots, pairs, *refs):
    blocks = refs[:bins_axis]
    weights, meta = refs[bins_axis : bins_axis + 2]
    values, outs = refs[-1], refs[-1 - pairs : -1]
    rows, columns = blocks[0].shape
    all_bins = values.shape[0]
    held = all_bins // CHUNKS
    tall = outs[0].shape[2]
    at_owner = quarters[0] == CHUNKS - 1
    me = lax.axis_index("bins")
    values[...] = jnp.zeros_like(values)
    row = iota((rows, columns), 0)
    for m in range(bins_axis):
        block = me ^ m
        at = pl.ds(pl.multiple_of(block * local_bins - 4 * (block & 1), 8), rows)
        arrived = blocks[m][...].astype(F32)
        if at_owner:
            lead = 4 * (block & 1)
            arrived = jnp.where((row >= lead) & (row < local_bins + lead), arrived, 0.0)
        values[at, :] += arrived
    flat = values[...].astype(BF16)
    energy = jnp.sum(values[...], axis=0, keepdims=True) / all_bins
    if at_owner:
        own = blocks[0][...].astype(F32)
        spare = jnp.where((me & 1) == 1, own[0:4, :], own[local_bins : local_bins + 4, :])
        weight, rank = spare[0:1, :], spare[1:2, :]
        lane = iota((1, columns), 1)
        slot = lane & (slots - 1)
        low = ((lane // slots) & (CHUNKS - 1)) ^ me
        towards = lane // LANES * CHUNKS + low
    else:
        facts = meta[:, quarters[0] * LANES : (quarters[-1] + 1) * LANES]
        slot, towards = facts[0:1, :].astype(I32), facts[1:2, :].astype(I32)
        rank, weight = facts[2:3, :], facts[3:4, :]
    scale = weight / (1.0 + energy)
    step = all_bins // 9
    for start in range(0, all_bins, step):
        at = slice(start, start + step)
        coupled = jnp.dot(weights[at, :], flat, preferred_element_type=F32)
        values[at, :] = (values[at, :] + coupled) * scale
    width = columns // len(quarters)
    slot_id = iota((2 * pairs * slots, width), 0)
    row_id = iota((tall, width), 0)
    for n, quarter in enumerate(quarters):
        cut = slice(n * width, (n + 1) * width)
        sent = []
        for v in range(CHUNKS):
            start = (v ^ quarter) * held
            lead = start % 8
            updated = values[start - lead : start - lead + tall, cut]
            if lead:
                updated = pltpu.roll(updated, tall - lead, 0)
            updated = jnp.where(row_id < held, updated, jnp.where(row_id == held, rank[:, cut], 0.0))
            group = (towards[:, cut] & (CHUNKS - 1)) ^ v
            column = towards[:, cut] // CHUNKS * LANES + group * slots + slot[:, cut]
            route = (slot_id == column).astype(F32).astype(BF16)
            sent.append(dot_nt(updated.astype(BF16), route).astype(BF16))
        for x in range(2 * pairs):
            at = slice(x // CHUNKS * LANES, (x // CHUNKS + 1) * LANES)
            outs[x // 2][x % 2, n] = lane_groups([rows_v[:, at] for rows_v in sent], x % CHUNKS)


def place_kernel(held, sources, picks, *refs):
    out, staged, sems = refs[-3:]
    me = lax.axis_index("pts")
    tall = refs[0].shape[-2]
    slot_id = iota((LANES, LANES), 0)
    copies = []
    for number, x in enumerate(sources):
        blocks = [refs[n][index] for n, index in picks[number]]
        pieces = []
        for g in range(CHUNKS):
            lhs = lane_groups(blocks, (x % CHUNKS) ^ g)
            rank = lhs[tall - 8 :, :].astype(F32)[held - tall + 8 : held - tall + 9, :].astype(I32)
            spots = (slot_id == rank).astype(F32).astype(BF16)
            pieces.append(dot_nt(lhs, spots)[:held])
        staged[number] = jnp.concatenate(pieces, axis=0).astype(BF16)
        at = pl.ds(pl.multiple_of((me ^ x) * LANES, LANES), LANES)
        copy = pltpu.make_async_copy(staged.at[number], out.at[:, at], sems.at[number])
        copy.start()
        copies.append(copy)
    for copy in copies:
        copy.wait()


def place(out, owners_count, all_bins, sources):
    arrays, picks = [], []
    for x in sorted(sources):
        mine = []
        for array, index in sources[x]:
            known = [n for n, a in enumerate(arrays) if a is array]
            if not known:
                arrays.append(array)
                known = [len(arrays) - 1]
            mine.append((known[0], index))
        picks.append(tuple(mine))
    held = [] if out is None else [out]
    return pl.pallas_call(
        functools.partial(place_kernel, all_bins // CHUNKS, tuple(sorted(sources)), tuple(picks)),
        out_shape=jax.ShapeDtypeStruct((all_bins, owners_count * LANES), BF16),
        in_specs=vmem(len(arrays)) + [pl.BlockSpec(memory_space=pl.ANY)] * len(held),
        out_specs=pl.BlockSpec(memory_space=pl.ANY),
        scratch_shapes=[
            pltpu.VMEM((len(sources), all_bins, LANES), BF16),
            pltpu.SemaphoreType.DMA((len(sources),)),
        ],
        input_output_aliases={len(arrays): 0} if held else {},
        compiler_params=params(16),
        cost_estimate=cost(1, 1),
        name="place",
    )(*arrays, *held)


def gate_kernel(array, *refs):
    refs[-1][...] = array[...]


def gate(array, *after):
    return pl.pallas_call(
        gate_kernel,
        out_shape=jax.ShapeDtypeStruct(array.shape, array.dtype),
        in_specs=vmem(1 + len(after)),
        out_specs=vmem(1)[0],
        compiler_params=params(16),
        cost_estimate=cost(1, 1),
        name="gate",
    )(array, *after)


def stack_kernel(count, *refs):
    for t in range(count):
        refs[-1][t] = refs[t][1]


def stack(pairs, *after):
    return pl.pallas_call(
        functools.partial(stack_kernel, len(pairs)),
        out_shape=jax.ShapeDtypeStruct((len(pairs),) + pairs[0].shape[1:], pairs[0].dtype),
        in_specs=vmem(len(pairs) + len(after)),
        out_specs=vmem(1)[0],
        compiler_params=params(8),
        cost_estimate=cost(1, 1),
        name="stack",
    )(*pairs, *after)


def params(mib):
    return pltpu.CompilerParams(vmem_limit_bytes=mib << 20)


def vmem(count):
    return [pl.BlockSpec(memory_space=pltpu.VMEM)] * count


def cost(flops, bytes_accessed):
    del bytes_accessed
    return pl.CostEstimate(flops=int(flops), bytes_accessed=1, transcendentals=0)


def exchange(array, axis, offset):
    return lax.ppermute(array, axis, [(i, i ^ offset) for i in range(lax.axis_size(axis))])


def chunked(spectrum, courant, upwind, coupling, sea, owner):
    local_bins, lon_rows, lats = spectrum.shape
    all_bins = courant.shape[0]
    bins_axis = lax.axis_size("bins")
    owners_count = lax.axis_size("pts")
    points = lon_rows * LANES
    width = points // CHUNKS
    slots = 2 * points // owners_count // CHUNKS
    tall = round_up(local_bins, 16)
    rows = round_up(local_bins + 1, 8)
    order_columns = (CHUNKS - 1) * width + owners_count * slots
    pairs = owners_count // 2
    quarter_rows = round_up(all_bins // CHUNKS + 1, 8)
    first_bin = lax.axis_index("bins") * local_bins

    planes = jnp.pad(jnp.transpose(spectrum, (1, 0, 2)), ((0, 0), (0, tall - local_bins), (0, 0)))
    even = lax.axis_index("pts") % 2 == 0
    rows_at = [jnp.where(even, 0, lon_rows - 1), jnp.where(even, lon_rows - 1, 0)]
    edges = [
        lax.dynamic_index_in_dim(planes, r, 0, False)[:local_bins]
        * lax.dynamic_index_in_dim(sea, r, 0, False).astype(BF16)[None]
        for r in rows_at
    ]
    between = [(i, i + 1) for i in range(1, owners_count - 1, 2)]
    far = lax.ppermute(edges[0], "pts", between + [(b, a) for a, b in between])
    near = exchange(edges[1], "pts", 1)
    own = owner.reshape(1, points)
    owners = [own, *reversed([exchange(own, "bins", m) for m in range(bins_axis - 1, 0, -1)])]

    def wide(table, dtype):
        mine = lax.dynamic_slice_in_dim(table.T, first_bin, local_bins, 1).astype(dtype)
        mine = jnp.pad(mine, ((0, 0), (0, tall - local_bins)))
        return jnp.broadcast_to(mine[:, :, None], (2, tall, LANES))

    speed, side = wide(courant, F32), wide(upwind, BF16)

    weights = pl.pallas_call(
        transpose_kernel,
        out_shape=jax.ShapeDtypeStruct(coupling.shape, BF16),
        in_specs=vmem(1),
        out_specs=vmem(1)[0],
        compiler_params=params(16),
        cost_estimate=cost(1, 1),
        name="transpose",
    )(coupling)

    inner = pl.pallas_call(
        inner_kernel,
        out_shape=jax.ShapeDtypeStruct((lon_rows - 1, tall, lats), BF16),
        in_specs=vmem(5),
        out_specs=vmem(1)[0],
        compiler_params=params(16),
        cost_estimate=cost(1, 1),
        name="inner",
    )(planes, near, speed, side, sea)
    ordered = []
    for group in (tuple(range(bins_axis - 1)), (bins_axis - 1,)):
        shapes = [
            jax.ShapeDtypeStruct((len(group), tall, order_columns), BF16),
            jax.ShapeDtypeStruct((len(group), order_columns, LANES), BF16),
        ]
        if group[0] == 0:
            shapes.append(jax.ShapeDtypeStruct((8, (CHUNKS - 1) * width), F32))
        ordered.append(
            pl.pallas_call(
                functools.partial(order_kernel, group, owners_count, width, slots),
                out_shape=shapes,
                in_specs=vmem(2 + len(group)),
                out_specs=vmem(len(shapes)),
                scratch_shapes=[pltpu.VMEM((order_columns, points), BF16)],
                compiler_params=params(16),
                cost_estimate=cost(1, 1),
                name="order",
            )(inner, sea, *[owners[m] for m in group])
        )
    meta = ordered[0][2]
    packed = pl.pallas_call(
        functools.partial(pack_kernel, rows, bins_axis, width, pairs),
        out_shape=[
            jax.ShapeDtypeStruct((rows, len(quarters) * width), BF16)
            for quarters in MAIN
            for _ in range(bins_axis)
        ]
        + [jax.ShapeDtypeStruct((2, 1, rows, LANES), BF16)] * pairs,
        in_specs=vmem(9),
        out_specs=vmem(len(MAIN) * bins_axis + pairs),
        scratch_shapes=[pltpu.VMEM((tall, lats), BF16)],
        compiler_params=params(16),
        cost_estimate=cost(1, 1),
        name="pack",
    )(planes, far, speed, side, sea, *[o[0] for o in ordered], *[o[1] for o in ordered])

    def couple(quarters, blocks, ready):
        shape = (2, len(quarters), quarter_rows, LANES)
        return pl.pallas_call(
            functools.partial(couple_kernel, quarters, bins_axis, local_bins, slots, pairs),
            out_shape=[jax.ShapeDtypeStruct(shape, BF16)] * pairs,
            in_specs=vmem(len(blocks) + 2 + len(ready)),
            out_specs=vmem(pairs),
            scratch_shapes=[pltpu.VMEM((all_bins, blocks[0].shape[1]), F32)],
            compiler_params=params(16),
            cost_estimate=cost((3e9, 1, 3e10, 3e10)[quarters[0]], 1),
            name="couple",
        )(*blocks, weights, meta, *ready)

    def over_bins(blocks):
        return [blocks[0]] + [exchange(blocks[m], "bins", m) for m in range(1, bins_axis)]

    def over_pts(pays):
        sent = {0: pays[0]}
        for t in range(pairs - 1, 0, -1):
            sent[t] = exchange(pays[t], "pts", 2 * t)
        return [sent[t] for t in range(pairs)]

    def held_back(blocks, *after):
        return [blocks[0]] + [gate(b, *after) for b in blocks[1:]]

    early, late = packed[:bins_axis], packed[bins_axis : 2 * bins_axis]
    direct = packed[2 * bins_axis :]
    first = over_bins(early)
    direct = over_pts(direct)
    regrouped = pl.pallas_call(
        functools.partial(regroup_kernel, bins_axis, pairs),
        out_shape=[jax.ShapeDtypeStruct((rows, owners_count * slots), BF16)] * bins_axis,
        in_specs=vmem(pairs + 1),
        out_specs=vmem(bins_axis),
        compiler_params=params(16),
        cost_estimate=cost(1, 1),
        name="regroup",
    )(*direct, exchange(stack(direct, first[1], first[2]), "pts", 1))
    late = [late[0], gate(late[1], first[1], weights), *[gate(b, *first[1:]) for b in late[2:]]]
    second = over_bins(late)
    came = [over_pts(couple(MAIN[0], first, late[1:]))]
    regrouped = [
        regrouped[0],
        gate(regrouped[1], *second[1:], came[0][0], came[0][pairs - 1]),
        *[gate(b, *second[1:], came[0][0]) for b in regrouped[2:]],
    ]
    third = over_bins(regrouped)
    came.append(over_pts(couple(MAIN[1], second, regrouped[2:])))
    last = came[-1]
    here = couple((CHUNKS - 1,), third, [])
    swapped = [exchange(stack(came[0], last[0]), "pts", 1), exchange(stack(last, here[0]), "pts", 1)]

    shape = (owners_count, all_bins)
    cuts = [(c, n) for c, quarters in enumerate(MAIN) for n in range(len(quarters))]
    near_side = {
        2 * t: [(came[c][t], (0, n)) for c, n in cuts] + [(here[t], (0, 0))] for t in range(pairs)
    }
    far_side = {
        2 * t + 1: [(swapped[c], (t, n)) for c, n in cuts] + [(here[t], (1, 0))] for t in range(pairs)
    }
    placed = place(place(None, *shape, near_side), *shape, far_side)
    return jnp.transpose(placed).reshape(1, 1, owners_count * LANES, all_bins)


def padded_2(block, sides, width):
    for axis, dim in sides:
        count = lax.axis_size(axis)
        forward = [(i, i + 1) for i in range(count - 1)]
        backward = [(target, source) for source, target in forward]
        low = lax.ppermute(
            lax.slice_in_dim(block, block.shape[dim] - width, None, axis=dim), axis, forward
        )
        high = lax.ppermute(lax.slice_in_dim(block, 0, width, axis=dim), axis, backward)
        block = jnp.concatenate([low, block, high], axis=dim)
    return block


def advect(padded, sea_mask, courant, upwind):
    center = padded[:, 1:-1, 1:-1]
    donor_x = jnp.where(upwind[:, 0][:, None, None] == 0, padded[:, :-2, 1:-1], padded[:, 2:, 1:-1])
    donor_y = jnp.where(upwind[:, 1][:, None, None] == 0, padded[:, 1:-1, :-2], padded[:, 1:-1, 2:])
    moved = (
        center
        - courant[:, 0][:, None, None] * (center - donor_x)
        - courant[:, 1][:, None, None] * (center - donor_y)
    )
    return (moved * sea_mask[None]).astype(jnp.bfloat16)


def whole(spectrum, courant, upwind, coupling, sea, owner):
    local_bins = spectrum.shape[0]
    lon_rows = spectrum.shape[1]
    bins_count = lax.axis_size("bins")
    lat_cells = spectrum.shape[2] // bins_count
    masked = spectrum * sea.astype(jnp.bfloat16)[None]
    local_sea = lax.dynamic_slice_in_dim(
        sea, lax.axis_index("bins") * lat_cells, lat_cells, 1
    ).astype(jnp.float32)
    first_bin = lax.axis_index("bins") * local_bins
    my_courant = lax.dynamic_slice_in_dim(courant, first_bin, local_bins, 0)
    my_upwind = lax.dynamic_slice_in_dim(upwind, first_bin, local_bins, 0)
    extended = padded_2(masked, (("pts", 1),), 1)
    extended = jnp.pad(extended.astype(jnp.float32), ((0, 0), (0, 0), (1, 1)))
    moved = advect(extended, sea.astype(jnp.float32), my_courant, my_upwind)
    columns = lax.all_to_all(moved, "bins", split_axis=2, concat_axis=0, tiled=True)
    all_bins = columns.shape[0]
    points = lon_rows * lat_cells
    flat = columns.reshape(all_bins, points)
    energy = jnp.mean(flat.astype(jnp.float32), axis=0)
    coupled = jnp.einsum("bp,bc->pc", flat, coupling, preferred_element_type=jnp.float32)
    weights = local_sea.reshape(points)
    updated = (
        weights[:, None] * (flat.astype(jnp.float32).T + coupled) / (1.0 + energy)[:, None]
    ).astype(jnp.bfloat16)
    owners_count = lax.axis_size("pts")
    capacity = max(2, (2 * points + owners_count - 1) // owners_count)
    target = owner.reshape(points)
    onehot = (target[:, None] == jnp.arange(owners_count, dtype=jnp.int32)[None, :]).astype(
        jnp.int32
    )
    slot_rank = jnp.sum(jnp.cumsum(onehot, axis=0) * onehot, axis=1) - 1
    slot_index = target * capacity + slot_rank
    selector = (
        slot_index[None, :] == jnp.arange(owners_count * capacity, dtype=jnp.int32)[:, None]
    ).astype(jnp.bfloat16)
    outgoing = jnp.dot(selector, updated, preferred_element_type=jnp.float32).astype(jnp.bfloat16)
    outgoing = outgoing.reshape(owners_count, capacity, all_bins)
    received = lax.all_to_all(outgoing, "pts", split_axis=0, concat_axis=0, tiled=True)
    return received.reshape(1, 1, owners_count * capacity, all_bins)


def local(spectrum, courant, upwind, coupling, sea, owner):
    bins_axis, owners_count = lax.axis_size("bins"), lax.axis_size("pts")
    points = owner.shape[2]
    suits = (
        spectrum.shape[2] == bins_axis * LANES
        and points % (2 * LANES) == 0
        and 2 * points == owners_count * LANES
        and bins_axis & (bins_axis - 1) == 0
        and owners_count & (owners_count - 1) == 0
        and bins_axis % 2 == 0
        and spectrum.shape[0] % 16 == 4
        and courant.shape[0] % 144 == 0
        and courant.shape[0] // CHUNKS % 8 == 4
        and points == CHUNKS * LANES
        and bins_axis == CHUNKS
        and owners_count == 8
        and spectrum.shape[1] >= 3
    )
    form = chunked if suits else whole
    return form(spectrum, courant, upwind, coupling, sea, owner)


def solution(mesh):
    placed = (P("bins", "pts", None), P(), P(), P(), P("pts", None), P("pts", "bins", None, None))
    return jax.shard_map(
        local, mesh=mesh, in_specs=placed, out_specs=P("pts", "bins", None, None), check_vma=False
    )
```

```python
import functools

import jax
import jax.numpy as jnp
from jax import lax
from jax.experimental import pallas as pl
from jax.experimental.pallas import tpu as pltpu
from jax.sharding import PartitionSpec as P

F32 = jnp.float32
BF16 = jnp.bfloat16
I32 = jnp.int32
LANES = 128
CHUNKS = 4
MAIN = ((0, 1), (2,))
NT = (((1,), (1,)), ((), ()))


def round_up(size, unit):
    return -(-size // unit) * unit


def iota(shape, axis):
    return lax.broadcasted_iota(I32, shape, axis)


def dot_nt(lhs, rhs):
    return lax.dot_general(lhs, rhs, NT, preferred_element_type=F32)


def upwind_row(at, speed, side, before, center, after, sea_row):
    lats = center.shape[1]
    lane = iota(center.shape, 1)
    wide = lats // LANES
    cx, cy = [jnp.concatenate([speed[k, at, :]] * wide, axis=1) for k in range(2)]
    ux, uy = [jnp.concatenate([side[k, at, :]] * wide, axis=1) for k in range(2)]
    donor_x = jnp.where(ux == 0, before, after).astype(F32)
    left = jnp.where(lane == 0, 0, pltpu.roll(center, 1, 1))
    right = jnp.where(lane == lats - 1, 0, pltpu.roll(center, lats - 1, 1))
    donor_y = jnp.where(uy == 0, left, right).astype(F32)
    center = center.astype(F32)
    value = center - cx * (center - donor_x) - cy * (center - donor_y)
    return (value * sea_row).astype(BF16)


def inner_kernel(planes, near, speed, side, sea, moved):
    lon_rows, rows, _ = planes.shape
    top = lon_rows - 1
    even = lax.axis_index("pts") % 2 == 0
    sea_f = sea[...].astype(F32)
    sea_b = sea_f.astype(BF16)

    def tile(at, close):
        masked = [planes[l, at, :] * sea_b[l : l + 1, :] for l in range(lon_rows)]
        for l in range(1, top):
            moved[l - 1, at, :] = upwind_row(
                at, speed, side, masked[l - 1], masked[l], masked[l + 1], sea_f[l : l + 1, :]
            )
        center = jnp.where(even, masked[top], masked[0])
        below = jnp.where(even, masked[top - 1], close)
        above = jnp.where(even, close, masked[1])
        weight = jnp.where(even, sea_f[top : top + 1, :], sea_f[0:1, :])
        moved[top - 1, at, :] = upwind_row(at, speed, side, below, center, above, weight)

    over_rows(tile, rows, near)


def over_rows(tile, rows, halo):
    held = halo.shape[0]
    full = held // 16 * 16

    def step(index, carry):
        at = pl.ds(pl.multiple_of(index * 16, 16), 16)
        tile(at, halo[at, :])
        return carry

    lax.fori_loop(0, full // 16, step, 0, unroll=5)
    if full < rows:
        spare = jnp.zeros((rows - held, halo.shape[1]), F32)
        end = jnp.concatenate([halo[full:, :].astype(F32), spare], axis=0).astype(BF16)
        tile(pl.ds(full, 16), end)


def order_kernel(blocks, owners_count, width, slots, *refs):
    inner, sea = refs[:2]
    owner = refs[2 : 2 + len(blocks)]
    part, far_order = refs[2 + len(blocks) : 4 + len(blocks)]
    order = refs[-1]
    lon_rows, rows = inner.shape[0] + 1, inner.shape[1]
    points = lon_rows * LANES
    me = lax.axis_index("bins")
    me_pts = lax.axis_index("pts")
    even = me_pts % 2 == 0
    last = (lon_rows - 1) * LANES
    near_at = pl.ds(pl.multiple_of(jnp.where(even, last, 0), LANES), LANES)
    far_at = pl.ds(pl.multiple_of(jnp.where(even, 0, last), LANES), LANES)
    owners_id = iota((owners_count, points), 0)
    hot = [(owner[m][...] == owners_id).astype(F32) for m in range(len(blocks))]
    earlier = (iota((points, points), 0) < iota((points, points), 1)).astype(F32).astype(BF16)
    before = jnp.dot(
        jnp.concatenate(hot, axis=0).astype(BF16), earlier, preferred_element_type=F32
    )
    main = (CHUNKS - 1) * width
    place_id = iota(order.shape, 0)
    none = [jnp.zeros((1, points), F32)]
    for m, offset_of in enumerate(blocks):
        own = owner[m][...]
        count = jnp.sum(hot[m], axis=1, keepdims=True)
        offset = jnp.sum(jnp.where(owners_id < own, count, 0.0), axis=0, keepdims=True)
        mine = before[m * owners_count : (m + 1) * owners_count, :]
        rank = jnp.sum(hot[m] * mine, axis=0, keepdims=True)
        key, first = (offset + rank).astype(I32), offset.astype(I32)
        quarter = key & (CHUNKS - 1)
        slot = (key - first - ((quarter - first) & (CHUNKS - 1))) // CHUNKS
        towards = own ^ me_pts
        block = me ^ offset_of
        group = (towards & (CHUNKS - 1)) ^ block
        spread = main + towards // CHUNKS * LANES + group * slots + slot
        place = jnp.where(quarter < CHUNKS - 1, quarter * width + key // CHUNKS, spread)
        order[...] = (place_id == place).astype(F32).astype(BF16)
        far_order[m] = order[:, far_at]
        at = pl.ds(pl.multiple_of(block * LANES, LANES), LANES)
        cells = jnp.concatenate([inner[l, :, at] for l in range(lon_rows - 1)], axis=1)
        columns = jnp.concatenate([order[:, LANES:last], order[:, near_at]], axis=1)
        part[m] = dot_nt(cells, columns).astype(BF16)
        weight = jnp.concatenate([sea[l : l + 1, at].astype(F32) for l in range(lon_rows)], axis=1)
        facts = jnp.concatenate(none * 4 + [weight, rank] + none * 10, axis=0).astype(BF16)
        end = slice(rows - 16, rows)
        spare = part[m, end, main:].astype(F32) + dot_nt(facts, order[main:, :])
        part[m, end, main:] = spare.astype(BF16)
        if offset_of == 0:
            facts = [slot.astype(F32), towards.astype(F32), rank, weight] + none * 4
            refs[-2][...] = dot_nt(jnp.concatenate(facts, axis=0).astype(BF16), order[:main, :])


def pack_kernel(rows_out, bins_axis, width, pairs, *refs):
    planes, far, speed, side, sea = refs[:5]
    parts, far_orders = refs[5:7], refs[7:9]
    chunks, moved = refs[9:-1], refs[-1]
    direct = chunks[len(MAIN) * bins_axis :]
    lon_rows, rows, _ = planes.shape
    top = lon_rows - 1
    me = lax.axis_index("bins")
    even = lax.axis_index("pts") % 2 == 0
    center_row, next_row = jnp.where(even, 0, top), jnp.where(even, 1, top - 1)
    sea_f = sea[...].astype(F32)
    center_sea = jnp.where(even, sea_f[0:1, :], sea_f[top : top + 1, :])
    next_sea = jnp.where(even, sea_f[1:2, :], sea_f[top - 1 : top, :]).astype(BF16)

    def tile(at, distant):
        center = planes[center_row, at, :] * center_sea.astype(BF16)
        beside = planes[next_row, at, :] * next_sea
        below, above = jnp.where(even, distant, beside), jnp.where(even, beside, distant)
        moved[at, :] = upwind_row(at, speed, side, below, center, above, center_sea)

    over_rows(tile, rows, far)
    spread = []
    for m in range(bins_axis):
        at = pl.ds(pl.multiple_of((me ^ m) * LANES, LANES), LANES)
        late = m == bins_axis - 1
        index = 0 if late else m
        ordered = dot_nt(moved[:, at], far_orders[late][index]) + parts[late][index].astype(F32)
        ordered = ordered[:rows_out]
        ordered = jnp.where((me & 1) == 1, pltpu.roll(ordered, 4, 0), ordered).astype(BF16)
        for c, quarters in enumerate(MAIN):
            at = slice(quarters[0] * width, (quarters[-1] + 1) * width)
            chunks[c * bins_axis + m][...] = ordered[:, at]
        spread.append(ordered[:, (CHUNKS - 1) * width :])
    group = iota((rows_out, LANES), 1) // (LANES // CHUNKS)
    for x in range(2 * pairs):
        at = slice(x // CHUNKS * LANES, (x // CHUNKS + 1) * LANES)
        mixed = spread[0][:, at]
        for m in range(1, bins_axis):
            mixed = jnp.where(group == ((me ^ m) ^ (x % CHUNKS)), spread[m][:, at], mixed)
        direct[x // 2][x % 2, 0] = mixed


def regroup_kernel(bins_axis, pairs, *refs):
    came, swapped, outs = refs[:pairs], refs[pairs], refs[pairs + 1 :]
    me = lax.axis_index("bins")
    sources = [swapped[x // 2, 0] if x % 2 else came[x // 2][0, 0] for x in range(2 * pairs)]
    group = iota(sources[0].shape, 1) // (LANES // CHUNKS)
    for m in range(bins_axis):
        for u in range(2 * pairs // CHUNKS):
            mixed = sources[u * CHUNKS]
            for k in range(1, CHUNKS):
                mixed = jnp.where(group == ((me ^ m) ^ k), sources[u * CHUNKS + k], mixed)
            outs[m][:, u * LANES : (u + 1) * LANES] = mixed


def transpose_kernel(coupling, out):
    bins = coupling.shape[0]
    for start in range(0, bins, 256):
        size = min(256, bins - start)
        eye = (iota((size, size), 0) == iota((size, size), 1)).astype(F32).astype(BF16)
        out[start : start + size, :] = dot_nt(eye, coupling[:, start : start + size]).astype(BF16)


def lane_groups(blocks, shift):
    group = iota(blocks[0].shape, 1) // (LANES // CHUNKS)
    mixed = blocks[shift]
    for q in range(1, CHUNKS):
        mixed = jnp.where(group == q, blocks[q ^ shift], mixed)
    return mixed


def couple_kernel(quarters, bins_axis, local_bins, slots, pairs, *refs):
    blocks = refs[:bins_axis]
    weights, meta = refs[bins_axis : bins_axis + 2]
    values, outs = refs[-1], refs[-1 - pairs : -1]
    rows, columns = blocks[0].shape
    all_bins = values.shape[0]
    held = all_bins // CHUNKS
    tall = outs[0].shape[2]
    at_owner = quarters[0] == CHUNKS - 1
    me = lax.axis_index("bins")
    values[...] = jnp.zeros_like(values)
    row = iota((rows, columns), 0)
    for m in range(bins_axis):
        block = me ^ m
        at = pl.ds(pl.multiple_of(block * local_bins - 4 * (block & 1), 8), rows)
        arrived = blocks[m][...].astype(F32)
        if at_owner:
            lead = 4 * (block & 1)
            arrived = jnp.where((row >= lead) & (row < local_bins + lead), arrived, 0.0)
        values[at, :] += arrived
    flat = values[...].astype(BF16)
    energy = jnp.sum(values[...], axis=0, keepdims=True) / all_bins
    if at_owner:
        own = blocks[0][...].astype(F32)
        spare = jnp.where((me & 1) == 1, own[0:4, :], own[local_bins : local_bins + 4, :])
        weight, rank = spare[0:1, :], spare[1:2, :]
        lane = iota((1, columns), 1)
        slot = lane & (slots - 1)
        low = ((lane // slots) & (CHUNKS - 1)) ^ me
        towards = lane // LANES * CHUNKS + low
    else:
        facts = meta[:, quarters[0] * LANES : (quarters[-1] + 1) * LANES]
        slot, towards = facts[0:1, :].astype(I32), facts[1:2, :].astype(I32)
        rank, weight = facts[2:3, :], facts[3:4, :]
    scale = weight / (1.0 + energy)
    step = all_bins // 9
    for start in range(0, all_bins, step):
        at = slice(start, start + step)
        coupled = jnp.dot(weights[at, :], flat, preferred_element_type=F32)
        values[at, :] = (values[at, :] + coupled) * scale
    width = columns // len(quarters)
    slot_id = iota((2 * pairs * slots, width), 0)
    row_id = iota((tall, width), 0)
    for n, quarter in enumerate(quarters):
        cut = slice(n * width, (n + 1) * width)
        sent = []
        for v in range(CHUNKS):
            start = (v ^ quarter) * held
            lead = start % 8
            updated = values[start - lead : start - lead + tall, cut]
            if lead:
                updated = pltpu.roll(updated, tall - lead, 0)
            updated = jnp.where(row_id < held, updated, jnp.where(row_id == held, rank[:, cut], 0.0))
            group = (towards[:, cut] & (CHUNKS - 1)) ^ v
            column = towards[:, cut] // CHUNKS * LANES + group * slots + slot[:, cut]
            route = (slot_id == column).astype(F32).astype(BF16)
            sent.append(dot_nt(updated.astype(BF16), route).astype(BF16))
        for x in range(2 * pairs):
            at = slice(x // CHUNKS * LANES, (x // CHUNKS + 1) * LANES)
            outs[x // 2][x % 2, n] = lane_groups([rows_v[:, at] for rows_v in sent], x % CHUNKS)


def place_kernel(held, sources, picks, *refs):
    out, staged, sems = refs[-3:]
    me = lax.axis_index("pts")
    tall = refs[0].shape[-2]
    slot_id = iota((LANES, LANES), 0)
    copies = []
    for number, x in enumerate(sources):
        blocks = [refs[n][index] for n, index in picks[number]]
        pieces = []
        for g in range(CHUNKS):
            lhs = lane_groups(blocks, (x % CHUNKS) ^ g)
            rank = lhs[tall - 8 :, :].astype(F32)[held - tall + 8 : held - tall + 9, :].astype(I32)
            spots = (slot_id == rank).astype(F32).astype(BF16)
            pieces.append(dot_nt(lhs, spots)[:held])
        staged[number] = jnp.concatenate(pieces, axis=0).astype(BF16)
        at = pl.ds(pl.multiple_of((me ^ x) * LANES, LANES), LANES)
        copy = pltpu.make_async_copy(staged.at[number], out.at[:, at], sems.at[number])
        copy.start()
        copies.append(copy)
    for copy in copies:
        copy.wait()


def place(out, owners_count, all_bins, sources):
    arrays, picks = [], []
    for x in sorted(sources):
        mine = []
        for array, index in sources[x]:
            known = [n for n, a in enumerate(arrays) if a is array]
            if not known:
                arrays.append(array)
                known = [len(arrays) - 1]
            mine.append((known[0], index))
        picks.append(tuple(mine))
    held = [] if out is None else [out]
    return pl.pallas_call(
        functools.partial(place_kernel, all_bins // CHUNKS, tuple(sorted(sources)), tuple(picks)),
        out_shape=jax.ShapeDtypeStruct((all_bins, owners_count * LANES), BF16),
        in_specs=vmem(len(arrays)) + [pl.BlockSpec(memory_space=pl.ANY)] * len(held),
        out_specs=pl.BlockSpec(memory_space=pl.ANY),
        scratch_shapes=[
            pltpu.VMEM((len(sources), all_bins, LANES), BF16),
            pltpu.SemaphoreType.DMA((len(sources),)),
        ],
        input_output_aliases={len(arrays): 0} if held else {},
        compiler_params=params(16),
        cost_estimate=cost(1, 1),
        name="place",
    )(*arrays, *held)


def gate_kernel(array, *refs):
    refs[-1][...] = array[...]


def gate(array, *after):
    return pl.pallas_call(
        gate_kernel,
        out_shape=jax.ShapeDtypeStruct(array.shape, array.dtype),
        in_specs=vmem(1 + len(after)),
        out_specs=vmem(1)[0],
        compiler_params=params(16),
        cost_estimate=cost(1, 1),
        name="gate",
    )(array, *after)


def stack_kernel(count, *refs):
    for t in range(count):
        refs[-1][t] = refs[t][1]


def stack(pairs, *after):
    return pl.pallas_call(
        functools.partial(stack_kernel, len(pairs)),
        out_shape=jax.ShapeDtypeStruct((len(pairs),) + pairs[0].shape[1:], pairs[0].dtype),
        in_specs=vmem(len(pairs) + len(after)),
        out_specs=vmem(1)[0],
        compiler_params=params(8),
        cost_estimate=cost(1, 1),
        name="stack",
    )(*pairs, *after)


def params(mib):
    return pltpu.CompilerParams(vmem_limit_bytes=mib << 20)


def vmem(count):
    return [pl.BlockSpec(memory_space=pltpu.VMEM)] * count


def cost(flops, bytes_accessed):
    del bytes_accessed
    return pl.CostEstimate(flops=int(flops), bytes_accessed=1, transcendentals=0)


def exchange(array, axis, offset):
    return lax.ppermute(array, axis, [(i, i ^ offset) for i in range(lax.axis_size(axis))])


def chunked(spectrum, courant, upwind, coupling, sea, owner):
    local_bins, lon_rows, lats = spectrum.shape
    all_bins = courant.shape[0]
    bins_axis = lax.axis_size("bins")
    owners_count = lax.axis_size("pts")
    points = lon_rows * LANES
    width = points // CHUNKS
    slots = 2 * points // owners_count // CHUNKS
    tall = round_up(local_bins, 16)
    rows = round_up(local_bins + 1, 8)
    order_columns = (CHUNKS - 1) * width + owners_count * slots
    pairs = owners_count // 2
    quarter_rows = round_up(all_bins // CHUNKS + 1, 8)
    first_bin = lax.axis_index("bins") * local_bins

    planes = jnp.pad(jnp.transpose(spectrum, (1, 0, 2)), ((0, 0), (0, tall - local_bins), (0, 0)))
    even = lax.axis_index("pts") % 2 == 0
    rows_at = [jnp.where(even, 0, lon_rows - 1), jnp.where(even, lon_rows - 1, 0)]
    edges = [
        lax.dynamic_index_in_dim(planes, r, 0, False)[:local_bins]
        * lax.dynamic_index_in_dim(sea, r, 0, False).astype(BF16)[None]
        for r in rows_at
    ]
    between = [(i, i + 1) for i in range(1, owners_count - 1, 2)]
    far = lax.ppermute(edges[0], "pts", between + [(b, a) for a, b in between])
    near = exchange(edges[1], "pts", 1)
    own = owner.reshape(1, points)
    owners = [own, *reversed([exchange(own, "bins", m) for m in range(bins_axis - 1, 0, -1)])]

    def wide(table, dtype):
        mine = lax.dynamic_slice_in_dim(table.T, first_bin, local_bins, 1).astype(dtype)
        mine = jnp.pad(mine, ((0, 0), (0, tall - local_bins)))
        return jnp.broadcast_to(mine[:, :, None], (2, tall, LANES))

    speed, side = wide(courant, F32), wide(upwind, BF16)

    weights = pl.pallas_call(
        transpose_kernel,
        out_shape=jax.ShapeDtypeStruct(coupling.shape, BF16),
        in_specs=vmem(1),
        out_specs=vmem(1)[0],
        compiler_params=params(16),
        cost_estimate=cost(1, 1),
        name="transpose",
    )(coupling)

    inner = pl.pallas_call(
        inner_kernel,
        out_shape=jax.ShapeDtypeStruct((lon_rows - 1, tall, lats), BF16),
        in_specs=vmem(5),
        out_specs=vmem(1)[0],
        compiler_params=params(16),
        cost_estimate=cost(1, 1),
        name="inner",
    )(planes, near, speed, side, sea)
    ordered = []
    for group in (tuple(range(bins_axis - 1)), (bins_axis - 1,)):
        shapes = [
            jax.ShapeDtypeStruct((len(group), tall, order_columns), BF16),
            jax.ShapeDtypeStruct((len(group), order_columns, LANES), BF16),
        ]
        if group[0] == 0:
            shapes.append(jax.ShapeDtypeStruct((8, (CHUNKS - 1) * width), F32))
        ordered.append(
            pl.pallas_call(
                functools.partial(order_kernel, group, owners_count, width, slots),
                out_shape=shapes,
                in_specs=vmem(2 + len(group)),
                out_specs=vmem(len(shapes)),
                scratch_shapes=[pltpu.VMEM((order_columns, points), BF16)],
                compiler_params=params(16),
                cost_estimate=cost(1, 1),
                name="order",
            )(inner, sea, *[owners[m] for m in group])
        )
    meta = ordered[0][2]
    packed = pl.pallas_call(
        functools.partial(pack_kernel, rows, bins_axis, width, pairs),
        out_shape=[
            jax.ShapeDtypeStruct((rows, len(quarters) * width), BF16)
            for quarters in MAIN
            for _ in range(bins_axis)
        ]
        + [jax.ShapeDtypeStruct((2, 1, rows, LANES), BF16)] * pairs,
        in_specs=vmem(9),
        out_specs=vmem(len(MAIN) * bins_axis + pairs),
        scratch_shapes=[pltpu.VMEM((tall, lats), BF16)],
        compiler_params=params(16),
        cost_estimate=cost(1, 1),
        name="pack",
    )(planes, far, speed, side, sea, *[o[0] for o in ordered], *[o[1] for o in ordered])

    def couple(quarters, blocks, ready):
        shape = (2, len(quarters), quarter_rows, LANES)
        return pl.pallas_call(
            functools.partial(couple_kernel, quarters, bins_axis, local_bins, slots, pairs),
            out_shape=[jax.ShapeDtypeStruct(shape, BF16)] * pairs,
            in_specs=vmem(len(blocks) + 2 + len(ready)),
            out_specs=vmem(pairs),
            scratch_shapes=[pltpu.VMEM((all_bins, blocks[0].shape[1]), F32)],
            compiler_params=params(16),
            cost_estimate=cost((3e9, 1, 3e10, 3e10)[quarters[0]], 1),
            name="couple",
        )(*blocks, weights, meta, *ready)

    def over_bins(blocks):
        return [blocks[0]] + [exchange(blocks[m], "bins", m) for m in range(1, bins_axis)]

    def over_pts(pays):
        sent = {0: pays[0]}
        for t in range(pairs - 1, 0, -1):
            sent[t] = exchange(pays[t], "pts", 2 * t)
        return [sent[t] for t in range(pairs)]

    def held_back(blocks, *after):
        return [blocks[0]] + [gate(b, *after) for b in blocks[1:]]

    early, late = packed[:bins_axis], packed[bins_axis : 2 * bins_axis]
    direct = packed[2 * bins_axis :]
    first = over_bins(early)
    direct = over_pts(direct)
    regrouped = pl.pallas_call(
        functools.partial(regroup_kernel, bins_axis, pairs),
        out_shape=[jax.ShapeDtypeStruct((rows, owners_count * slots), BF16)] * bins_axis,
        in_specs=vmem(pairs + 1),
        out_specs=vmem(bins_axis),
        compiler_params=params(16),
        cost_estimate=cost(1, 1),
        name="regroup",
    )(*direct, exchange(stack(direct, first[1], first[2]), "pts", 1))
    late = [late[0], gate(late[1], first[1], weights), *[gate(b, *first[1:]) for b in late[2:]]]
    second = over_bins(late)
    came = [over_pts(couple(MAIN[0], first, late[1:]))]
    regrouped = [
        regrouped[0],
        gate(regrouped[1], *second[1:], came[0][0], came[0][pairs - 1]),
        *[gate(b, *second[2:], came[0][0]) for b in regrouped[2:]],
    ]
    third = over_bins(regrouped)
    came.append(over_pts(couple(MAIN[1], second, regrouped[2:])))
    last = came[-1]
    here = couple((CHUNKS - 1,), third, [])
    swapped = [exchange(stack(came[0], last[0]), "pts", 1), exchange(stack(last, here[0]), "pts", 1)]

    shape = (owners_count, all_bins)
    cuts = [(c, n) for c, quarters in enumerate(MAIN) for n in range(len(quarters))]
    near_side = {
        2 * t: [(came[c][t], (0, n)) for c, n in cuts] + [(here[t], (0, 0))] for t in range(pairs)
    }
    far_side = {
        2 * t + 1: [(swapped[c], (t, n)) for c, n in cuts] + [(here[t], (1, 0))] for t in range(pairs)
    }
    placed = place(place(None, *shape, near_side), *shape, far_side)
    return jnp.transpose(placed).reshape(1, 1, owners_count * LANES, all_bins)


def padded_2(block, sides, width):
    for axis, dim in sides:
        count = lax.axis_size(axis)
        forward = [(i, i + 1) for i in range(count - 1)]
        backward = [(target, source) for source, target in forward]
        low = lax.ppermute(
            lax.slice_in_dim(block, block.shape[dim] - width, None, axis=dim), axis, forward
        )
        high = lax.ppermute(lax.slice_in_dim(block, 0, width, axis=dim), axis, backward)
        block = jnp.concatenate([low, block, high], axis=dim)
    return block


def advect(padded, sea_mask, courant, upwind):
    center = padded[:, 1:-1, 1:-1]
    donor_x = jnp.where(upwind[:, 0][:, None, None] == 0, padded[:, :-2, 1:-1], padded[:, 2:, 1:-1])
    donor_y = jnp.where(upwind[:, 1][:, None, None] == 0, padded[:, 1:-1, :-2], padded[:, 1:-1, 2:])
    moved = (
        center
        - courant[:, 0][:, None, None] * (center - donor_x)
        - courant[:, 1][:, None, None] * (center - donor_y)
    )
    return (moved * sea_mask[None]).astype(jnp.bfloat16)


def whole(spectrum, courant, upwind, coupling, sea, owner):
    local_bins = spectrum.shape[0]
    lon_rows = spectrum.shape[1]
    bins_count = lax.axis_size("bins")
    lat_cells = spectrum.shape[2] // bins_count
    masked = spectrum * sea.astype(jnp.bfloat16)[None]
    local_sea = lax.dynamic_slice_in_dim(
        sea, lax.axis_index("bins") * lat_cells, lat_cells, 1
    ).astype(jnp.float32)
    first_bin = lax.axis_index("bins") * local_bins
    my_courant = lax.dynamic_slice_in_dim(courant, first_bin, local_bins, 0)
    my_upwind = lax.dynamic_slice_in_dim(upwind, first_bin, local_bins, 0)
    extended = padded_2(masked, (("pts", 1),), 1)
    extended = jnp.pad(extended.astype(jnp.float32), ((0, 0), (0, 0), (1, 1)))
    moved = advect(extended, sea.astype(jnp.float32), my_courant, my_upwind)
    columns = lax.all_to_all(moved, "bins", split_axis=2, concat_axis=0, tiled=True)
    all_bins = columns.shape[0]
    points = lon_rows * lat_cells
    flat = columns.reshape(all_bins, points)
    energy = jnp.mean(flat.astype(jnp.float32), axis=0)
    coupled = jnp.einsum("bp,bc->pc", flat, coupling, preferred_element_type=jnp.float32)
    weights = local_sea.reshape(points)
    updated = (
        weights[:, None] * (flat.astype(jnp.float32).T + coupled) / (1.0 + energy)[:, None]
    ).astype(jnp.bfloat16)
    owners_count = lax.axis_size("pts")
    capacity = max(2, (2 * points + owners_count - 1) // owners_count)
    target = owner.reshape(points)
    onehot = (target[:, None] == jnp.arange(owners_count, dtype=jnp.int32)[None, :]).astype(
        jnp.int32
    )
    slot_rank = jnp.sum(jnp.cumsum(onehot, axis=0) * onehot, axis=1) - 1
    slot_index = target * capacity + slot_rank
    selector = (
        slot_index[None, :] == jnp.arange(owners_count * capacity, dtype=jnp.int32)[:, None]
    ).astype(jnp.bfloat16)
    outgoing = jnp.dot(selector, updated, preferred_element_type=jnp.float32).astype(jnp.bfloat16)
    outgoing = outgoing.reshape(owners_count, capacity, all_bins)
    received = lax.all_to_all(outgoing, "pts", split_axis=0, concat_axis=0, tiled=True)
    return received.reshape(1, 1, owners_count * capacity, all_bins)


def local(spectrum, courant, upwind, coupling, sea, owner):
    bins_axis, owners_count = lax.axis_size("bins"), lax.axis_size("pts")
    points = owner.shape[2]
    suits = (
        spectrum.shape[2] == bins_axis * LANES
        and points % (2 * LANES) == 0
        and 2 * points == owners_count * LANES
        and bins_axis & (bins_axis - 1) == 0
        and owners_count & (owners_count - 1) == 0
        and bins_axis % 2 == 0
        and spectrum.shape[0] % 16 == 4
        and courant.shape[0] % 144 == 0
        and courant.shape[0] // CHUNKS % 8 == 4
        and points == CHUNKS * LANES
        and bins_axis == CHUNKS
        and owners_count == 8
        and spectrum.shape[1] >= 3
    )
    form = chunked if suits else whole
    return form(spectrum, courant, upwind, coupling, sea, owner)


def solution(mesh):
    placed = (P("bins", "pts", None), P(), P(), P(), P("pts", None), P("pts", "bins", None, None))
    return jax.shard_map(
        local, mesh=mesh, in_specs=placed, out_specs=P("pts", "bins", None, None), check_vma=False
    )
```

```python
import functools

import jax
import jax.numpy as jnp
from jax import lax
from jax.experimental import pallas as pl
from jax.experimental.pallas import tpu as pltpu
from jax.sharding import PartitionSpec as P

F32 = jnp.float32
BF16 = jnp.bfloat16
I32 = jnp.int32
LANES = 128
CHUNKS = 4
MAIN = ((0, 1), (2,))
NT = (((1,), (1,)), ((), ()))


def round_up(size, unit):
    return -(-size // unit) * unit


def iota(shape, axis):
    return lax.broadcasted_iota(I32, shape, axis)


def dot_nt(lhs, rhs):
    return lax.dot_general(lhs, rhs, NT, preferred_element_type=F32)


def upwind_row(at, speed, side, before, center, after, sea_row):
    lats = center.shape[1]
    lane = iota(center.shape, 1)
    wide = lats // LANES
    cx, cy = [jnp.concatenate([speed[k, at, :]] * wide, axis=1) for k in range(2)]
    ux, uy = [jnp.concatenate([side[k, at, :]] * wide, axis=1) for k in range(2)]
    donor_x = jnp.where(ux == 0, before, after).astype(F32)
    left = jnp.where(lane == 0, 0, pltpu.roll(center, 1, 1))
    right = jnp.where(lane == lats - 1, 0, pltpu.roll(center, lats - 1, 1))
    donor_y = jnp.where(uy == 0, left, right).astype(F32)
    center = center.astype(F32)
    value = center - cx * (center - donor_x) - cy * (center - donor_y)
    return (value * sea_row).astype(BF16)


def inner_kernel(planes, near, speed, side, sea, moved):
    lon_rows, rows, _ = planes.shape
    top = lon_rows - 1
    even = lax.axis_index("pts") % 2 == 0
    sea_f = sea[...].astype(F32)
    sea_b = sea_f.astype(BF16)

    def tile(at, close):
        masked = [planes[l, at, :] * sea_b[l : l + 1, :] for l in range(lon_rows)]
        for l in range(1, top):
            moved[l - 1, at, :] = upwind_row(
                at, speed, side, masked[l - 1], masked[l], masked[l + 1], sea_f[l : l + 1, :]
            )
        center = jnp.where(even, masked[top], masked[0])
        below = jnp.where(even, masked[top - 1], close)
        above = jnp.where(even, close, masked[1])
        weight = jnp.where(even, sea_f[top : top + 1, :], sea_f[0:1, :])
        moved[top - 1, at, :] = upwind_row(at, speed, side, below, center, above, weight)

    over_rows(tile, rows, near)


def over_rows(tile, rows, halo):
    held = halo.shape[0]
    full = held // 16 * 16

    def step(index, carry):
        at = pl.ds(pl.multiple_of(index * 16, 16), 16)
        tile(at, halo[at, :])
        return carry

    lax.fori_loop(0, full // 16, step, 0, unroll=5)
    if full < rows:
        spare = jnp.zeros((rows - held, halo.shape[1]), F32)
        end = jnp.concatenate([halo[full:, :].astype(F32), spare], axis=0).astype(BF16)
        tile(pl.ds(full, 16), end)


def order_kernel(blocks, owners_count, width, slots, *refs):
    inner, sea = refs[:2]
    owner = refs[2 : 2 + len(blocks)]
    part, far_order = refs[2 + len(blocks) : 4 + len(blocks)]
    order = refs[-1]
    lon_rows, rows = inner.shape[0] + 1, inner.shape[1]
    points = lon_rows * LANES
    me = lax.axis_index("bins")
    me_pts = lax.axis_index("pts")
    even = me_pts % 2 == 0
    last = (lon_rows - 1) * LANES
    near_at = pl.ds(pl.multiple_of(jnp.where(even, last, 0), LANES), LANES)
    far_at = pl.ds(pl.multiple_of(jnp.where(even, 0, last), LANES), LANES)
    owners_id = iota((owners_count, points), 0)
    hot = [(owner[m][...] == owners_id).astype(F32) for m in range(len(blocks))]
    earlier = (iota((points, points), 0) < iota((points, points), 1)).astype(F32).astype(BF16)
    before = jnp.dot(
        jnp.concatenate(hot, axis=0).astype(BF16), earlier, preferred_element_type=F32
    )
    main = (CHUNKS - 1) * width
    place_id = iota(order.shape, 0)
    none = [jnp.zeros((1, points), F32)]
    for m, offset_of in enumerate(blocks):
        own = owner[m][...]
        count = jnp.sum(hot[m], axis=1, keepdims=True)
        offset = jnp.sum(jnp.where(owners_id < own, count, 0.0), axis=0, keepdims=True)
        mine = before[m * owners_count : (m + 1) * owners_count, :]
        rank = jnp.sum(hot[m] * mine, axis=0, keepdims=True)
        key, first = (offset + rank).astype(I32), offset.astype(I32)
        quarter = key & (CHUNKS - 1)
        slot = (key - first - ((quarter - first) & (CHUNKS - 1))) // CHUNKS
        towards = own ^ me_pts
        block = me ^ offset_of
        group = (towards & (CHUNKS - 1)) ^ block
        spread = main + towards // CHUNKS * LANES + group * slots + slot
        place = jnp.where(quarter < CHUNKS - 1, quarter * width + key // CHUNKS, spread)
        order[...] = (place_id == place).astype(F32).astype(BF16)
        far_order[m] = order[:, far_at]
        at = pl.ds(pl.multiple_of(block * LANES, LANES), LANES)
        cells = jnp.concatenate([inner[l, :, at] for l in range(lon_rows - 1)], axis=1)
        columns = jnp.concatenate([order[:, LANES:last], order[:, near_at]], axis=1)
        part[m] = dot_nt(cells, columns).astype(BF16)
        weight = jnp.concatenate([sea[l : l + 1, at].astype(F32) for l in range(lon_rows)], axis=1)
        facts = jnp.concatenate(none * 4 + [weight, rank] + none * 10, axis=0).astype(BF16)
        end = slice(rows - 16, rows)
        spare = part[m, end, main:].astype(F32) + dot_nt(facts, order[main:, :])
        part[m, end, main:] = spare.astype(BF16)
        if offset_of == 0:
            facts = [slot.astype(F32), towards.astype(F32), rank, weight] + none * 4
            refs[-2][...] = dot_nt(jnp.concatenate(facts, axis=0).astype(BF16), order[:main, :])


def pack_kernel(rows_out, bins_axis, width, pairs, *refs):
    planes, far, speed, side, sea = refs[:5]
    parts, far_orders = refs[5:7], refs[7:9]
    chunks, moved = refs[9:-1], refs[-1]
    direct = chunks[len(MAIN) * bins_axis :]
    lon_rows, rows, _ = planes.shape
    top = lon_rows - 1
    me = lax.axis_index("bins")
    even = lax.axis_index("pts") % 2 == 0
    center_row, next_row = jnp.where(even, 0, top), jnp.where(even, 1, top - 1)
    sea_f = sea[...].astype(F32)
    center_sea = jnp.where(even, sea_f[0:1, :], sea_f[top : top + 1, :])
    next_sea = jnp.where(even, sea_f[1:2, :], sea_f[top - 1 : top, :]).astype(BF16)

    def tile(at, distant):
        center = planes[center_row, at, :] * center_sea.astype(BF16)
        beside = planes[next_row, at, :] * next_sea
        below, above = jnp.where(even, distant, beside), jnp.where(even, beside, distant)
        moved[at, :] = upwind_row(at, speed, side, below, center, above, center_sea)

    over_rows(tile, rows, far)
    spread = []
    for m in range(bins_axis):
        at = pl.ds(pl.multiple_of((me ^ m) * LANES, LANES), LANES)
        late = m == bins_axis - 1
        index = 0 if late else m
        ordered = dot_nt(moved[:, at], far_orders[late][index]) + parts[late][index].astype(F32)
        ordered = ordered[:rows_out]
        ordered = jnp.where((me & 1) == 1, pltpu.roll(ordered, 4, 0), ordered).astype(BF16)
        for c, quarters in enumerate(MAIN):
            at = slice(quarters[0] * width, (quarters[-1] + 1) * width)
            chunks[c * bins_axis + m][...] = ordered[:, at]
        spread.append(ordered[:, (CHUNKS - 1) * width :])
    group = iota((rows_out, LANES), 1) // (LANES // CHUNKS)
    for x in range(2 * pairs):
        at = slice(x // CHUNKS * LANES, (x // CHUNKS + 1) * LANES)
        mixed = spread[0][:, at]
        for m in range(1, bins_axis):
            mixed = jnp.where(group == ((me ^ m) ^ (x % CHUNKS)), spread[m][:, at], mixed)
        direct[x // 2][x % 2, 0] = mixed


def regroup_kernel(bins_axis, pairs, *refs):
    came, swapped, outs = refs[:pairs], refs[pairs], refs[pairs + 1 :]
    me = lax.axis_index("bins")
    sources = [swapped[x // 2, 0] if x % 2 else came[x // 2][0, 0] for x in range(2 * pairs)]
    group = iota(sources[0].shape, 1) // (LANES // CHUNKS)
    for m in range(bins_axis):
        for u in range(2 * pairs // CHUNKS):
            mixed = sources[u * CHUNKS]
            for k in range(1, CHUNKS):
                mixed = jnp.where(group == ((me ^ m) ^ k), sources[u * CHUNKS + k], mixed)
            outs[m][:, u * LANES : (u + 1) * LANES] = mixed


def transpose_kernel(coupling, out):
    bins = coupling.shape[0]
    for start in range(0, bins, 256):
        size = min(256, bins - start)
        eye = (iota((size, size), 0) == iota((size, size), 1)).astype(F32).astype(BF16)
        out[start : start + size, :] = dot_nt(eye, coupling[:, start : start + size]).astype(BF16)


def lane_groups(blocks, shift):
    group = iota(blocks[0].shape, 1) // (LANES // CHUNKS)
    mixed = blocks[shift]
    for q in range(1, CHUNKS):
        mixed = jnp.where(group == q, blocks[q ^ shift], mixed)
    return mixed


def couple_kernel(quarters, bins_axis, local_bins, slots, pairs, *refs):
    blocks = refs[:bins_axis]
    weights, meta = refs[bins_axis : bins_axis + 2]
    values, outs = refs[-1], refs[-1 - pairs : -1]
    rows, columns = blocks[0].shape
    all_bins = values.shape[0]
    held = all_bins // CHUNKS
    tall = outs[0].shape[2]
    at_owner = quarters[0] == CHUNKS - 1
    me = lax.axis_index("bins")
    values[...] = jnp.zeros_like(values)
    row = iota((rows, columns), 0)
    for m in range(bins_axis):
        block = me ^ m
        at = pl.ds(pl.multiple_of(block * local_bins - 4 * (block & 1), 8), rows)
        arrived = blocks[m][...].astype(F32)
        if at_owner:
            lead = 4 * (block & 1)
            arrived = jnp.where((row >= lead) & (row < local_bins + lead), arrived, 0.0)
        values[at, :] += arrived
    flat = values[...].astype(BF16)
    energy = jnp.sum(values[...], axis=0, keepdims=True) / all_bins
    if at_owner:
        own = blocks[0][...].astype(F32)
        spare = jnp.where((me & 1) == 1, own[0:4, :], own[local_bins : local_bins + 4, :])
        weight, rank = spare[0:1, :], spare[1:2, :]
        lane = iota((1, columns), 1)
        slot = lane & (slots - 1)
        low = ((lane // slots) & (CHUNKS - 1)) ^ me
        towards = lane // LANES * CHUNKS + low
    else:
        facts = meta[:, quarters[0] * LANES : (quarters[-1] + 1) * LANES]
        slot, towards = facts[0:1, :].astype(I32), facts[1:2, :].astype(I32)
        rank, weight = facts[2:3, :], facts[3:4, :]
    scale = weight / (1.0 + energy)
    step = all_bins // 9
    for start in range(0, all_bins, step):
        at = slice(start, start + step)
        coupled = jnp.dot(weights[at, :], flat, preferred_element_type=F32)
        values[at, :] = (values[at, :] + coupled) * scale
    width = columns // len(quarters)
    slot_id = iota((2 * pairs * slots, width), 0)
    row_id = iota((tall, width), 0)
    for n, quarter in enumerate(quarters):
        cut = slice(n * width, (n + 1) * width)
        sent = []
        for v in range(CHUNKS):
            start = (v ^ quarter) * held
            lead = start % 8
            updated = values[start - lead : start - lead + tall, cut]
            spare = row_id == (0 if lead else held)
            mine = row_id >= lead if lead else row_id < held
            updated = jnp.where(spare, rank[:, cut], jnp.where(mine, updated, 0.0))
            group = (towards[:, cut] & (CHUNKS - 1)) ^ v
            column = towards[:, cut] // CHUNKS * LANES + group * slots + slot[:, cut]
            route = (slot_id == column).astype(F32).astype(BF16)
            sent.append(dot_nt(updated.astype(BF16), route).astype(BF16))
        for x in range(2 * pairs):
            at = slice(x // CHUNKS * LANES, (x // CHUNKS + 1) * LANES)
            outs[x // 2][x % 2, n] = lane_groups([rows_v[:, at] for rows_v in sent], x % CHUNKS)


def place_kernel(held, sources, picks, *refs):
    out, staged, sems = refs[-3:]
    me = lax.axis_index("pts")
    tall = refs[0].shape[-2]
    slot_id = iota((LANES, LANES), 0)
    is_first = iota((8, LANES), 0) < 4
    copies = []
    for number, x in enumerate(sources):
        blocks = [refs[n][index] for n, index in picks[number]]
        groups = []
        for g in range(CHUNKS):
            lhs = lane_groups(blocks, (x % CHUNKS) ^ g)
            if g * held % 8:
                rank = lhs[0:8, :].astype(F32)[0:1, :].astype(I32)
            else:
                rank = lhs[tall - 8 :, :].astype(F32)[held - tall + 8 : held - tall + 9, :].astype(I32)
            spots = (slot_id == rank).astype(F32).astype(BF16)
            groups.append(dot_nt(lhs, spots))
        pieces = []
        for g in range(0, CHUNKS, 2):
            seam = jnp.where(is_first, groups[g][tall - 8 :], groups[g + 1][:8])
            pieces += [groups[g][: tall - 8], seam, groups[g + 1][8:]]
        staged[number] = jnp.concatenate(pieces, axis=0).astype(BF16)
        at = pl.ds(pl.multiple_of((me ^ x) * LANES, LANES), LANES)
        copy = pltpu.make_async_copy(staged.at[number], out.at[:, at], sems.at[number])
        copy.start()
        copies.append(copy)
    for copy in copies:
        copy.wait()


def place(out, owners_count, all_bins, sources):
    arrays, picks = [], []
    for x in sorted(sources):
        mine = []
        for array, index in sources[x]:
            known = [n for n, a in enumerate(arrays) if a is array]
            if not known:
                arrays.append(array)
                known = [len(arrays) - 1]
            mine.append((known[0], index))
        picks.append(tuple(mine))
    held = [] if out is None else [out]
    return pl.pallas_call(
        functools.partial(place_kernel, all_bins // CHUNKS, tuple(sorted(sources)), tuple(picks)),
        out_shape=jax.ShapeDtypeStruct((all_bins, owners_count * LANES), BF16),
        in_specs=vmem(len(arrays)) + [pl.BlockSpec(memory_space=pl.ANY)] * len(held),
        out_specs=pl.BlockSpec(memory_space=pl.ANY),
        scratch_shapes=[
            pltpu.VMEM((len(sources), all_bins, LANES), BF16),
            pltpu.SemaphoreType.DMA((len(sources),)),
        ],
        input_output_aliases={len(arrays): 0} if held else {},
        compiler_params=params(16),
        cost_estimate=cost(1, 1),
        name="place",
    )(*arrays, *held)


def gate_kernel(array, *refs):
    refs[-1][...] = array[...]


def gate(array, *after):
    return pl.pallas_call(
        gate_kernel,
        out_shape=jax.ShapeDtypeStruct(array.shape, array.dtype),
        in_specs=vmem(1 + len(after)),
        out_specs=vmem(1)[0],
        compiler_params=params(16),
        cost_estimate=cost(1, 1),
        name="gate",
    )(array, *after)


def stack_kernel(count, *refs):
    for t in range(count):
        refs[-1][t] = refs[t][1]


def stack(pairs, *after):
    return pl.pallas_call(
        functools.partial(stack_kernel, len(pairs)),
        out_shape=jax.ShapeDtypeStruct((len(pairs),) + pairs[0].shape[1:], pairs[0].dtype),
        in_specs=vmem(len(pairs) + len(after)),
        out_specs=vmem(1)[0],
        compiler_params=params(8),
        cost_estimate=cost(1, 1),
        name="stack",
    )(*pairs, *after)


def params(mib):
    return pltpu.CompilerParams(vmem_limit_bytes=mib << 20)


def vmem(count):
    return [pl.BlockSpec(memory_space=pltpu.VMEM)] * count


def cost(flops, bytes_accessed):
    del bytes_accessed
    return pl.CostEstimate(flops=int(flops), bytes_accessed=1, transcendentals=0)


def exchange(array, axis, offset):
    return lax.ppermute(array, axis, [(i, i ^ offset) for i in range(lax.axis_size(axis))])


def chunked(spectrum, courant, upwind, coupling, sea, owner):
    local_bins, lon_rows, lats = spectrum.shape
    all_bins = courant.shape[0]
    bins_axis = lax.axis_size("bins")
    owners_count = lax.axis_size("pts")
    points = lon_rows * LANES
    width = points // CHUNKS
    slots = 2 * points // owners_count // CHUNKS
    tall = round_up(local_bins, 16)
    rows = round_up(local_bins + 1, 8)
    order_columns = (CHUNKS - 1) * width + owners_count * slots
    pairs = owners_count // 2
    quarter_rows = round_up(all_bins // CHUNKS + 1, 8)
    first_bin = lax.axis_index("bins") * local_bins

    planes = jnp.pad(jnp.transpose(spectrum, (1, 0, 2)), ((0, 0), (0, tall - local_bins), (0, 0)))
    even = lax.axis_index("pts") % 2 == 0
    rows_at = [jnp.where(even, 0, lon_rows - 1), jnp.where(even, lon_rows - 1, 0)]
    edges = [
        lax.dynamic_index_in_dim(planes, r, 0, False)[:local_bins]
        * lax.dynamic_index_in_dim(sea, r, 0, False).astype(BF16)[None]
        for r in rows_at
    ]
    between = [(i, i + 1) for i in range(1, owners_count - 1, 2)]
    far = lax.ppermute(edges[0], "pts", between + [(b, a) for a, b in between])
    near = exchange(edges[1], "pts", 1)
    own = owner.reshape(1, points)
    owners = [own, *reversed([exchange(own, "bins", m) for m in range(bins_axis - 1, 0, -1)])]

    def wide(table, dtype):
        mine = lax.dynamic_slice_in_dim(table.T, first_bin, local_bins, 1).astype(dtype)
        mine = jnp.pad(mine, ((0, 0), (0, tall - local_bins)))
        return jnp.broadcast_to(mine[:, :, None], (2, tall, LANES))

    speed, side = wide(courant, F32), wide(upwind, BF16)

    weights = pl.pallas_call(
        transpose_kernel,
        out_shape=jax.ShapeDtypeStruct(coupling.shape, BF16),
        in_specs=vmem(1),
        out_specs=vmem(1)[0],
        compiler_params=params(16),
        cost_estimate=cost(1, 1),
        name="transpose",
    )(coupling)

    inner = pl.pallas_call(
        inner_kernel,
        out_shape=jax.ShapeDtypeStruct((lon_rows - 1, tall, lats), BF16),
        in_specs=vmem(5),
        out_specs=vmem(1)[0],
        compiler_params=params(16),
        cost_estimate=cost(1, 1),
        name="inner",
    )(planes, near, speed, side, sea)
    ordered = []
    for group in (tuple(range(bins_axis - 1)), (bins_axis - 1,)):
        shapes = [
            jax.ShapeDtypeStruct((len(group), tall, order_columns), BF16),
            jax.ShapeDtypeStruct((len(group), order_columns, LANES), BF16),
        ]
        if group[0] == 0:
            shapes.append(jax.ShapeDtypeStruct((8, (CHUNKS - 1) * width), F32))
        ordered.append(
            pl.pallas_call(
                functools.partial(order_kernel, group, owners_count, width, slots),
                out_shape=shapes,
                in_specs=vmem(2 + len(group)),
                out_specs=vmem(len(shapes)),
                scratch_shapes=[pltpu.VMEM((order_columns, points), BF16)],
                compiler_params=params(16),
                cost_estimate=cost(1, 1),
                name="order",
            )(inner, sea, *[owners[m] for m in group])
        )
    meta = ordered[0][2]
    packed = pl.pallas_call(
        functools.partial(pack_kernel, rows, bins_axis, width, pairs),
        out_shape=[
            jax.ShapeDtypeStruct((rows, len(quarters) * width), BF16)
            for quarters in MAIN
            for _ in range(bins_axis)
        ]
        + [jax.ShapeDtypeStruct((2, 1, rows, LANES), BF16)] * pairs,
        in_specs=vmem(9),
        out_specs=vmem(len(MAIN) * bins_axis + pairs),
        scratch_shapes=[pltpu.VMEM((tall, lats), BF16)],
        compiler_params=params(16),
        cost_estimate=cost(1, 1),
        name="pack",
    )(planes, far, speed, side, sea, *[o[0] for o in ordered], *[o[1] for o in ordered])

    def couple(quarters, blocks, ready):
        shape = (2, len(quarters), quarter_rows, LANES)
        return pl.pallas_call(
            functools.partial(couple_kernel, quarters, bins_axis, local_bins, slots, pairs),
            out_shape=[jax.ShapeDtypeStruct(shape, BF16)] * pairs,
            in_specs=vmem(len(blocks) + 2 + len(ready)),
            out_specs=vmem(pairs),
            scratch_shapes=[pltpu.VMEM((all_bins, blocks[0].shape[1]), F32)],
            compiler_params=params(16),
            cost_estimate=cost((3e9, 1, 3e10, 3e10)[quarters[0]], 1),
            name="couple",
        )(*blocks, weights, meta, *ready)

    def over_bins(blocks):
        return [blocks[0]] + [exchange(blocks[m], "bins", m) for m in range(1, bins_axis)]

    def over_pts(pays):
        sent = {0: pays[0]}
        for t in range(pairs - 1, 0, -1):
            sent[t] = exchange(pays[t], "pts", 2 * t)
        return [sent[t] for t in range(pairs)]

    def held_back(blocks, *after):
        return [blocks[0]] + [gate(b, *after) for b in blocks[1:]]

    early, late = packed[:bins_axis], packed[bins_axis : 2 * bins_axis]
    direct = packed[2 * bins_axis :]
    first = over_bins(early)
    direct = over_pts(direct)
    regrouped = pl.pallas_call(
        functools.partial(regroup_kernel, bins_axis, pairs),
        out_shape=[jax.ShapeDtypeStruct((rows, owners_count * slots), BF16)] * bins_axis,
        in_specs=vmem(pairs + 1),
        out_specs=vmem(bins_axis),
        compiler_params=params(16),
        cost_estimate=cost(1, 1),
        name="regroup",
    )(*direct, exchange(stack(direct, first[1], first[2]), "pts", 1))
    late = [late[0], gate(late[1], first[1], weights), *[gate(b, *first[1:]) for b in late[2:]]]
    second = over_bins(late)
    came = [over_pts(couple(MAIN[0], first, late[1:]))]
    regrouped = [
        regrouped[0],
        gate(regrouped[1], *second[1:], came[0][0], came[0][pairs - 1]),
        *[gate(b, *second[2:], came[0][0]) for b in regrouped[2:]],
    ]
    third = over_bins(regrouped)
    came.append(over_pts(couple(MAIN[1], second, regrouped[2:])))
    last = came[-1]
    here = couple((CHUNKS - 1,), third, [])
    swapped = [exchange(stack(came[0], last[0]), "pts", 1), exchange(stack(last, here[0]), "pts", 1)]

    shape = (owners_count, all_bins)
    cuts = [(c, n) for c, quarters in enumerate(MAIN) for n in range(len(quarters))]
    near_side = {
        2 * t: [(came[c][t], (0, n)) for c, n in cuts] + [(here[t], (0, 0))] for t in range(pairs)
    }
    far_side = {
        2 * t + 1: [(swapped[c], (t, n)) for c, n in cuts] + [(here[t], (1, 0))] for t in range(pairs)
    }
    placed = place(place(None, *shape, near_side), *shape, far_side)
    return jnp.transpose(placed).reshape(1, 1, owners_count * LANES, all_bins)


def padded_2(block, sides, width):
    for axis, dim in sides:
        count = lax.axis_size(axis)
        forward = [(i, i + 1) for i in range(count - 1)]
        backward = [(target, source) for source, target in forward]
        low = lax.ppermute(
            lax.slice_in_dim(block, block.shape[dim] - width, None, axis=dim), axis, forward
        )
        high = lax.ppermute(lax.slice_in_dim(block, 0, width, axis=dim), axis, backward)
        block = jnp.concatenate([low, block, high], axis=dim)
    return block


def advect(padded, sea_mask, courant, upwind):
    center = padded[:, 1:-1, 1:-1]
    donor_x = jnp.where(upwind[:, 0][:, None, None] == 0, padded[:, :-2, 1:-1], padded[:, 2:, 1:-1])
    donor_y = jnp.where(upwind[:, 1][:, None, None] == 0, padded[:, 1:-1, :-2], padded[:, 1:-1, 2:])
    moved = (
        center
        - courant[:, 0][:, None, None] * (center - donor_x)
        - courant[:, 1][:, None, None] * (center - donor_y)
    )
    return (moved * sea_mask[None]).astype(jnp.bfloat16)


def whole(spectrum, courant, upwind, coupling, sea, owner):
    local_bins = spectrum.shape[0]
    lon_rows = spectrum.shape[1]
    bins_count = lax.axis_size("bins")
    lat_cells = spectrum.shape[2] // bins_count
    masked = spectrum * sea.astype(jnp.bfloat16)[None]
    local_sea = lax.dynamic_slice_in_dim(
        sea, lax.axis_index("bins") * lat_cells, lat_cells, 1
    ).astype(jnp.float32)
    first_bin = lax.axis_index("bins") * local_bins
    my_courant = lax.dynamic_slice_in_dim(courant, first_bin, local_bins, 0)
    my_upwind = lax.dynamic_slice_in_dim(upwind, first_bin, local_bins, 0)
    extended = padded_2(masked, (("pts", 1),), 1)
    extended = jnp.pad(extended.astype(jnp.float32), ((0, 0), (0, 0), (1, 1)))
    moved = advect(extended, sea.astype(jnp.float32), my_courant, my_upwind)
    columns = lax.all_to_all(moved, "bins", split_axis=2, concat_axis=0, tiled=True)
    all_bins = columns.shape[0]
    points = lon_rows * lat_cells
    flat = columns.reshape(all_bins, points)
    energy = jnp.mean(flat.astype(jnp.float32), axis=0)
    coupled = jnp.einsum("bp,bc->pc", flat, coupling, preferred_element_type=jnp.float32)
    weights = local_sea.reshape(points)
    updated = (
        weights[:, None] * (flat.astype(jnp.float32).T + coupled) / (1.0 + energy)[:, None]
    ).astype(jnp.bfloat16)
    owners_count = lax.axis_size("pts")
    capacity = max(2, (2 * points + owners_count - 1) // owners_count)
    target = owner.reshape(points)
    onehot = (target[:, None] == jnp.arange(owners_count, dtype=jnp.int32)[None, :]).astype(
        jnp.int32
    )
    slot_rank = jnp.sum(jnp.cumsum(onehot, axis=0) * onehot, axis=1) - 1
    slot_index = target * capacity + slot_rank
    selector = (
        slot_index[None, :] == jnp.arange(owners_count * capacity, dtype=jnp.int32)[:, None]
    ).astype(jnp.bfloat16)
    outgoing = jnp.dot(selector, updated, preferred_element_type=jnp.float32).astype(jnp.bfloat16)
    outgoing = outgoing.reshape(owners_count, capacity, all_bins)
    received = lax.all_to_all(outgoing, "pts", split_axis=0, concat_axis=0, tiled=True)
    return received.reshape(1, 1, owners_count * capacity, all_bins)


def local(spectrum, courant, upwind, coupling, sea, owner):
    bins_axis, owners_count = lax.axis_size("bins"), lax.axis_size("pts")
    points = owner.shape[2]
    suits = (
        spectrum.shape[2] == bins_axis * LANES
        and points % (2 * LANES) == 0
        and 2 * points == owners_count * LANES
        and bins_axis & (bins_axis - 1) == 0
        and owners_count & (owners_count - 1) == 0
        and bins_axis % 2 == 0
        and spectrum.shape[0] % 16 == 4
        and courant.shape[0] % 144 == 0
        and courant.shape[0] // CHUNKS % 8 == 4
        and points == CHUNKS * LANES
        and bins_axis == CHUNKS
        and owners_count == 8
        and spectrum.shape[1] >= 3
    )
    form = chunked if suits else whole
    return form(spectrum, courant, upwind, coupling, sea, owner)


def solution(mesh):
    placed = (P("bins", "pts", None), P(), P(), P(), P("pts", None), P("pts", "bins", None, None))
    return jax.shard_map(
        local, mesh=mesh, in_specs=placed, out_specs=P("pts", "bins", None, None), check_vma=False
    )
```
